512 devices in a mesh: pts: 512 (over x, y, z, core).
Axes of the slice: x: 4, y: 8, z: 8, core: 2. Of those that a mesh axis runs over, the one named last changes fastest.
Arguments:
- points: bfloat16 [262144, 256], P('pts'), may hold values from -24 to 24
- patch_ids: int32 [262144], P('pts'), may hold values from 0 to 639, never falling along the last dimension, each value on 1 to 512 neighbouring positions
- cell_ids: int32 [262144], P('pts'), may hold values from 0 to 65535, as said below
- norm_gain: float32 [256], replicated, may hold values from 0.8 to 2
- w_qkv: bfloat16 [256, 768], replicated, may hold values from -0.375 to 0.375
- w_out: bfloat16 [256, 256], replicated, may hold values from -0.375 to 0.375
- w_pool: bfloat16 [256, 512], replicated, may hold values from -0.375 to 0.375
- b_pool: float32 [512], replicated, may hold values from -4 to 4
- pool_gain: float32 [512], replicated, may hold values from 0.5 to 1.5
- cotangent: float32 [65536, 512], P('pts'), may hold values from -6 to 6
Outputs:
- grad_points: float32 [262144, 256], P('pts')
- grad_qkv: float32 [256, 768], replicated
- grad_w_out: float32 [256, 256], replicated
- grad_norm_gain: float32 [256], replicated
- grad_w_pool: float32 [256, 512], replicated
- grad_b_pool: float32 [512], replicated
- grad_pool_gain: float32 [512], replicated
The draws below stay inside these ranges and needn't reach their ends.
Inputs may be any that keep to these rules, and one draw needn't show every extreme that they name: `patch_ids`: patch ids never fall; every patch has 1 to 512 points and some patch has exactly 512. `cell_ids`: cell ids never fall and every cell has a point; point 0 is in cell 0; points d * 512 to (d + 1) * 512 - 1 hold the first points of exactly the cells d * 128 to (d + 1) * 128 - 1, for d above 0 none of them among the first 128 points of that range, so for d above 0 those first points belong to cell d * 128 - 1.
All inputs are finite; a program needn't handle non-finite values.
Results may differ from the reference program's by a relative error of at most 0.024.
Values may be sent and summed in bfloat16 or wider, within the bound.
A program may use at most 64 MiB of HBM per device.

```python
import math
import jax
import jax.numpy as jnp
import numpy as np
from jax import lax

WIDTH = 256
HEADS = 16
POOLED = 512
PATCH = 512
QBLOCK = 512
P_DEV = 512
CELL_DEV = 128
POINTS = 262144
CELLS = 65536
PATCHES = 640


def draw_points(key, part):
    key = jax.random.fold_in(key, 5)
    key_rows, key_cols, key_vals = jax.random.split(key, 3)
    row_scale = jnp.exp(jax.random.uniform(key_rows, (POINTS, 1), jnp.float32, math.log(0.3), math.log(3.0)))
    col_scale = jnp.exp(jax.random.uniform(key_cols, (1, WIDTH), jnp.float32, math.log(0.6), math.log(1.6)))
    entries = jnp.clip(jax.random.normal(key_vals, (POINTS, WIDTH), jnp.float32), -4.0, 4.0)
    return (entries * row_scale * col_scale).astype(jnp.bfloat16)


def draw_norm_gain(key, part):
    key = jax.random.fold_in(key, 7)
    return jnp.exp(jax.random.uniform(key, (WIDTH,), jnp.float32, math.log(0.8), math.log(1.25)))


def draw_cell_ids(key, part):
    key = jax.random.fold_in(key, 13)
    block_total = POINTS // P_DEV
    block_keys = jax.random.split(key, block_total)
    lead = P_DEV // 4

    def block_flags(one_key):
        order = jax.random.permutation(one_key, P_DEV - lead)
        tail = (order < CELL_DEV).astype(jnp.int32)
        return jnp.concatenate([jnp.zeros((lead,), jnp.int32), tail])
    flags = jax.vmap(block_flags)(block_keys)
    return jnp.maximum(jnp.cumsum(flags.reshape(-1)) - 1, 0).astype(jnp.int32)


def levels(stream_key, dims, pieces, low, high):
    factor_of = 1.0
    for dim, parts in pieces:
        heights = jax.random.uniform(jax.random.fold_in(jax.random.fold_in(stream_key, 6), dim), (parts,), jnp.float32, low / len(pieces), high / len(pieces))
        factor_of = factor_of * jnp.repeat(jnp.exp(heights), dims[dim] // parts).reshape((-1,) + (1,) * (len(dims) - 1 - dim))
    return factor_of


def length_profile(number_of, total, bound, slope):
    portions = [(1 << 20) // math.isqrt(grade ** slope) + 1 for grade in range(2, number_of + 1)]
    rest, holding = total - bound - (number_of - 1), [1] * (number_of - 1)
    while rest > 0:
        candidates = [i for i in range(number_of - 1) if holding[i] < bound]
        mass, budget = sum([portions[i] for i in candidates]), rest
        for i in candidates:
            extra = min(bound - holding[i], max(1, budget * portions[i] // mass), rest)
            holding[i] = holding[i] + extra
            rest = rest - extra
    return np.array([bound] + holding)


def ragged_sizes(rng, amount, total, reach, slope):
    if amount == 2:
        one = jax.random.randint(rng, (), max(1, total - reach), min(reach, total - 1) + 1)
        return jnp.stack([one, total - one])
    sizes = jnp.asarray(length_profile(amount, total, reach, slope), jnp.int32)
    pairs = (amount - 1) // 2
    donor, taker = sizes[1:1 + 2 * pairs:2], sizes[2:2 + 2 * pairs:2]
    room = jnp.minimum(donor - 1, reach - taker)
    moved = jax.random.randint(jax.random.fold_in(rng, 1), (pairs,), 0, 1 << 20) % (room + 1)
    sizes = sizes.at[1:1 + 2 * pairs:2].set(donor - moved).at[2:2 + 2 * pairs:2].set(taker + moved)
    return sizes[jax.random.permutation(jax.random.fold_in(rng, 2), amount)]


def centred(stream_key, extent, width, limit, shards=(), held_as=jnp.bfloat16):
    values = width * jax.random.normal(stream_key, extent, jnp.float32)
    if shards:
        values = values * levels(stream_key, extent, shards, -0.22, 0.18)
    return jnp.clip(values, -limit, limit).astype(held_as)


def setup_inputs(seed: int = 0) -> dict:
    streams_of = jax.random.split(jax.random.key(seed), 11)
    return {
        "points": draw_points(jax.random.fold_in(streams_of[10], 71), 0),
        "patch_ids": jnp.searchsorted(jnp.cumsum(ragged_sizes(streams_of[1], PATCHES, POINTS, PATCH, 1)), jnp.arange(POINTS), side="right").astype(jnp.int32),
        "cell_ids": draw_cell_ids(jax.random.fold_in(streams_of[10], 71), 0),
        "norm_gain": draw_norm_gain(jax.random.fold_in(streams_of[10], 71), 0),
        "w_qkv": centred(streams_of[4], (WIDTH, 3 * WIDTH), WIDTH ** -0.5, 0.375),
        "w_out": centred(streams_of[5], (WIDTH, WIDTH), WIDTH ** -0.5, 0.375),
        "w_pool": centred(streams_of[6], (WIDTH, POOLED), WIDTH ** -0.5, 0.375),
        "b_pool": centred(streams_of[7], (POOLED,), 1.0, 4.0, (), jnp.float32),
        "pool_gain": jnp.clip(1.0 + 0.1 * jax.random.normal(streams_of[8], (POOLED,), jnp.float32), 0.5, 1.5),
        "cotangent": centred(streams_of[9], (CELLS, POOLED), 1.0, 6.0, ((0, 512),), jnp.float32),
    }


EPS = 1e-05
ROOT_HALF = 0.7071067811865476
ROOT_TWO_PI = 2.5066282746310002

def layer_stats(values):
    centered = values - lax.optimization_barrier(jnp.mean(values, axis=-1, keepdims=True))
    inv_std = lax.rsqrt(lax.optimization_barrier(jnp.mean(centered * centered, axis=-1, keepdims=True)) + EPS)
    return (centered * inv_std, inv_std)

def norm_back(grad_normed, normed, inv_std):
    first_mean = lax.optimization_barrier(jnp.mean(grad_normed, axis=-1, keepdims=True))
    second_mean = lax.optimization_barrier(jnp.mean(grad_normed * normed, axis=-1, keepdims=True))
    return inv_std * (grad_normed - first_mean - normed * second_mean)

def gelu_slope(scaled):
    normal_cdf = 0.5 * (1.0 + jax.scipy.special.erf(scaled * ROOT_HALF))
    return normal_cdf + scaled * jnp.exp(-0.5 * scaled * scaled) / ROOT_TWO_PI

def inner_rows(left, right):
    return lax.dot_general(left, right, (((0,), (0,)), ((), ())), preferred_element_type=jnp.float32)

def against_rows(left, right):
    return lax.dot_general(left, right, (((1,), (1,)), ((), ())), preferred_element_type=jnp.float32)

def pool_rows(sums, counts, w_pool, b_pool, pool_gain, cotangent):
    pooled_mean = (sums / counts[:, None]).astype(jnp.bfloat16)
    pre_norm = jnp.dot(pooled_mean, w_pool, preferred_element_type=jnp.float32) + b_pool
    pooled_normed, pooled_inv = layer_stats(pre_norm)
    slope_grad = cotangent * gelu_slope(pooled_normed * pool_gain)
    grad_pre = norm_back(slope_grad * pool_gain, pooled_normed, pooled_inv)
    grad_pre_b = grad_pre.astype(jnp.bfloat16)
    share = against_rows(grad_pre_b, w_pool) / counts[:, None]
    return (pooled_mean, pooled_normed, slope_grad, grad_pre, grad_pre_b, share)

def pad_rows(array, count):
    widths = [(count, count)] + [(0, 0)] * (array.ndim - 1)
    return jnp.pad(array, widths)

def reference(points, patch_ids, cell_ids, norm_gain, w_qkv, w_out, w_pool, b_pool, pool_gain, cotangent):
    head_size = WIDTH // HEADS
    score_scale = 1.0 / math.sqrt(head_size)
    key_window = QBLOCK + 2 * PATCH
    feats = points.astype(jnp.float32)
    normed, inv_std = layer_stats(feats)
    hidden = (normed * norm_gain).astype(jnp.bfloat16)
    qkv = jnp.dot(hidden, w_qkv, preferred_element_type=jnp.float32).astype(jnp.bfloat16)
    queries = qkv[:, :WIDTH].reshape(POINTS, HEADS, head_size)
    key_rows = qkv[:, WIDTH:2 * WIDTH].reshape(POINTS, HEADS, head_size)
    values = qkv[:, 2 * WIDTH:].reshape(POINTS, HEADS, head_size)
    patch_marks = (patch_ids + 1).astype(jnp.int32)
    key_pad = pad_rows(key_rows, PATCH)
    value_pad = pad_rows(values, PATCH)
    query_pad = pad_rows(queries, PATCH)
    mark_pad = pad_rows(patch_marks, PATCH)
    starts = (jnp.arange(POINTS // QBLOCK) * QBLOCK).astype(jnp.int32)

    def forward_block(start):
        q_tile = lax.dynamic_slice_in_dim(queries, start, QBLOCK, 0).astype(jnp.float32)
        k_tile = lax.dynamic_slice_in_dim(key_pad, start, key_window, 0).astype(jnp.float32)
        v_tile = lax.dynamic_slice_in_dim(value_pad, start, key_window, 0).astype(jnp.float32)
        q_marks = lax.dynamic_slice_in_dim(patch_marks, start, QBLOCK, 0)
        k_marks = lax.dynamic_slice_in_dim(mark_pad, start, key_window, 0)
        visible = (q_marks[:, None] == k_marks[None, :])[None]
        scores = jnp.einsum('qhd,khd->hqk', q_tile, k_tile) * score_scale
        masked = jnp.where(visible, scores, -jnp.inf)
        row_top = lax.optimization_barrier(jnp.max(masked, axis=-1, keepdims=True))
        log_totals = row_top + jnp.log(lax.optimization_barrier(jnp.sum(jnp.exp(masked - row_top), axis=-1, keepdims=True)))
        weights = jnp.where(visible, jnp.exp(scores - log_totals), 0.0).astype(jnp.bfloat16)
        mixed_heads = jnp.einsum('hqk,khd->qhd', weights.astype(jnp.float32), v_tile)
        return (mixed_heads.reshape(QBLOCK, WIDTH).astype(jnp.bfloat16), log_totals[:, :, 0])
    block_outs, block_totals = lax.map(forward_block, starts)
    attended = block_outs.reshape(POINTS, WIDTH)
    log_totals = jnp.transpose(block_totals, (1, 0, 2)).reshape(HEADS, POINTS)
    mixed = (feats + jnp.dot(attended, w_out, preferred_element_type=jnp.float32)).astype(jnp.bfloat16)
    sums = jax.ops.segment_sum(mixed.astype(jnp.float32), cell_ids, num_segments=CELLS)
    counts = jax.ops.segment_sum(jnp.ones((POINTS,), jnp.float32), cell_ids, num_segments=CELLS)
    pooled_mean, pooled_normed, slope_grad, grad_pre, grad_pre_b, share = pool_rows(sums, counts, w_pool, b_pool, pool_gain, cotangent)
    grad_w_pool = inner_rows(pooled_mean, grad_pre_b)
    grad_b_pool = lax.optimization_barrier(jnp.sum(grad_pre, axis=0))
    grad_pool_gain = lax.optimization_barrier(jnp.sum(slope_grad * pooled_normed, axis=0))
    dmixed = jnp.take(share, cell_ids, axis=0)
    dmixed_b = dmixed.astype(jnp.bfloat16)
    grad_w_out = inner_rows(attended, dmixed_b)
    dattended = against_rows(dmixed_b, w_out).astype(jnp.bfloat16)
    deltas = lax.optimization_barrier(jnp.sum((dattended.astype(jnp.float32) * attended.astype(jnp.float32)).reshape(POINTS, HEADS, head_size), axis=-1)).T
    dout_rows = dattended.reshape(POINTS, HEADS, head_size)
    dout_pad = pad_rows(dout_rows, PATCH)
    totals_pad = jnp.pad(log_totals, ((0, 0), (PATCH, PATCH)))
    deltas_pad = jnp.pad(deltas, ((0, 0), (PATCH, PATCH)))

    def pair_terms(scores, visible, totals_tile, delta_tile, dout_tile, value_tile):
        weights = jnp.where(visible, jnp.exp(scores - totals_tile[:, :, None]), 0.0)
        dweights = jnp.einsum('qhd,khd->hqk', dout_tile.astype(jnp.float32), value_tile.astype(jnp.float32))
        dscores = (weights * (dweights - delta_tile[:, :, None]) * score_scale).astype(jnp.bfloat16)
        return (weights.astype(jnp.bfloat16), dscores)

    def query_block(start):
        q_tile = lax.dynamic_slice_in_dim(queries, start, QBLOCK, 0)
        k_tile = lax.dynamic_slice_in_dim(key_pad, start, key_window, 0)
        v_tile = lax.dynamic_slice_in_dim(value_pad, start, key_window, 0)
        q_marks = lax.dynamic_slice_in_dim(patch_marks, start, QBLOCK, 0)
        k_marks = lax.dynamic_slice_in_dim(mark_pad, start, key_window, 0)
        visible = (q_marks[:, None] == k_marks[None, :])[None]
        scores = jnp.einsum('qhd,khd->hqk', q_tile.astype(jnp.float32), k_tile.astype(jnp.float32)) * score_scale
        totals_tile = lax.dynamic_slice_in_dim(log_totals, start, QBLOCK, 1)
        delta_tile = lax.dynamic_slice_in_dim(deltas, start, QBLOCK, 1)
        dout_tile = lax.dynamic_slice_in_dim(dout_rows, start, QBLOCK, 0)
        weights_b, dscores = pair_terms(scores, visible, totals_tile, delta_tile, dout_tile, v_tile)
        dquery = jnp.einsum('hqk,khd->qhd', dscores.astype(jnp.float32), k_tile.astype(jnp.float32))
        return dquery.reshape(QBLOCK, WIDTH)

    def key_block(start):
        k_tile = lax.dynamic_slice_in_dim(key_rows, start, QBLOCK, 0)
        v_tile = lax.dynamic_slice_in_dim(values, start, QBLOCK, 0)
        q_tile = lax.dynamic_slice_in_dim(query_pad, start, key_window, 0)
        dout_tile = lax.dynamic_slice_in_dim(dout_pad, start, key_window, 0)
        q_marks = lax.dynamic_slice_in_dim(mark_pad, start, key_window, 0)
        k_marks = lax.dynamic_slice_in_dim(patch_marks, start, QBLOCK, 0)
        visible = (q_marks[:, None] == k_marks[None, :])[None]
        scores = jnp.einsum('qhd,khd->hqk', q_tile.astype(jnp.float32), k_tile.astype(jnp.float32)) * score_scale
        totals_tile = lax.dynamic_slice_in_dim(totals_pad, start, key_window, 1)
        delta_tile = lax.dynamic_slice_in_dim(deltas_pad, start, key_window, 1)
        weights_b, dscores = pair_terms(scores, visible, totals_tile, delta_tile, dout_tile, v_tile)
        dkey = jnp.einsum('hqk,qhd->khd', dscores.astype(jnp.float32), q_tile.astype(jnp.float32))
        dvalue = jnp.einsum('hqk,qhd->khd', weights_b.astype(jnp.float32), dout_tile.astype(jnp.float32))
        return jnp.concatenate([dkey.reshape(QBLOCK, WIDTH), dvalue.reshape(QBLOCK, WIDTH)], axis=1)
    dquery = lax.map(query_block, starts).reshape(POINTS, WIDTH)
    dkeyval = lax.map(key_block, starts).reshape(POINTS, 2 * WIDTH)
    dqkv = jnp.concatenate([dquery, dkeyval], axis=1).astype(jnp.bfloat16)
    grad_qkv = inner_rows(hidden, dqkv)
    dhidden = against_rows(dqkv, w_qkv)
    grad_norm_gain = lax.optimization_barrier(jnp.sum(dhidden * normed, axis=0))
    grad_points = dmixed + norm_back(dhidden * norm_gain, normed, inv_std)
    grad_scale = 1.0 / math.sqrt(POINTS)
    return (grad_points, grad_qkv * grad_scale, grad_w_out * grad_scale, grad_norm_gain * grad_scale, grad_w_pool * grad_scale, grad_b_pool * grad_scale, grad_pool_gain * grad_scale)
```

```python
import functools
import math

import jax
import jax.numpy as jnp
from jax import lax
from jax.experimental import pallas as pl
from jax.experimental.pallas import tpu as pltpu
from jax.sharding import PartitionSpec as P

PATCH = 512


EPS = 1e-05
ROOT_HALF = 0.7071067811865476
ROOT_TWO_PI = 2.5066282746310002


def padded(block, sides, width):
    for axis, dim in sides:
        count = lax.axis_size(axis)
        forward = [(i, i + 1) for i in range(count - 1)]
        backward = [(target, source) for source, target in forward]
        low = lax.ppermute(
            lax.slice_in_dim(block, block.shape[dim] - width, None, axis=dim), axis, forward
        )
        high = lax.ppermute(lax.slice_in_dim(block, 0, width, axis=dim), axis, backward)
        block = jnp.concatenate([low, block, high], axis=dim)
    return block


def from_behind(value, axis, steps):
    count = lax.axis_size(axis)
    initial, last = (max(0, -steps), min(count, count - steps))
    return lax.ppermute(value, axis, [(source, source + steps) for source in range(initial, last)])


def layer_stats(values):
    centered = values - jnp.mean(values, axis=-1, keepdims=True)
    inv_std = lax.rsqrt(jnp.mean(centered * centered, axis=-1, keepdims=True) + EPS)
    return (centered * inv_std, inv_std)


def norm_back(grad_normed, normed, inv_std):
    first_mean = jnp.mean(grad_normed, axis=-1, keepdims=True)
    second_mean = jnp.mean(grad_normed * normed, axis=-1, keepdims=True)
    return inv_std * (grad_normed - first_mean - normed * second_mean)


def gelu_slope(scaled):
    normal_cdf = 0.5 * (1.0 + jax.scipy.special.erf(scaled * ROOT_HALF))
    return normal_cdf + scaled * jnp.exp(-0.5 * scaled * scaled) / ROOT_TWO_PI


def inner_rows(left, right):
    return lax.dot_general(
        left, right, (((0,), (0,)), ((), ())), preferred_element_type=jnp.float32
    )


def against_rows(left, right):
    return lax.dot_general(
        left, right, (((1,), (1,)), ((), ())), preferred_element_type=jnp.float32
    )


def pool_rows(sums, counts, w_pool, b_pool, pool_gain, cotangent):
    pooled_mean = (sums / counts[:, None]).astype(jnp.bfloat16)
    pre_norm = jnp.dot(pooled_mean, w_pool, preferred_element_type=jnp.float32) + b_pool
    pooled_normed, pooled_inv = layer_stats(pre_norm)
    slope_grad = cotangent * gelu_slope(pooled_normed * pool_gain)
    grad_pre = norm_back(slope_grad * pool_gain, pooled_normed, pooled_inv)
    grad_pre_b = grad_pre.astype(jnp.bfloat16)
    share = against_rows(grad_pre_b, w_pool) / counts[:, None]
    return (pooled_mean, pooled_normed, slope_grad, grad_pre, grad_pre_b, share)


HALF = 128
PER_HALF = 8
HEAD_SIZE = 16
TILE = 256
CHUNK = 256
WINDOW = 3 * PATCH
FAR = float(2**30)
DIGIT = 32
LOG_LANE = 64


def head_lanes(h):
    lane = lax.broadcasted_iota(jnp.int32, (1, 2 * HALF), 1)
    own = (lane >= h * HEAD_SIZE) & (lane < (h + 1) * HEAD_SIZE)
    marks = (lane >= HALF) & (lane < HALF + LOG_LANE)
    terms = (lane >= HALF + LOG_LANE) & (lane < HALF + LOG_LANE + 24) & (lane % PER_HALF == h)
    return (own | marks | terms).astype(jnp.float32).astype(jnp.bfloat16)


def three_terms(columns):
    lane = lax.broadcasted_iota(jnp.int32, (1, HALF), 1)
    placed = jnp.zeros((columns[0].shape[0], HALF), jnp.float32)
    for h, column in enumerate(columns):
        here = (lane >= LOG_LANE) & (lane < LOG_LANE + 24) & (lane % PER_HALF == h)
        placed = jnp.where(here, column, placed)
    first = placed.astype(jnp.bfloat16).astype(jnp.float32)
    second = (placed - first).astype(jnp.bfloat16).astype(jnp.float32)
    third = placed - first - second
    which = (lane - LOG_LANE) // PER_HALF
    return jnp.where(which == 0, first, jnp.where(which == 1, second, third))


def forward_kernel(spans, q_ref, f_ref, kg_ref, v_ref, att_ref, logs_ref, qf, kept, top, total):
    tile = pl.program_id(1)
    start, count = spans[tile, 0], spans[tile, 1]
    both = jnp.concatenate([q_ref[...], f_ref[...]], axis=1)
    for h in range(PER_HALF):
        qf[h] = both * head_lanes(h)
        top[h] = jnp.full((TILE, HALF), -3e38, jnp.float32)
        total[h] = jnp.zeros((TILE, HALF), jnp.float32)

    def score_chunk(c, carry):
        kg = kg_ref[pl.ds(pl.multiple_of(start + c * CHUNK, 16), CHUNK), :]
        for h in range(PER_HALF):
            scores = against_rows(qf[h], kg)
            kept[c, h] = scores
            top[h] = jnp.maximum(top[h], jnp.maximum(scores[:, :HALF], scores[:, HALF:]))
        return carry

    lax.fori_loop(0, count, score_chunk, 0)
    for h in range(PER_HALF):
        top[h] = jnp.broadcast_to(jnp.max(top[h], axis=1, keepdims=True), (TILE, HALF))

    def weigh_chunk(c, acc):
        values = v_ref[pl.ds(pl.multiple_of(start + c * CHUNK, 16), CHUNK), :]
        for h in range(PER_HALF):
            shift = top[h]
            left = jnp.exp(kept[c, h, :, :HALF] - shift)
            right = jnp.exp(kept[c, h, :, HALF:] - shift)
            total[h] += left + right
            weights = jnp.concatenate([left, right], axis=1).astype(jnp.bfloat16)
            acc = acc + jnp.dot(
                weights, values * head_lanes(h)[:, :HALF], preferred_element_type=jnp.float32
            )
        return acc

    acc = lax.fori_loop(0, count, weigh_chunk, jnp.zeros((TILE, HALF), jnp.float32))
    lane = lax.broadcasted_iota(jnp.int32, (1, HALF), 1)
    factor = jnp.zeros((TILE, HALF), jnp.float32)
    logs = []
    for h in range(PER_HALF):
        row_total = jnp.sum(total[h], axis=1, keepdims=True)
        factor = jnp.where(lane // HEAD_SIZE == h, 1.0 / row_total, factor)
        logs.append(-(top[h][:, :1] + jnp.log(row_total)))
    att_ref[...] = (acc * factor).astype(jnp.bfloat16)
    logs_ref[...] = (f_ref[...].astype(jnp.float32) + three_terms(logs)).astype(jnp.bfloat16)


def attend(spans, queries, marks_f, keys_g, values):
    return pl.pallas_call(
        forward_kernel,
        grid=(2, 2),
        out_shape=[
            jax.ShapeDtypeStruct((512, 256), jnp.bfloat16),
            jax.ShapeDtypeStruct((2, 512, HALF), jnp.bfloat16),
        ],
        in_specs=[
            pl.BlockSpec(memory_space=pltpu.SMEM),
            pl.BlockSpec((TILE, HALF), lambda g, t: (t, g)),
            pl.BlockSpec((TILE, HALF), lambda g, t: (t, 0)),
            pl.BlockSpec((None, WINDOW, 2 * HALF), lambda g, t: (g, 0, 0)),
            pl.BlockSpec((WINDOW, HALF), lambda g, t: (0, g)),
        ],
        out_specs=[
            pl.BlockSpec((TILE, HALF), lambda g, t: (t, g)),
            pl.BlockSpec((None, TILE, HALF), lambda g, t: (g, t, 0)),
        ],
        scratch_shapes=[
            pltpu.VMEM((PER_HALF, TILE, 2 * HALF), jnp.bfloat16),
            pltpu.VMEM((WINDOW // CHUNK, PER_HALF, TILE, CHUNK), jnp.float32),
            pltpu.VMEM((PER_HALF, TILE, HALF), jnp.float32),
            pltpu.VMEM((PER_HALF, TILE, HALF), jnp.float32),
        ],
        compiler_params=pltpu.CompilerParams(vmem_limit_bytes=48 * 1024 * 1024),
        name="attention",
    )(spans, queries, marks_f, keys_g, values)


def backward_kernel(
    spans, q_ref, logs_ref, do_ref, deltas_ref, kg_ref, vg_ref, dq_ref, dk_ref, dv_ref, qf, df, dqt
):
    tile = pl.program_id(1)
    start, count = spans[tile, 0], spans[tile, 1]
    q_both = jnp.concatenate([q_ref[...], logs_ref[...]], axis=1)
    d_both = jnp.concatenate([do_ref[...], deltas_ref[...]], axis=1)
    for h in range(PER_HALF):
        lanes = head_lanes(h)
        qf[h] = q_both * lanes
        df[h] = d_both * lanes
    dqt[...] = jnp.zeros_like(dqt)

    @pl.when(tile == 0)
    def _():
        dk_ref[...] = jnp.zeros_like(dk_ref)
        dv_ref[...] = jnp.zeros_like(dv_ref)

    def chunk(c, carry):
        rows = pl.ds(pl.multiple_of(start + c * CHUNK, 16), CHUNK)
        kg = kg_ref[rows, :]
        vg = vg_ref[rows, :]
        keys_t = kg[:, :HALF].astype(jnp.float32).T.astype(jnp.bfloat16)
        dk = jnp.zeros((CHUNK, HALF), jnp.float32)
        dv = jnp.zeros((CHUNK, HALF), jnp.float32)
        for h in range(PER_HALF):
            weights = jnp.exp(against_rows(kg, qf[h]))
            dscores = (weights * against_rows(vg, df[h])).astype(jnp.bfloat16)
            dk = dk + jnp.dot(dscores, qf[h, :, :HALF], preferred_element_type=jnp.float32)
            dv = dv + jnp.dot(
                weights.astype(jnp.bfloat16), df[h, :, :HALF], preferred_element_type=jnp.float32
            )
            own = slice(h * HEAD_SIZE, (h + 1) * HEAD_SIZE)
            dqt[own, :] += jnp.dot(keys_t[own], dscores, preferred_element_type=jnp.float32)
        dk_ref[rows, :] += dk * 4.0
        dv_ref[rows, :] += dv * 4.0
        return carry

    lax.fori_loop(0, count, chunk, 0)
    dq_ref[...] = dqt[...].T.astype(jnp.bfloat16)


def attend_back(spans, queries, logs, douts, deltas, keys_g, values_g):
    tall = pl.BlockSpec((None, WINDOW, 2 * HALF), lambda g, t: (g, 0, 0))
    mine = pl.BlockSpec((TILE, HALF), lambda g, t: (t, g))
    terms = pl.BlockSpec((None, TILE, HALF), lambda g, t: (g, t, 0))
    sums = pl.BlockSpec((WINDOW, HALF), lambda g, t: (0, g))
    return pl.pallas_call(
        backward_kernel,
        grid=(2, 2),
        out_shape=[
            jax.ShapeDtypeStruct((512, 256), jnp.bfloat16),
            jax.ShapeDtypeStruct((WINDOW, 256), jnp.float32),
            jax.ShapeDtypeStruct((WINDOW, 256), jnp.float32),
        ],
        in_specs=[pl.BlockSpec(memory_space=pltpu.SMEM), mine, terms, mine, terms, tall, tall],
        out_specs=[mine, sums, sums],
        scratch_shapes=[
            pltpu.VMEM((PER_HALF, TILE, 2 * HALF), jnp.bfloat16),
            pltpu.VMEM((PER_HALF, TILE, 2 * HALF), jnp.bfloat16),
            pltpu.VMEM((HALF, TILE), jnp.float32),
        ],
        compiler_params=pltpu.CompilerParams(vmem_limit_bytes=48 * 1024 * 1024),
        name="attention_back",
    )(spans, queries, logs, douts, deltas, keys_g, values_g)


MESH = pl.DeviceIdType.MESH
RANKS = 8
UNIT = 128
SHARD = 3 * UNIT
PIECE = SHARD // RANKS
EXTRA = 16


def places():
    me = lax.axis_index("pts")
    core, z, y, x = me % 2, (me // 2) % 8, (me // 16) % 8, me // 128
    wide = (x * 2 + core, lambda r: (r // 2) * 128 + y * 16 + z * 2 + r % 2)
    middle = (y, lambda r: x * 128 + r * 16 + z * 2 + core)
    near = (z, lambda r: x * 128 + y * 16 + r * 2 + core)
    return wide, middle, near


def swap(place, source, landing, send_sem, recv_sem):
    rank, device = place
    copies = []
    for k in range(1, RANKS):
        peer = (rank + k) % RANKS
        copy = pltpu.make_async_remote_copy(
            src_ref=source(peer),
            dst_ref=landing(rank),
            send_sem=send_sem.at[k - 1],
            recv_sem=recv_sem.at[k - 1],
            device_id=(device(peer),),
            device_id_type=MESH,
        )
        copy.start()
        copies.append(copy)
    return copies


def greet(groups):
    barrier = pltpu.get_barrier_semaphore()
    for rank, device in groups:
        for k in range(1, RANKS):
            pl.semaphore_signal(
                barrier, inc=1, device_id=(device((rank + k) % RANKS),), device_id_type=MESH
            )
    pl.semaphore_wait(barrier, len(groups) * (RANKS - 1))


def slot_sum(ref, start, size):
    total = ref[0, start : start + size, :].astype(jnp.float32)
    for r in range(1, RANKS):
        total = total + ref[r, start : start + size, :].astype(jnp.float32)
    return total


def reduce_kernel(
    scale, gq, go, gn, gp, gb, gg, oq, oo, on, op, ob, og,
    send_a, recv_a, send_b, recv_b, recv_c, gather_b, gather_a, send_sems, recv_sems,
):
    wide, middle, near = places()
    for unit in range(24):
        column = unit // 2 * UNIT
        rows = slice(unit % 2 * UNIT, unit % 2 * UNIT + UNIT)
        if column < 768:
            block = gq[rows, column : column + UNIT]
        elif column < 1024:
            block = go[rows, column - 768 : column - 768 + UNIT]
        else:
            block = gp[rows, column - 1024 : column - 1024 + UNIT]
        start = unit % 3 * UNIT
        send_a[unit // 3, start : start + UNIT, :] = (block * scale).astype(jnp.bfloat16)
    pieces = [gn[:, i * UNIT : (i + 1) * UNIT] for i in range(2)]
    pieces += [gb[:, i * UNIT : (i + 1) * UNIT] for i in range(4)]
    pieces += [gg[:, i * UNIT : (i + 1) * UNIT] for i in range(4)]
    pieces += [jnp.zeros((EXTRA - 10, UNIT), jnp.float32)]
    extra = (jnp.concatenate(pieces, axis=0) * scale).astype(jnp.bfloat16)
    for r in range(RANKS):
        send_a[r, SHARD:, :] = extra
    greet((wide, middle, near))

    copies = swap(wide, lambda r: send_a.at[r], lambda r: recv_a.at[r], send_sems.at[0], recv_sems.at[0])
    recv_a[wide[0]] = send_a[wide[0]]
    for copy in copies:
        copy.wait()
    extra = slot_sum(recv_a, SHARD, EXTRA).astype(jnp.bfloat16)
    for r in range(RANKS):
        send_b[r, :PIECE, :] = slot_sum(recv_a, r * PIECE, PIECE).astype(jnp.bfloat16)
        send_b[r, PIECE:, :] = extra

    copies = swap(middle, lambda r: send_b.at[r], lambda r: recv_b.at[r], send_sems.at[1], recv_sems.at[1])
    recv_b[middle[0]] = send_b[middle[0]]
    for copy in copies:
        copy.wait()
    recv_c[near[0]] = slot_sum(recv_b, 0, PIECE + EXTRA).astype(jnp.bfloat16)

    copies = swap(near, lambda r: recv_c.at[near[0]], lambda r: recv_c.at[r], send_sems.at[2], recv_sems.at[2])
    for copy in copies:
        copy.wait()
    total = slot_sum(recv_c, 0, PIECE + EXTRA)
    gather_b[middle[0]] = total[:PIECE].astype(jnp.bfloat16)

    copies = swap(middle, lambda r: gather_b.at[middle[0]], lambda r: gather_b.at[r], send_sems.at[3], recv_sems.at[3])
    extra = total[PIECE:]
    for i in range(2):
        on[:, i * UNIT : (i + 1) * UNIT] = extra[i : i + 1]
    for i in range(4):
        ob[:, i * UNIT : (i + 1) * UNIT] = extra[2 + i : 3 + i]
        og[:, i * UNIT : (i + 1) * UNIT] = extra[6 + i : 7 + i]
    for copy in copies:
        copy.wait()
    gather_a[wide[0]] = gather_b[...]
    copies = swap(wide, lambda r: gather_b, lambda r: gather_a.at[r], send_sems.at[4], recv_sems.at[4])
    for copy in copies:
        copy.wait()
    for unit in range(24):
        column = unit // 2 * UNIT
        first = unit % 2 * UNIT
        for part in range(8):
            at = unit % 3 * UNIT + part * 16
            block = gather_a[unit // 3, at // PIECE, at % PIECE : at % PIECE + 16, :].astype(jnp.float32)
            rows = slice(first + part * 16, first + part * 16 + 16)
            if column < 768:
                oq[rows, column : column + UNIT] = block
            elif column < 1024:
                oo[rows, column - 768 : column - 768 + UNIT] = block
            else:
                op[rows, column - 1024 : column - 1024 + UNIT] = block


def reduce_all(scale, grad_qkv, grad_out, grad_gain, grad_pool, grad_bias, grad_pgain):
    arrays = (grad_qkv, grad_out, grad_gain, grad_pool, grad_bias, grad_pgain)
    vmem = pl.BlockSpec(memory_space=pltpu.VMEM)
    half = jnp.bfloat16
    return pl.pallas_call(
        functools.partial(reduce_kernel, scale),
        out_shape=[jax.ShapeDtypeStruct(a.shape, jnp.float32) for a in arrays],
        in_specs=[vmem] * 6,
        out_specs=[vmem] * 6,
        scratch_shapes=[
            pltpu.VMEM((RANKS, SHARD + EXTRA, UNIT), half),
            pltpu.VMEM((RANKS, SHARD + EXTRA, UNIT), half),
            pltpu.VMEM((RANKS, PIECE + EXTRA, UNIT), half),
            pltpu.VMEM((RANKS, PIECE + EXTRA, UNIT), half),
            pltpu.VMEM((RANKS, PIECE + EXTRA, UNIT), half),
            pltpu.VMEM((RANKS, PIECE, UNIT), half),
            pltpu.VMEM((RANKS, RANKS, PIECE, UNIT), half),
            pltpu.SemaphoreType.DMA((5, RANKS - 1)),
            pltpu.SemaphoreType.DMA((5, RANKS - 1)),
        ],
        compiler_params=pltpu.CompilerParams(
            collective_id=5, has_side_effects=True, vmem_limit_bytes=24 * 1024 * 1024
        ),
        name="parameter_gradients",
    )(*arrays)


def key_spans(patch_marks, marks_ext):
    spans = []
    for t in range(2):
        first, last = patch_marks[t * TILE], patch_marks[(t + 1) * TILE - 1]
        low = jnp.sum((marks_ext[: 2 * PATCH] < first).astype(jnp.int32))
        upper = marks_ext[PATCH:]
        high = PATCH + jnp.sum(((upper > 0) & (upper <= last)).astype(jnp.int32))
        low = low // 16 * 16
        count = (high - low + CHUNK - 1) // CHUNK
        spans.append(jnp.stack([jnp.minimum(low, WINDOW - count * CHUNK), count]))
    return jnp.stack(spans)


def mark_digits(marks):
    lane = jnp.arange(HALF, dtype=jnp.int32)[None, :]
    high, low = marks[:, None] // DIGIT, marks[:, None] % DIGIT
    return jnp.where(lane < DIGIT, lane == high, lane - DIGIT == low) & (lane < LOG_LANE)


def body(
    points, patch_ids, cell_ids, norm_gain, w_qkv, w_out, w_pool, b_pool, pool_gain, cotangent
):
    row_count, feat_width = points.shape
    cell_count = cotangent.shape[0]
    lane = jnp.arange(HALF, dtype=jnp.int32)[None, :]
    patch_marks = patch_ids + 1
    marks_ext = padded(patch_marks, (("pts", 0),), PATCH)
    points_ext = padded(points, (("pts", 0),), PATCH)
    spans = key_spans(patch_marks, marks_ext)
    digits = mark_digits(marks_ext)
    terms_on = (lane >= LOG_LANE) & (lane < LOG_LANE + 24)
    marks_g = (digits | terms_on).astype(jnp.bfloat16)
    own_digits = digits[PATCH : PATCH + row_count]
    marks_f = jnp.where(own_digits | (lane >= LOG_LANE), 0.0, -FAR).astype(jnp.bfloat16)
    normed_ext, inv_ext = layer_stats(points_ext.astype(jnp.float32))
    hidden_ext = (normed_ext * norm_gain).astype(jnp.bfloat16)
    qkv_ext = jnp.dot(hidden_ext, w_qkv, preferred_element_type=jnp.float32).astype(jnp.bfloat16)
    own = slice(PATCH, PATCH + row_count)
    feats = points.astype(jnp.float32)
    normed, inv_std, hidden = normed_ext[own], inv_ext[own], hidden_ext[own]
    queries = qkv_ext[own, :feat_width] * jnp.bfloat16(0.25)
    keys_g = jnp.stack(
        [jnp.concatenate([qkv_ext[:, 256 + g * HALF : 384 + g * HALF], marks_g], axis=1) for g in range(2)]
    )
    values = qkv_ext[:, 2 * feat_width :]
    values_g = jnp.stack(
        [jnp.concatenate([values[:, g * HALF : (g + 1) * HALF], marks_g], axis=1) for g in range(2)]
    )
    attended, logs = attend(spans, queries, marks_f, keys_g, values)

    mixed = (feats + jnp.dot(attended, w_out, preferred_element_type=jnp.float32)).astype(
        jnp.bfloat16
    )
    local_cells = cell_ids - lax.axis_index("pts") * cell_count
    slots = jnp.arange(cell_count, dtype=jnp.int32)
    member = slots[:, None] == local_cells[None, :]
    sums = jnp.dot(member.astype(jnp.bfloat16), mixed, preferred_element_type=jnp.float32)
    counts = jnp.sum(member.astype(jnp.float32), axis=1)
    leading = local_cells < 0
    lead_sum = jnp.dot(
        leading.astype(jnp.bfloat16)[None, :], mixed, preferred_element_type=jnp.float32
    )
    lead_count = jnp.sum(leading.astype(jnp.float32))
    lead_pack = jnp.concatenate(
        [lead_sum, jnp.full((1, feat_width), lead_count, jnp.float32)], axis=0
    )
    from_next = from_behind(lead_pack, "pts", -1)
    sums_all = sums.at[cell_count - 1].add(from_next[0])
    counts_all = counts.at[cell_count - 1].add(from_next[1, 0])
    pooled_mean, pooled_normed, slope_grad, grad_pre, grad_pre_b, share = pool_rows(
        sums_all, counts_all, w_pool, b_pool, pool_gain, cotangent
    )
    lead_share = from_behind(share[cell_count - 1 :], "pts", 1)[0]
    grad_w_pool = inner_rows(pooled_mean, grad_pre_b)
    grad_b_pool = jnp.sum(grad_pre, axis=0)
    grad_pool_gain = jnp.sum(slope_grad * pooled_normed, axis=0)
    dmixed = jnp.where(
        leading[:, None], lead_share[None, :], jnp.take(share, jnp.maximum(local_cells, 0), axis=0)
    )
    dmixed_b = dmixed.astype(jnp.bfloat16)
    grad_w_out = inner_rows(attended, dmixed_b)
    grad_scale = 1.0 / math.sqrt(row_count * lax.axis_size("pts"))
    dattended = against_rows(dmixed_b, w_out).astype(jnp.bfloat16)
    deltas = jnp.sum(
        (dattended.astype(jnp.float32) * attended.astype(jnp.float32)).reshape(row_count, 2, PER_HALF, HEAD_SIZE),
        axis=-1,
    ) * -0.25
    first = deltas.astype(jnp.bfloat16)
    second = (deltas - first.astype(jnp.float32)).astype(jnp.bfloat16)
    third = (deltas - first.astype(jnp.float32) - second.astype(jnp.float32)).astype(jnp.bfloat16)
    zeros = jnp.zeros((2, row_count, LOG_LANE), jnp.bfloat16)
    delta_terms = jnp.concatenate(
        [zeros] + [jnp.moveaxis(part, 1, 0) for part in (first, second, third)] + [zeros[:, :, :40]], axis=2
    )
    dquery, dkey_ext, dvalue_ext = attend_back(
        spans, queries, logs, dattended * jnp.bfloat16(0.25), delta_terms, keys_g, values_g
    )
    dkv_ext = jnp.concatenate([dkey_ext, dvalue_ext], axis=1)
    rim_pack = jnp.concatenate([dkv_ext[:PATCH], dkv_ext[PATCH + row_count :]], axis=0)
    rim_back = padded(rim_pack.astype(jnp.bfloat16), (("pts", 0),), PATCH).astype(jnp.float32)
    from_prev = rim_back[:PATCH]
    from_next_rows = rim_back[3 * PATCH :]
    dkv_own = dkv_ext[PATCH : PATCH + row_count] + from_prev + from_next_rows
    dqkv = jnp.concatenate([dquery, dkv_own.astype(jnp.bfloat16)], axis=1)
    grad_qkv = inner_rows(hidden, dqkv)
    dhidden = against_rows(dqkv, w_qkv)
    grad_norm_gain = jnp.sum(dhidden * normed, axis=0)
    grad_points = dmixed + norm_back(dhidden * norm_gain, normed, inv_std)
    summed = reduce_all(
        grad_scale, grad_qkv, grad_w_out, grad_norm_gain[None], grad_w_pool, grad_b_pool[None], grad_pool_gain[None]
    )
    return (grad_points, summed[0], summed[1], summed[2][0], summed[3], summed[4][0], summed[5][0])


def solution(mesh):
    in_specs = (P("pts", None), P("pts"), P("pts"), P(), P(), P(), P(), P(), P(), P("pts", None))
    out_specs = (P("pts", None), P(), P(), P(), P(), P(), P())
    return jax.shard_map(body, mesh=mesh, in_specs=in_specs, out_specs=out_specs, check_vma=False)
```

```python
import functools
import math

import jax
import jax.numpy as jnp
from jax import lax
from jax.experimental import pallas as pl
from jax.experimental.pallas import tpu as pltpu
from jax.sharding import PartitionSpec as P

PATCH = 512
MESH = pl.DeviceIdType.MESH


EPS = 1e-05
ROOT_HALF = 0.7071067811865476
ROOT_TWO_PI = 2.5066282746310002


def layer_stats(values):
    centered = values - jnp.mean(values, axis=-1, keepdims=True)
    inv_std = lax.rsqrt(jnp.mean(centered * centered, axis=-1, keepdims=True) + EPS)
    return (centered * inv_std, inv_std)


def norm_back(grad_normed, normed, inv_std):
    first_mean = jnp.mean(grad_normed, axis=-1, keepdims=True)
    second_mean = jnp.mean(grad_normed * normed, axis=-1, keepdims=True)
    return inv_std * (grad_normed - first_mean - normed * second_mean)


def gelu_slope(scaled):
    normal_cdf = 0.5 * (1.0 + lax.erf(scaled * ROOT_HALF))
    return normal_cdf + scaled * jnp.exp(-0.5 * scaled * scaled) / ROOT_TWO_PI


def inner_rows(left, right):
    return lax.dot_general(
        left, right, (((0,), (0,)), ((), ())), preferred_element_type=jnp.float32
    )


def against_rows(left, right):
    return lax.dot_general(
        left, right, (((1,), (1,)), ((), ())), preferred_element_type=jnp.float32
    )


HALF = 128
PER_HALF = 8
HEAD_SIZE = 16
TILE = 256
CHUNK = 256
WINDOW = 3 * PATCH
FAR = float(2**30)
DIGIT = 32
LOG_LANE = 64


def head_lanes(h):
    lane = lax.broadcasted_iota(jnp.int32, (1, 2 * HALF), 1)
    own = (lane >= h * HEAD_SIZE) & (lane < (h + 1) * HEAD_SIZE)
    marks = (lane >= HALF) & (lane < HALF + LOG_LANE)
    terms = (lane >= HALF + LOG_LANE) & (lane < HALF + LOG_LANE + 24) & (lane % PER_HALF == h)
    return (own | marks | terms).astype(jnp.float32).astype(jnp.bfloat16)


def three_terms(columns):
    lane = lax.broadcasted_iota(jnp.int32, (1, HALF), 1)
    placed = jnp.zeros((columns[0].shape[0], HALF), jnp.float32)
    for h, column in enumerate(columns):
        here = (lane >= LOG_LANE) & (lane < LOG_LANE + 24) & (lane % PER_HALF == h)
        placed = jnp.where(here, column, placed)
    first = placed.astype(jnp.bfloat16).astype(jnp.float32)
    second = (placed - first).astype(jnp.bfloat16).astype(jnp.float32)
    third = placed - first - second
    which = (lane - LOG_LANE) // PER_HALF
    return jnp.where(which == 0, first, jnp.where(which == 1, second, third))


def neighbours():
    me = lax.axis_index("pts")
    count = lax.axis_size("pts")
    return me, (me + count - 1) % count, (me + 1) % count


def greet_neighbours(before, after):
    barrier = pltpu.get_barrier_semaphore()
    for device in (before, after):
        pl.semaphore_signal(barrier, inc=1, device_id=(device,), device_id_type=MESH)
    pl.semaphore_wait(barrier, 2)


def send(source, landing, sems, index, device):
    copy = pltpu.make_async_remote_copy(
        src_ref=source,
        dst_ref=landing,
        send_sem=sems.at[0, index],
        recv_sem=sems.at[1, index],
        device_id=(device,),
        device_id_type=MESH,
    )
    copy.start()
    return copy


def digit_columns(marks):
    row = lax.broadcasted_iota(jnp.int32, (HALF, HALF), 0)
    high, low = marks // DIGIT, marks % DIGIT
    hit = ((row < DIGIT) & (row == high)) | ((row >= DIGIT) & (row < LOG_LANE) & (row - DIGIT == low))
    return hit.astype(jnp.float32).T


def prepare_kernel(
    points, ids, gain, w_qkv, q_ref, kg_ref, vg_ref, f_ref, hidden_ref, spans_ref,
    marks, marks_low, marks_high, rows_low, rows_high, sems,
):
    me, before, after = neighbours()
    marks[...] = jnp.zeros_like(marks)
    marks[:4, :] = ids[...] + 1
    greet_neighbours(before, after)
    copies = [
        send(points, rows_high, sems, 0, before),
        send(points, rows_low, sems, 1, after),
        send(marks, marks_high, sems, 2, before),
        send(marks, marks_low, sems, 3, after),
    ]

    def project(block, first, columns):
        normed, _ = layer_stats(block[...].astype(jnp.float32))
        hidden = (normed * gain[...]).astype(jnp.bfloat16)
        hidden_ref[first : first + PATCH, :] = hidden
        return jnp.dot(hidden, w_qkv[:, columns], preferred_element_type=jnp.float32)

    def place(first, keys, values):
        for g in range(2):
            lanes = slice(g * HALF, (g + 1) * HALF)
            kg_ref[g, first : first + PATCH, :HALF] = keys[:, lanes].astype(jnp.bfloat16)
            vg_ref[g, first : first + PATCH, :HALF] = values[:, lanes].astype(jnp.bfloat16)

    def place_marks(block, first, own):
        lane = lax.broadcasted_iota(jnp.int32, (HALF, HALF), 1)
        terms = (lane >= LOG_LANE) & (lane < LOG_LANE + 24)
        for i in range(4):
            rows = slice(first + i * HALF, first + (i + 1) * HALF)
            digits = digit_columns(block[i : i + 1, :])
            both = jnp.where(terms, 1.0, digits).astype(jnp.bfloat16)
            for g in range(2):
                kg_ref[g, rows, HALF:] = both
                vg_ref[g, rows, HALF:] = both
            if own:
                away = jnp.where(lane < LOG_LANE, (1.0 - digits) * -FAR, 0.0)
                f_ref[i * HALF : (i + 1) * HALF, :] = away.astype(jnp.bfloat16)

    qkv = project(points, PATCH, slice(None))
    q_ref[...] = (qkv[:, :256].astype(jnp.bfloat16).astype(jnp.float32) * 0.25).astype(jnp.bfloat16)
    place(PATCH, qkv[:, 256:512], qkv[:, 512:])
    own = marks[...]
    place_marks(own, PATCH, True)
    for copy in copies[2:]:
        copy.wait()
    low = jnp.where(me == 0, 0, marks_low[...])
    high = jnp.where(me == lax.axis_size("pts") - 1, 0, marks_high[...])
    place_marks(low, 0, False)
    place_marks(high, 2 * PATCH, False)
    own_f, low_f, high_f = (block[:4].astype(jnp.float32) for block in (own, low, high))
    for t in range(2):
        first = jnp.min(own_f[2 * t : 2 * t + 2])
        last = jnp.max(own_f[2 * t : 2 * t + 2])
        lower = jnp.sum((low_f < first).astype(jnp.float32) + (own_f < first).astype(jnp.float32))
        upper = jnp.sum(
            ((high_f > 0) & (high_f <= last)).astype(jnp.float32) + (own_f <= last).astype(jnp.float32)
        )
        lower = lower.astype(jnp.int32) // 16 * 16
        count = (PATCH + upper.astype(jnp.int32) - lower + CHUNK - 1) // CHUNK
        spans_ref[t, 0] = jnp.minimum(lower, WINDOW - count * CHUNK)
        spans_ref[t, 1] = count
    for copy, block, first in ((copies[1], rows_low, 0), (copies[0], rows_high, 2 * PATCH)):
        copy.wait()
        kv = project(block, first, slice(256, 768))
        place(first, kv[:, :256], kv[:, 256:])


def prepare(points, ids, gain, w_qkv):
    half = jnp.bfloat16
    vmem = pl.BlockSpec(memory_space=pltpu.VMEM)
    return pl.pallas_call(
        prepare_kernel,
        out_shape=[
            jax.ShapeDtypeStruct((PATCH, 256), half),
            jax.ShapeDtypeStruct((2, WINDOW, 2 * HALF), half),
            jax.ShapeDtypeStruct((2, WINDOW, 2 * HALF), half),
            jax.ShapeDtypeStruct((PATCH, HALF), half),
            jax.ShapeDtypeStruct((WINDOW, 256), half),
            jax.ShapeDtypeStruct((2, 2), jnp.int32),
        ],
        in_specs=[vmem] * 4,
        out_specs=[vmem] * 5 + [pl.BlockSpec(memory_space=pltpu.SMEM)],
        scratch_shapes=[
            pltpu.VMEM((8, HALF), jnp.int32),
            pltpu.VMEM((8, HALF), jnp.int32),
            pltpu.VMEM((8, HALF), jnp.int32),
            pltpu.VMEM((PATCH, 256), half),
            pltpu.VMEM((PATCH, 256), half),
            pltpu.SemaphoreType.DMA((2, 4)),
        ],
        compiler_params=pltpu.CompilerParams(
            collective_id=1, has_side_effects=True, vmem_limit_bytes=32 * 1024 * 1024
        ),
        name="prepare",
    )(points, ids, gain, w_qkv)


SLOTS = 144


def membership(cells):
    local = cells - lax.axis_index("pts") * HALF
    local = jnp.where(local < 0, HALF, local)
    slot = lax.broadcasted_iota(jnp.int32, (SLOTS, HALF), 0)
    parts = [(slot == local[i : i + 1, :]).astype(jnp.float32) for i in range(4)]
    return jnp.concatenate(parts, axis=1)


def forward_kernel(
    spans, q_ref, f_ref, kg_ref, vg_ref, points_ref, w_out_ref, cells_ref,
    att_ref, logs_ref, sums_ref, counts_ref, qf, kept, top, total,
):
    tile, half = pl.program_id(0), pl.program_id(1)
    start, count = spans[tile, 0], spans[tile, 1]
    both = jnp.concatenate([q_ref[...], f_ref[...]], axis=1)
    for h in range(PER_HALF):
        qf[h] = both * head_lanes(h)
        top[h] = jnp.full((TILE, HALF), -3e38, jnp.float32)
        total[h] = jnp.zeros((TILE, HALF), jnp.float32)

    def score_chunk(c, carry):
        kg = kg_ref[half, pl.ds(pl.multiple_of(start + c * CHUNK, 16), CHUNK), :]
        for h in range(PER_HALF):
            scores = against_rows(qf[h], kg)
            kept[c, h] = scores
            top[h] = jnp.maximum(top[h], jnp.maximum(scores[:, :HALF], scores[:, HALF:]))
        return carry

    lax.fori_loop(0, count, score_chunk, 0)
    for h in range(PER_HALF):
        top[h] = jnp.broadcast_to(jnp.max(top[h], axis=1, keepdims=True), (TILE, HALF))

    def weigh_chunk(c, acc):
        values = vg_ref[half, pl.ds(pl.multiple_of(start + c * CHUNK, 16), CHUNK), :HALF]
        for h in range(PER_HALF):
            shift = top[h]
            left = jnp.exp(kept[c, h, :, :HALF] - shift)
            right = jnp.exp(kept[c, h, :, HALF:] - shift)
            total[h] += left + right
            weights = jnp.concatenate([left, right], axis=1).astype(jnp.bfloat16)
            acc = acc + jnp.dot(
                weights, values * head_lanes(h)[:, :HALF], preferred_element_type=jnp.float32
            )
        return acc

    acc = lax.fori_loop(0, count, weigh_chunk, jnp.zeros((TILE, HALF), jnp.float32))
    lane = lax.broadcasted_iota(jnp.int32, (1, HALF), 1)
    factor = jnp.zeros((TILE, HALF), jnp.float32)
    logs = []
    for h in range(PER_HALF):
        row_total = jnp.sum(total[h], axis=1, keepdims=True)
        factor = jnp.where(lane // HEAD_SIZE == h, 1.0 / row_total, factor)
        logs.append(-(top[h][:, :1] + jnp.log(row_total)))
    attended = (acc * factor).astype(jnp.bfloat16)
    rows = pl.ds(pl.multiple_of(tile * TILE, TILE), TILE)
    for g in range(2):

        @pl.when(half == g)
        def _():
            att_ref[rows, g * HALF : (g + 1) * HALF] = attended

    logs_ref[...] = (f_ref[...].astype(jnp.float32) + three_terms(logs)).astype(jnp.bfloat16)

    @pl.when((tile == 1) & (half == 1))
    def _():
        mixed = points_ref[...].astype(jnp.float32) + jnp.dot(
            att_ref[...], w_out_ref[...], preferred_element_type=jnp.float32
        )
        member = membership(cells_ref[...])
        sums_ref[...] = jnp.dot(
            member.astype(jnp.bfloat16), mixed.astype(jnp.bfloat16), preferred_element_type=jnp.float32
        )
        counts_ref[...] = jnp.broadcast_to(jnp.sum(member, axis=1, keepdims=True), (SLOTS, HALF))


def attend(spans, queries, marks_f, keys_g, values_g, points, w_out, cells):
    def whole(*shape):
        return pl.BlockSpec(shape, lambda t, g: (0,) * len(shape))

    return pl.pallas_call(
        forward_kernel,
        grid=(2, 2),
        out_shape=[
            jax.ShapeDtypeStruct((PATCH, 256), jnp.bfloat16),
            jax.ShapeDtypeStruct((PATCH, 256), jnp.bfloat16),
            jax.ShapeDtypeStruct((SLOTS, 256), jnp.float32),
            jax.ShapeDtypeStruct((SLOTS, HALF), jnp.float32),
        ],
        in_specs=[
            pl.BlockSpec(memory_space=pltpu.SMEM),
            pl.BlockSpec((TILE, HALF), lambda t, g: (t, g)),
            pl.BlockSpec((TILE, HALF), lambda t, g: (t, 0)),
            whole(2, WINDOW, 2 * HALF),
            whole(2, WINDOW, 2 * HALF),
            whole(PATCH, 256),
            whole(256, 256),
            whole(4, HALF),
        ],
        out_specs=[
            whole(PATCH, 256),
            pl.BlockSpec((TILE, HALF), lambda t, g: (t, g)),
            whole(SLOTS, 256),
            whole(SLOTS, HALF),
        ],
        scratch_shapes=[
            pltpu.VMEM((PER_HALF, TILE, 2 * HALF), jnp.bfloat16),
            pltpu.VMEM((WINDOW // CHUNK, PER_HALF, TILE, CHUNK), jnp.float32),
            pltpu.VMEM((PER_HALF, TILE, HALF), jnp.float32),
            pltpu.VMEM((PER_HALF, TILE, HALF), jnp.float32),
        ],
        compiler_params=pltpu.CompilerParams(vmem_limit_bytes=48 * 1024 * 1024),
        name="attention",
    )(spans, queries, marks_f, keys_g, values_g, points, w_out, cells)


def split_three(values, which):
    first = values.astype(jnp.bfloat16).astype(jnp.float32)
    second = (values - first).astype(jnp.bfloat16).astype(jnp.float32)
    third = values - first - second
    return jnp.where(which == 0, first, jnp.where(which == 1, second, third))


def pool_kernel(
    scale, sums, counts, cells, att, w_out, w_pool, b_pool, pool_gain, cotangent,
    dmixed_ref, datt_ref, delta_ref, gw_pool, gw_out, gb_pool, g_gain,
    back_pack, ahead_pack, from_after, from_before, sems,
):
    me, before, after = neighbours()
    back_pack[:, :256] = sums[HALF : HALF + 8, :]
    back_pack[:, 256:] = counts[HALF : HALF + 8, :]
    ahead_pack[:, :256] = sums[HALF - 8 : HALF, :]
    ahead_pack[:, 256:384] = counts[HALF - 8 : HALF, :]
    ahead_pack[:, 384:] = cotangent[HALF - 8 :, :]
    greet_neighbours(before, after)
    copies = [
        send(back_pack, from_after, sems, 0, before),
        send(ahead_pack, from_before, sems, 1, after),
    ]
    member = membership(cells[...]).astype(jnp.bfloat16)
    for copy in copies:
        copy.wait()
    row = lax.broadcasted_iota(jnp.int32, (8, 1), 0)
    late, early = from_after[0:1, :], from_before[7:8, :]
    last_sum = sums[HALF - 8 : HALF, :] + jnp.where(row == 7, late[:, :256], 0.0)
    lead_sum = jnp.where(row == 0, sums[HALF : HALF + 8, :] + early[:, :256], 0.0)
    last_count = counts[HALF - 8 : HALF, :] + jnp.where(row == 7, late[:, 256:], 0.0)
    lead_count = jnp.where(row == 0, counts[HALF : HALF + 8, :] + early[:, 256:384], 0.0)
    spare = jnp.zeros((8, 256), jnp.float32)
    all_sums = jnp.concatenate([sums[: HALF - 8, :], last_sum, lead_sum, spare], axis=0)
    all_counts = jnp.concatenate(
        [counts[: HALF - 8, :], last_count, lead_count, spare[:, :HALF]], axis=0
    )[:, :1]
    all_counts = jnp.maximum(all_counts, 1.0)
    lead_cot = jnp.where(row == 0, early[:, 384:], 0.0)
    all_cot = jnp.concatenate([cotangent[...], lead_cot, jnp.zeros((8, 512), jnp.float32)], axis=0)

    pooled_mean = (all_sums / all_counts).astype(jnp.bfloat16)
    pre_norm = jnp.dot(pooled_mean, w_pool[...], preferred_element_type=jnp.float32) + b_pool[...]
    pooled_normed, pooled_inv = layer_stats(pre_norm)
    slope_grad = all_cot * gelu_slope(pooled_normed * pool_gain[...])
    grad_pre = norm_back(slope_grad * pool_gain[...], pooled_normed, pooled_inv)
    grad_pre_b = grad_pre.astype(jnp.bfloat16)
    share = against_rows(grad_pre_b, w_pool[...]) / all_counts
    share_b = share.astype(jnp.bfloat16)
    rest_b = (share - share_b.astype(jnp.float32)).astype(jnp.bfloat16)
    dmixed_main = inner_rows(member, share_b)
    dmixed_ref[...] = dmixed_main + inner_rows(member, rest_b)
    dmixed_b = dmixed_main.astype(jnp.bfloat16)
    datt = against_rows(dmixed_b, w_out[...]).astype(jnp.bfloat16)
    datt_f = datt.astype(jnp.float32)
    datt_ref[...] = (datt_f * 0.25).astype(jnp.bfloat16)
    product = datt_f * att[...].astype(jnp.float32)
    channel = lax.broadcasted_iota(jnp.int32, (256, 256), 0)
    lane = lax.broadcasted_iota(jnp.int32, (256, 256), 1)
    spot = lane % HALF - LOG_LANE
    place = (channel // HALF == lane // HALF) & (spot >= 0) & (spot < 24)
    place = (place & (spot % PER_HALF == channel % HALF // HEAD_SIZE)).astype(jnp.float32)
    place = place.astype(jnp.bfloat16)
    first = product.astype(jnp.bfloat16)
    second = product - first.astype(jnp.float32)
    second_b = second.astype(jnp.bfloat16)
    third_b = (second - second_b.astype(jnp.float32)).astype(jnp.bfloat16)
    deltas = jnp.dot(first, place, preferred_element_type=jnp.float32)
    deltas = deltas + jnp.dot(second_b, place, preferred_element_type=jnp.float32)
    deltas = deltas + jnp.dot(third_b, place, preferred_element_type=jnp.float32)
    which = (lax.broadcasted_iota(jnp.int32, (1, 256), 1) % HALF - LOG_LANE) // PER_HALF
    delta_ref[...] = split_three(deltas * -0.25, which).astype(jnp.bfloat16)
    gw_pool[...] = (inner_rows(pooled_mean[:HALF], grad_pre_b[:HALF]) * scale).astype(jnp.bfloat16)
    gw_out[...] = (inner_rows(att[...], dmixed_b) * scale).astype(jnp.bfloat16)
    gb_pool[...] = jnp.sum(grad_pre[:HALF], axis=0, keepdims=True) * scale
    g_gain[...] = jnp.sum(slope_grad[:HALF] * pooled_normed[:HALF], axis=0, keepdims=True) * scale


def pool(scale, *arrays):
    half = jnp.bfloat16
    vmem = pl.BlockSpec(memory_space=pltpu.VMEM)
    return pl.pallas_call(
        functools.partial(pool_kernel, scale),
        out_shape=[
            jax.ShapeDtypeStruct((PATCH, 256), jnp.float32),
            jax.ShapeDtypeStruct((PATCH, 256), half),
            jax.ShapeDtypeStruct((PATCH, 256), half),
            jax.ShapeDtypeStruct((256, 512), half),
            jax.ShapeDtypeStruct((256, 256), half),
            jax.ShapeDtypeStruct((1, 512), jnp.float32),
            jax.ShapeDtypeStruct((1, 512), jnp.float32),
        ],
        in_specs=[vmem] * 9,
        out_specs=[vmem] * 7,
        scratch_shapes=[
            pltpu.VMEM((8, 384), jnp.float32),
            pltpu.VMEM((8, 896), jnp.float32),
            pltpu.VMEM((8, 384), jnp.float32),
            pltpu.VMEM((8, 896), jnp.float32),
            pltpu.SemaphoreType.DMA((2, 2)),
        ],
        compiler_params=pltpu.CompilerParams(
            collective_id=2, has_side_effects=True, vmem_limit_bytes=32 * 1024 * 1024
        ),
        name="pooling",
    )(*arrays)


def backward_kernel(
    spans, q_ref, logs_ref, do_ref, deltas_ref, kg_ref, vg_ref, dq_ref, dk_ref, dv_ref, qf, df, dqt, dk_sum, dv_sum
):
    tile = pl.program_id(1)
    start, count = spans[tile, 0], spans[tile, 1]
    q_both = jnp.concatenate([q_ref[...], logs_ref[...]], axis=1)
    d_both = jnp.concatenate([do_ref[...], deltas_ref[...]], axis=1)
    for h in range(PER_HALF):
        lanes = head_lanes(h)
        qf[h] = q_both * lanes
        df[h] = d_both * lanes
    dqt[...] = jnp.zeros_like(dqt)

    @pl.when(tile == 0)
    def _():
        dk_sum[...] = jnp.zeros_like(dk_sum)
        dv_sum[...] = jnp.zeros_like(dv_sum)

    def chunk(c, carry):
        rows = pl.ds(pl.multiple_of(start + c * CHUNK, 16), CHUNK)
        kg = kg_ref[rows, :]
        vg = vg_ref[rows, :]
        keys_t = kg[:, :HALF].astype(jnp.float32).T.astype(jnp.bfloat16)
        dk = jnp.zeros((CHUNK, HALF), jnp.float32)
        dv = jnp.zeros((CHUNK, HALF), jnp.float32)
        for h in range(PER_HALF):
            weights = jnp.exp(against_rows(kg, qf[h]))
            dscores = (weights * against_rows(vg, df[h])).astype(jnp.bfloat16)
            dk = dk + jnp.dot(dscores, qf[h, :, :HALF], preferred_element_type=jnp.float32)
            dv = dv + jnp.dot(
                weights.astype(jnp.bfloat16), df[h, :, :HALF], preferred_element_type=jnp.float32
            )
            own = slice(h * HEAD_SIZE, (h + 1) * HEAD_SIZE)
            dqt[own, :] += jnp.dot(keys_t[own], dscores, preferred_element_type=jnp.float32)
        dk_sum[rows, :] += dk * 4.0
        dv_sum[rows, :] += dv * 4.0
        return carry

    lax.fori_loop(0, count, chunk, 0)
    dq_ref[...] = dqt[...].T.astype(jnp.bfloat16)

    @pl.when(tile == 1)
    def _():
        dk_ref[...] = dk_sum[...].astype(jnp.bfloat16)
        dv_ref[...] = dv_sum[...].astype(jnp.bfloat16)


def attend_back(spans, queries, logs, douts, deltas, keys_g, values_g):
    tall = pl.BlockSpec((None, WINDOW, 2 * HALF), lambda g, t: (g, 0, 0))
    mine = pl.BlockSpec((TILE, HALF), lambda g, t: (t, g))
    sums = pl.BlockSpec((WINDOW, HALF), lambda g, t: (0, g))
    return pl.pallas_call(
        backward_kernel,
        grid=(2, 2),
        out_shape=[
            jax.ShapeDtypeStruct((512, 256), jnp.bfloat16),
            jax.ShapeDtypeStruct((WINDOW, 256), jnp.bfloat16),
            jax.ShapeDtypeStruct((WINDOW, 256), jnp.bfloat16),
        ],
        in_specs=[pl.BlockSpec(memory_space=pltpu.SMEM), mine, mine, mine, mine, tall, tall],
        out_specs=[mine, sums, sums],
        scratch_shapes=[
            pltpu.VMEM((PER_HALF, TILE, 2 * HALF), jnp.bfloat16),
            pltpu.VMEM((PER_HALF, TILE, 2 * HALF), jnp.bfloat16),
            pltpu.VMEM((HALF, TILE), jnp.float32),
            pltpu.VMEM((WINDOW, HALF), jnp.float32),
            pltpu.VMEM((WINDOW, HALF), jnp.float32),
        ],
        compiler_params=pltpu.CompilerParams(vmem_limit_bytes=48 * 1024 * 1024),
        name="attention_back",
    )(spans, queries, logs, douts, deltas, keys_g, values_g)


UNIT = 128
EXTRA = 16
CORE_ROWS = 12 * UNIT
X_ROWS = CORE_ROWS // 4
Y_ROWS = X_ROWS // 8


def axes():
    me = lax.axis_index("pts")
    core, z, y, x = me % 2, (me // 2) % 8, (me // 16) % 8, me // 128
    return (
        (core, 2, lambda r: x * 128 + y * 16 + z * 2 + r),
        (x, 4, lambda r: r * 128 + y * 16 + z * 2 + core),
        (y, 8, lambda r: x * 128 + r * 16 + z * 2 + core),
        (z, 8, lambda r: x * 128 + y * 16 + r * 2 + core),
    )


def swap(axis, source, landing, sems, first):
    rank, size, device = axis
    copies = []
    for k in range(1, size):
        peer = (rank + k) % size
        copies.append(send(source(peer), landing(rank), sems, first + k - 1, device(peer)))
    return copies


def wait_all(copies):
    for copy in copies:
        copy.wait()


def slot_sum(ref, start, size):
    total = ref[0, start : start + size, :].astype(jnp.float32)
    for r in range(1, ref.shape[0]):
        total = total + ref[r, start : start + size, :].astype(jnp.float32)
    return total


def finish_kernel(
    scale, hidden, dq, dk, dv, dmixed, points, gain, w_qkv, gw_out, gw_pool, gb_pool, g_gain,
    grad_points, reduced, extras,
    low_k, low_v, high_k, high_v, send_c, recv_c, send_x, recv_x, send_y, recv_y, recv_z,
    gather_y, gather_x, gather_c, sems,
):
    me, before, after = neighbours()
    on_core, on_x, on_y, on_z = axes()
    barrier = pltpu.get_barrier_semaphore()
    greeted = [before, after]
    for rank, size, device in (on_core, on_x, on_y, on_z):
        greeted += [device((rank + k) % size) for k in range(1, size)]
    for device in greeted:
        pl.semaphore_signal(barrier, inc=1, device_id=(device,), device_id_type=MESH)

    def fill(block, first_unit):
        for column in range(block.shape[1] // UNIT):
            unit = first_unit + 2 * column
            start = unit % 12 * UNIT
            send_c[unit // 12, start : start + 2 * UNIT, :] = block[:, column * UNIT : (column + 1) * UNIT]

    fill(gw_out[...], 12)
    fill(gw_pool[...], 16)
    pieces = [gb_pool[:, i * UNIT : (i + 1) * UNIT] for i in range(4)]
    pieces += [g_gain[:, i * UNIT : (i + 1) * UNIT] for i in range(4)]
    pieces += [jnp.zeros((EXTRA - 8, UNIT), jnp.float32)]
    packed = jnp.concatenate(pieces, axis=0).astype(jnp.bfloat16)
    for r in range(2):
        send_c[r, CORE_ROWS:, :] = packed
    pl.semaphore_wait(barrier, len(greeted))
    rims = [
        send(dk.at[pl.ds(0, PATCH)], high_k, sems, 40, before),
        send(dv.at[pl.ds(0, PATCH)], high_v, sems, 41, before),
        send(dk.at[pl.ds(2 * PATCH, PATCH)], low_k, sems, 42, after),
        send(dv.at[pl.ds(2 * PATCH, PATCH)], low_v, sems, 43, after),
    ]
    own = slice(PATCH, 2 * PATCH)
    fill((inner_rows(hidden[own, :], dq[...]) * scale).astype(jnp.bfloat16), 0)
    fill((inner_rows(hidden[...], dk[...]) * scale).astype(jnp.bfloat16), 4)
    fill((inner_rows(hidden[...], dv[...]) * scale).astype(jnp.bfloat16), 8)

    copies = swap(on_core, lambda r: send_c.at[r], lambda r: recv_c, sems, 0)
    dhidden = against_rows(dq[...], w_qkv[:, :256])
    wait_all(copies)
    kept = send_c.at[on_core[0]]
    extra = (
        kept[CORE_ROWS:, :].astype(jnp.float32) + recv_c[CORE_ROWS:, :].astype(jnp.float32)
    ).astype(jnp.bfloat16)
    for r in range(4):
        rows = slice(r * X_ROWS, (r + 1) * X_ROWS)
        total = kept[rows, :].astype(jnp.float32) + recv_c[rows, :].astype(jnp.float32)
        send_x[r, :X_ROWS, :] = total.astype(jnp.bfloat16)
        send_x[r, X_ROWS:, :] = extra

    copies = swap(on_x, lambda r: send_x.at[r], lambda r: recv_x.at[r], sems, 1)
    recv_x[on_x[0]] = send_x[on_x[0]]
    wait_all(rims)
    for columns, mine, low, high in (
        (slice(256, 512), dk, low_k, high_k), (slice(512, 768), dv, low_v, high_v)
    ):
        total = mine[own, :].astype(jnp.float32) + low[...].astype(jnp.float32)
        total = (total + high[...].astype(jnp.float32)).astype(jnp.bfloat16)
        dhidden = dhidden + against_rows(total, w_qkv[:, columns])
    normed, inv_std = layer_stats(points[...].astype(jnp.float32))
    grad_points[...] = dmixed[...] + norm_back(dhidden * gain[...], normed, inv_std)
    wait_all(copies)
    extra = slot_sum(recv_x, X_ROWS, EXTRA).astype(jnp.bfloat16)
    for r in range(8):
        send_y[r, :Y_ROWS, :] = slot_sum(recv_x, r * Y_ROWS, Y_ROWS).astype(jnp.bfloat16)
        send_y[r, Y_ROWS:, :] = extra

    copies = swap(on_y, lambda r: send_y.at[r], lambda r: recv_y.at[r], sems, 4)
    recv_y[on_y[0]] = send_y[on_y[0]]
    wait_all(copies)
    recv_z[on_z[0]] = slot_sum(recv_y, 0, Y_ROWS + EXTRA).astype(jnp.bfloat16)

    wait_all(swap(on_z, lambda r: recv_z.at[on_z[0]], lambda r: recv_z.at[r], sems, 11))
    total = slot_sum(recv_z, 0, Y_ROWS + EXTRA)
    extras[...] = total[Y_ROWS:]
    gather_y[on_y[0]] = total[:Y_ROWS].astype(jnp.bfloat16)
    wait_all(swap(on_y, lambda r: gather_y.at[on_y[0]], lambda r: gather_y.at[r], sems, 18))
    gather_x[on_x[0]] = gather_y[...]
    copies = swap(on_x, lambda r: gather_y, lambda r: gather_x.at[r], sems, 25)
    wait_all(copies)
    gather_c[on_core[0]] = gather_x[...]
    wait_all(swap(on_core, lambda r: gather_x, lambda r: gather_c.at[r], sems, 28))
    for c in range(2):
        for r in range(4):
            for s in range(8):
                start = c * CORE_ROWS + r * X_ROWS + s * Y_ROWS
                reduced[start : start + Y_ROWS, :] = gather_c[c, r, s]


def finish(scale, *arrays):
    half = jnp.bfloat16
    vmem = pl.BlockSpec(memory_space=pltpu.VMEM)
    return pl.pallas_call(
        functools.partial(finish_kernel, scale),
        out_shape=[
            jax.ShapeDtypeStruct((PATCH, 256), jnp.float32),
            jax.ShapeDtypeStruct((2 * CORE_ROWS, UNIT), half),
            jax.ShapeDtypeStruct((EXTRA, UNIT), jnp.float32),
        ],
        in_specs=[vmem] * 12,
        out_specs=[vmem] * 3,
        scratch_shapes=[pltpu.VMEM((PATCH, 256), half)] * 4
        + [
            pltpu.VMEM((2, CORE_ROWS + EXTRA, UNIT), half),
            pltpu.VMEM((CORE_ROWS + EXTRA, UNIT), half),
            pltpu.VMEM((4, X_ROWS + EXTRA, UNIT), half),
            pltpu.VMEM((4, X_ROWS + EXTRA, UNIT), half),
            pltpu.VMEM((8, Y_ROWS + EXTRA, UNIT), half),
            pltpu.VMEM((8, Y_ROWS + EXTRA, UNIT), half),
            pltpu.VMEM((8, Y_ROWS + EXTRA, UNIT), half),
            pltpu.VMEM((8, Y_ROWS, UNIT), half),
            pltpu.VMEM((4, 8, Y_ROWS, UNIT), half),
            pltpu.VMEM((2, 4, 8, Y_ROWS, UNIT), half),
            pltpu.SemaphoreType.DMA((2, 44)),
        ],
        compiler_params=pltpu.CompilerParams(
            collective_id=3, has_side_effects=True, vmem_limit_bytes=40 * 1024 * 1024
        ),
        name="finish",
    )(*arrays)


def unpack_kernel(reduced, extras, gain, w_qkv, gq, go, gn, gp, gb, gg):
    weighted = jnp.zeros((256, UNIT), jnp.float32)
    for column in range(12):
        block = reduced[column * 256 : (column + 1) * 256, :].astype(jnp.float32)
        lanes = slice(column % 12 * UNIT, (column % 12 + 1) * UNIT)
        if column < 6:
            gq[:, lanes] = block
            weighted = weighted + block * w_qkv[:, lanes].astype(jnp.float32)
        elif column < 8:
            go[:, (column - 6) * UNIT : (column - 5) * UNIT] = block
        else:
            gp[:, (column - 8) * UNIT : (column - 7) * UNIT] = block
    gn[...] = jnp.sum(weighted.T, axis=0, keepdims=True) / gain[...]
    for i in range(4):
        gb[:, i * UNIT : (i + 1) * UNIT] = extras[i : i + 1, :]
        gg[:, i * UNIT : (i + 1) * UNIT] = extras[4 + i : 5 + i, :]


def unpack(reduced, extras, gain, w_qkv):
    vmem = pl.BlockSpec(memory_space=pltpu.VMEM)
    shapes = ((256, 768), (256, 256), (1, 256), (256, 512), (1, 512), (1, 512))
    return pl.pallas_call(
        unpack_kernel,
        out_shape=[jax.ShapeDtypeStruct(shape, jnp.float32) for shape in shapes],
        in_specs=[vmem] * 4,
        out_specs=[vmem] * 6,
        name="unpack",
    )(reduced, extras, gain, w_qkv)


def body(
    points, patch_ids, cell_ids, norm_gain, w_qkv, w_out, w_pool, b_pool, pool_gain, cotangent
):
    scale = 1.0 / math.sqrt(points.shape[0] * lax.axis_size("pts"))
    gain = norm_gain[None]
    cells = cell_ids.reshape(4, HALF)
    queries, keys_g, values_g, marks_f, hidden, spans = prepare(
        points, patch_ids.reshape(4, HALF), gain, w_qkv
    )
    attended, logs, sums, counts = attend(
        spans, queries, marks_f, keys_g, values_g, points, w_out, cells
    )
    dmixed, datt, deltas, gw_pool, gw_out, gb_pool, g_gain = pool(
        scale, sums, counts, cells, attended, w_out, w_pool, b_pool[None], pool_gain[None], cotangent
    )
    dq, dk, dv = attend_back(spans, queries, logs, datt, deltas, keys_g, values_g)
    grad_points, reduced, extras = finish(
        scale, hidden, dq, dk, dv, dmixed, points, gain, w_qkv, gw_out, gw_pool, gb_pool, g_gain
    )
    gq, go, gn, gp, gb, gg = unpack(reduced, extras, gain, w_qkv)
    return (grad_points, gq, go, gn[0], gp, gb[0], gg[0])


def solution(mesh):
    in_specs = (P("pts", None), P("pts"), P("pts"), P(), P(), P(), P(), P(), P(), P("pts", None))
    out_specs = (P("pts", None), P(), P(), P(), P(), P(), P())
    return jax.shard_map(body, mesh=mesh, in_specs=in_specs, out_specs=out_specs, check_vma=False)
```

```python
import functools
import math

import jax
import jax.numpy as jnp
from jax import lax
from jax.experimental import pallas as pl
from jax.experimental.pallas import tpu as pltpu
from jax.sharding import PartitionSpec as P

PATCH = 512
MESH = pl.DeviceIdType.MESH


EPS = 1e-05
ROOT_HALF = 0.7071067811865476
ROOT_TWO_PI = 2.5066282746310002


def layer_stats(values):
    centered = values - jnp.mean(values, axis=-1, keepdims=True)
    inv_std = lax.rsqrt(jnp.mean(centered * centered, axis=-1, keepdims=True) + EPS)
    return (centered * inv_std, inv_std)


def norm_back(grad_normed, normed, inv_std):
    first_mean = jnp.mean(grad_normed, axis=-1, keepdims=True)
    second_mean = jnp.mean(grad_normed * normed, axis=-1, keepdims=True)
    return inv_std * (grad_normed - first_mean - normed * second_mean)


def gelu_slope(scaled):
    normal_cdf = 0.5 * (1.0 + lax.erf(scaled * ROOT_HALF))
    return normal_cdf + scaled * jnp.exp(-0.5 * scaled * scaled) / ROOT_TWO_PI


def inner_rows(left, right):
    return lax.dot_general(
        left, right, (((0,), (0,)), ((), ())), preferred_element_type=jnp.float32
    )


def against_rows(left, right):
    return lax.dot_general(
        left, right, (((1,), (1,)), ((), ())), preferred_element_type=jnp.float32
    )


HALF = 128
PER_HALF = 8
HEAD_SIZE = 16
TILE = 256
SPANS = (528, 784, 1040, 1296)
WINDOW = 3 * PATCH
FAR = float(2**30)
DIGIT = 32
LOG_LANE = 64


def head_mask(h, axis):
    shape = (1, 2 * HALF) if axis else (2 * HALF, 1)
    place = lax.broadcasted_iota(jnp.int32, shape, axis)
    own = (place >= h * HEAD_SIZE) & (place < (h + 1) * HEAD_SIZE)
    marks = (place >= HALF) & (place < HALF + LOG_LANE)
    terms = (place >= HALF + LOG_LANE) & (place < HALF + LOG_LANE + 24) & (place % PER_HALF == h)
    return (own | marks | terms).astype(jnp.float32).astype(jnp.bfloat16)


def by_span(size, run):
    for i, span in enumerate(SPANS):

        @pl.when(size == i)
        def _():
            run(span)


def split_three(values, which):
    first = values.astype(jnp.bfloat16).astype(jnp.float32)
    second = (values - first).astype(jnp.bfloat16).astype(jnp.float32)
    third = values - first - second
    return jnp.where(which == 0, first, jnp.where(which == 1, second, third))


def neighbours():
    me = lax.axis_index("pts")
    count = lax.axis_size("pts")
    return me, (me + count - 1) % count, (me + 1) % count


def greet_neighbours(before, after):
    barrier = pltpu.get_barrier_semaphore()
    for device in (before, after):
        pl.semaphore_signal(barrier, inc=1, device_id=(device,), device_id_type=MESH)
    pl.semaphore_wait(barrier, 2)


def send(source, landing, sems, index, device):
    copy = pltpu.make_async_remote_copy(
        src_ref=source,
        dst_ref=landing,
        send_sem=sems.at[0, index],
        recv_sem=sems.at[1, index],
        device_id=(device,),
        device_id_type=MESH,
    )
    copy.start()
    return copy


def digit_columns(marks):
    row = lax.broadcasted_iota(jnp.int32, (HALF, HALF), 0)
    high, low = marks // DIGIT, marks % DIGIT
    hit = ((row < DIGIT) & (row == high)) | ((row >= DIGIT) & (row < LOG_LANE) & (row - DIGIT == low))
    return hit.astype(jnp.float32)


def prepare_kernel(
    points_hbm, ids_hbm, gain_hbm, w_hbm, q_ref, qt_ref, kg_ref, vg_ref, f_ref, hidden_ref, spans_ref,
    points, ids, gain, w_qkv, marks, marks_low, marks_high, rows_low, rows_high, sems, local_sems,
):
    me, before, after = neighbours()
    local = []
    for i, (source, target) in enumerate(
        ((ids_hbm, ids), (points_hbm, points), (w_hbm, w_qkv), (gain_hbm, gain))
    ):
        local.append(pltpu.make_async_copy(source, target, local_sems.at[i]))
        local[-1].start()
    marks[...] = jnp.zeros_like(marks)
    greet_neighbours(before, after)
    local[0].wait()
    marks[:4, :] = ids[...] + 1
    local[1].wait()
    copies = [
        send(points, rows_high, sems, 0, before),
        send(points, rows_low, sems, 1, after),
        send(marks, marks_high, sems, 2, before),
        send(marks, marks_low, sems, 3, after),
    ]
    local[2].wait()
    local[3].wait()

    def project(block, first, columns):
        normed, _ = layer_stats(block[...].astype(jnp.float32))
        hidden = (normed * gain[...]).astype(jnp.bfloat16)
        hidden_ref[first : first + PATCH, :] = hidden
        return jnp.dot(hidden, w_qkv[:, columns], preferred_element_type=jnp.float32)

    def place(first, keys, values):
        for g in range(2):
            lanes = slice(g * HALF, (g + 1) * HALF)
            kg_ref[g, first : first + PATCH, :HALF] = keys[:, lanes].astype(jnp.bfloat16)
            vg_ref[g, first : first + PATCH, :HALF] = values[:, lanes].astype(jnp.bfloat16)

    def place_marks(block, first, own):
        lane = lax.broadcasted_iota(jnp.int32, (HALF, HALF), 1)
        row = lax.broadcasted_iota(jnp.int32, (HALF, HALF), 0)
        terms = (lane >= LOG_LANE) & (lane < LOG_LANE + 24)
        for i in range(4):
            rows = slice(first + i * HALF, first + (i + 1) * HALF)
            digits = digit_columns(block[i : i + 1, :])
            both = jnp.where(terms, 1.0, digits.T).astype(jnp.bfloat16)
            for g in range(2):
                kg_ref[g, rows, HALF:] = both
                vg_ref[g, rows, HALF:] = both
            if own:
                away = jnp.where(row < LOG_LANE, (1.0 - digits) * -FAR, 0.0)
                f_ref[:, i * HALF : (i + 1) * HALF] = away.astype(jnp.bfloat16)

    qkv = project(points, PATCH, slice(None))
    queries = qkv[:, :256].astype(jnp.bfloat16).astype(jnp.float32) * 0.25
    q_ref[...] = queries.astype(jnp.bfloat16)
    qt_ref[...] = queries.T.astype(jnp.bfloat16)
    place(PATCH, qkv[:, 256:512], qkv[:, 512:])
    own = marks[...]
    place_marks(own, PATCH, True)
    for copy in copies[2:]:
        copy.wait()
    low = jnp.where(me == 0, 0, marks_low[...])
    high = jnp.where(me == lax.axis_size("pts") - 1, 0, marks_high[...])
    place_marks(low, 0, False)
    place_marks(high, 2 * PATCH, False)
    own_f, low_f, high_f = (block[:4].astype(jnp.float32) for block in (own, low, high))
    for t in range(2):
        first = jnp.min(own_f[2 * t : 2 * t + 2])
        last = jnp.max(own_f[2 * t : 2 * t + 2])
        lower = jnp.sum((low_f < first).astype(jnp.float32) + (own_f < first).astype(jnp.float32))
        upper = jnp.sum(
            ((high_f > 0) & (high_f <= last)).astype(jnp.float32) + (own_f <= last).astype(jnp.float32)
        )
        lower = lower.astype(jnp.int32) // 16 * 16
        need = PATCH + upper.astype(jnp.int32) - lower
        size, span = jnp.int32(0), jnp.int32(SPANS[0])
        for s in range(len(SPANS) - 1):
            size = jnp.where(need > SPANS[s], s + 1, size)
            span = jnp.where(need > SPANS[s], SPANS[s + 1], span)
        spans_ref[t, 0] = jnp.minimum(lower, WINDOW - span)
        spans_ref[t, 1] = size
    for copy, block, first in ((copies[1], rows_low, 0), (copies[0], rows_high, 2 * PATCH)):
        copy.wait()
        kv = project(block, first, slice(256, 768))
        place(first, kv[:, :256], kv[:, 256:])


def prepare(points, ids, gain, w_qkv):
    half = jnp.bfloat16
    vmem = pl.BlockSpec(memory_space=pltpu.VMEM)
    return pl.pallas_call(
        prepare_kernel,
        out_shape=[
            jax.ShapeDtypeStruct((PATCH, 256), half),
            jax.ShapeDtypeStruct((256, PATCH), half),
            jax.ShapeDtypeStruct((2, WINDOW, 2 * HALF), half),
            jax.ShapeDtypeStruct((2, WINDOW, 2 * HALF), half),
            jax.ShapeDtypeStruct((HALF, PATCH), half),
            jax.ShapeDtypeStruct((WINDOW, 256), half),
            jax.ShapeDtypeStruct((2, 2), jnp.int32),
        ],
        in_specs=[pl.BlockSpec(memory_space=pl.ANY)] * 4,
        out_specs=[vmem] * 6 + [pl.BlockSpec(memory_space=pltpu.SMEM)],
        scratch_shapes=[
            pltpu.VMEM((PATCH, 256), half),
            pltpu.VMEM((4, HALF), jnp.int32),
            pltpu.VMEM((1, 256), jnp.float32),
            pltpu.VMEM((256, 768), half),
            pltpu.VMEM((8, HALF), jnp.int32),
            pltpu.VMEM((8, HALF), jnp.int32),
            pltpu.VMEM((8, HALF), jnp.int32),
            pltpu.VMEM((PATCH, 256), half),
            pltpu.VMEM((PATCH, 256), half),
            pltpu.SemaphoreType.DMA((2, 4)),
            pltpu.SemaphoreType.DMA((4,)),
        ],
        compiler_params=pltpu.CompilerParams(
            collective_id=1, has_side_effects=True, vmem_limit_bytes=32 * 1024 * 1024
        ),
        name="prepare",
    )(points, ids, gain, w_qkv)


SLOTS = 144


def membership(cells):
    local = cells - lax.axis_index("pts") * HALF
    local = jnp.where(local < 0, HALF, local)
    slot = lax.broadcasted_iota(jnp.int32, (SLOTS, HALF), 0)
    parts = [(slot == local[i : i + 1, :]).astype(jnp.float32) for i in range(4)]
    return jnp.concatenate(parts, axis=1)


def forward_kernel(
    spans, qt_ref, f_ref, kg_ref, vg_ref, points_hbm, w_out_hbm, cells_hbm,
    att_ref, logs_ref, sums_ref, counts_ref, qt, vt, att_t, logs_t, points, w_out, cells, sems,
):
    tile, half = pl.program_id(0), pl.program_id(1)
    start, size = spans[tile, 0], spans[tile, 1]
    late = [
        pltpu.make_async_copy(source, target, sems.at[i])
        for i, (source, target) in enumerate(
            ((points_hbm, points), (w_out_hbm, w_out), (cells_hbm, cells))
        )
    ]

    @pl.when((tile == 0) & (half == 0))
    def _():
        for copy in late:
            copy.start()

    both = jnp.concatenate([qt_ref[...], f_ref[...]], axis=0)
    for h in range(PER_HALF):
        qt[h] = both * head_mask(h, 0)

    def run(span):
        rows = pl.ds(pl.multiple_of(start, 16), span)
        vt[:, :span] = vg_ref[half, rows, :HALF].astype(jnp.float32).T.astype(jnp.bfloat16)
        for h in range(PER_HALF):
            scores = jnp.dot(kg_ref[half, rows, :], qt[h], preferred_element_type=jnp.float32)
            top = jnp.max(scores, axis=0, keepdims=True)
            weights = jnp.exp(scores - top)
            total = jnp.sum(weights, axis=0, keepdims=True)
            own = slice(h * HEAD_SIZE, (h + 1) * HEAD_SIZE)
            mixed = jnp.dot(
                vt[own, :span], weights.astype(jnp.bfloat16), preferred_element_type=jnp.float32
            )
            att_t[own, :] = mixed / total
            logs_t[h : h + 1, :] = -(top + jnp.log(total))

    by_span(size, run)
    rows = pl.ds(pl.multiple_of(tile * TILE, TILE), TILE)
    attended = att_t[...].T.astype(jnp.bfloat16)
    for g in range(2):

        @pl.when(half == g)
        def _():
            att_ref[rows, g * HALF : (g + 1) * HALF] = attended

    logs = logs_t[...]
    terms = [split_three(logs, i) for i in range(3)]
    logs_ref[:LOG_LANE, :] = f_ref[:LOG_LANE, :]
    spare = jnp.zeros((HALF - LOG_LANE - 24, TILE), jnp.float32)
    logs_ref[LOG_LANE:, :] = jnp.concatenate(terms + [spare], axis=0).astype(jnp.bfloat16)

    @pl.when((tile == 1) & (half == 1))
    def _():
        for copy in late:
            copy.wait()
        mixed = points[...].astype(jnp.float32) + jnp.dot(
            att_ref[...], w_out[...], preferred_element_type=jnp.float32
        )
        member = membership(cells[...])
        sums_ref[...] = jnp.dot(
            member.astype(jnp.bfloat16), mixed.astype(jnp.bfloat16), preferred_element_type=jnp.float32
        )
        counts_ref[...] = jnp.broadcast_to(jnp.sum(member, axis=1, keepdims=True), (SLOTS, HALF))


def attend(spans, queries_t, marks_f, keys_g, values_g, points, w_out, cells):
    def whole(*shape):
        return pl.BlockSpec(shape, lambda t, g: (0,) * len(shape))

    outside = pl.BlockSpec(memory_space=pl.ANY)
    return pl.pallas_call(
        forward_kernel,
        grid=(2, 2),
        out_shape=[
            jax.ShapeDtypeStruct((PATCH, 256), jnp.bfloat16),
            jax.ShapeDtypeStruct((256, PATCH), jnp.bfloat16),
            jax.ShapeDtypeStruct((SLOTS, 256), jnp.float32),
            jax.ShapeDtypeStruct((SLOTS, HALF), jnp.float32),
        ],
        in_specs=[
            pl.BlockSpec(memory_space=pltpu.SMEM),
            pl.BlockSpec((HALF, TILE), lambda t, g: (g, t)),
            pl.BlockSpec((HALF, TILE), lambda t, g: (0, t)),
            whole(2, WINDOW, 2 * HALF),
            whole(2, WINDOW, 2 * HALF),
            outside,
            outside,
            outside,
        ],
        out_specs=[
            whole(PATCH, 256),
            pl.BlockSpec((HALF, TILE), lambda t, g: (g, t)),
            whole(SLOTS, 256),
            whole(SLOTS, HALF),
        ],
        scratch_shapes=[
            pltpu.VMEM((PER_HALF, 2 * HALF, TILE), jnp.bfloat16),
            pltpu.VMEM((HALF, SPANS[-1]), jnp.bfloat16),
            pltpu.VMEM((HALF, TILE), jnp.float32),
            pltpu.VMEM((PER_HALF, TILE), jnp.float32),
            pltpu.VMEM((PATCH, 256), jnp.bfloat16),
            pltpu.VMEM((256, 256), jnp.bfloat16),
            pltpu.VMEM((4, HALF), jnp.int32),
            pltpu.SemaphoreType.DMA((3,)),
        ],
        compiler_params=pltpu.CompilerParams(vmem_limit_bytes=40 * 1024 * 1024),
        name="attention",
    )(spans, queries_t, marks_f, keys_g, values_g, points, w_out, cells)


def pool_kernel(
    scale, sums, counts, cells, att, w_out, w_pool, b_pool, pool_gain, cotangent,
    dmixed_ref, datt_ref, datt_t_ref, delta_ref, gw_pool, gw_out, gb_pool, g_gain,
    back_pack, ahead_pack, from_after, from_before, sems,
):
    me, before, after = neighbours()
    back_pack[:, :256] = sums[HALF : HALF + 8, :]
    back_pack[:, 256:] = counts[HALF : HALF + 8, :]
    ahead_pack[:, :256] = sums[HALF - 8 : HALF, :]
    ahead_pack[:, 256:384] = counts[HALF - 8 : HALF, :]
    ahead_pack[:, 384:] = cotangent[HALF - 8 :, :]
    greet_neighbours(before, after)
    copies = [
        send(back_pack, from_after, sems, 0, before),
        send(ahead_pack, from_before, sems, 1, after),
    ]
    member = membership(cells[...]).astype(jnp.bfloat16)
    for copy in copies:
        copy.wait()
    row = lax.broadcasted_iota(jnp.int32, (8, 1), 0)
    late, early = from_after[0:1, :], from_before[7:8, :]
    last_sum = sums[HALF - 8 : HALF, :] + jnp.where(row == 7, late[:, :256], 0.0)
    lead_sum = jnp.where(row == 0, sums[HALF : HALF + 8, :] + early[:, :256], 0.0)
    last_count = counts[HALF - 8 : HALF, :] + jnp.where(row == 7, late[:, 256:], 0.0)
    lead_count = jnp.where(row == 0, counts[HALF : HALF + 8, :] + early[:, 256:384], 0.0)
    spare = jnp.zeros((8, 256), jnp.float32)
    all_sums = jnp.concatenate([sums[: HALF - 8, :], last_sum, lead_sum, spare], axis=0)
    all_counts = jnp.concatenate(
        [counts[: HALF - 8, :], last_count, lead_count, spare[:, :HALF]], axis=0
    )[:, :1]
    all_counts = jnp.maximum(all_counts, 1.0)
    lead_cot = jnp.where(row == 0, early[:, 384:], 0.0)
    all_cot = jnp.concatenate([cotangent[...], lead_cot, jnp.zeros((8, 512), jnp.float32)], axis=0)

    pooled_mean = (all_sums / all_counts).astype(jnp.bfloat16)
    pre_norm = jnp.dot(pooled_mean, w_pool[...], preferred_element_type=jnp.float32) + b_pool[...]
    pooled_normed, pooled_inv = layer_stats(pre_norm)
    slope_grad = all_cot * gelu_slope(pooled_normed * pool_gain[...])
    grad_pre = norm_back(slope_grad * pool_gain[...], pooled_normed, pooled_inv)
    grad_pre_b = grad_pre.astype(jnp.bfloat16)
    share = against_rows(grad_pre_b, w_pool[...]) / all_counts
    share_b = share.astype(jnp.bfloat16)
    rest_b = (share - share_b.astype(jnp.float32)).astype(jnp.bfloat16)
    dmixed_main = inner_rows(member, share_b)
    dmixed_ref[...] = dmixed_main + inner_rows(member, rest_b)
    dmixed_b = dmixed_main.astype(jnp.bfloat16)
    datt = against_rows(dmixed_b, w_out[...]).astype(jnp.bfloat16)
    datt_f = datt.astype(jnp.float32)
    datt_ref[...] = (datt_f * 0.25).astype(jnp.bfloat16)
    product = datt_f * att[...].astype(jnp.float32)
    datt_t = against_rows(w_out[...], dmixed_b).astype(jnp.bfloat16).astype(jnp.float32)
    datt_t_ref[...] = (datt_t * 0.25).astype(jnp.bfloat16)
    slot = lax.broadcasted_iota(jnp.int32, (256, 256), 0)
    channel = lax.broadcasted_iota(jnp.int32, (256, 256), 1)
    spot = slot % HALF - LOG_LANE
    place = (channel // HALF == slot // HALF) & (spot >= 0) & (spot < 24)
    place = (place & (spot % PER_HALF == channel % HALF // HEAD_SIZE)).astype(jnp.float32)
    place = place.astype(jnp.bfloat16)
    first = product.astype(jnp.bfloat16)
    second = product - first.astype(jnp.float32)
    second_b = second.astype(jnp.bfloat16)
    third_b = (second - second_b.astype(jnp.float32)).astype(jnp.bfloat16)
    deltas = against_rows(place, first) + against_rows(place, second_b) + against_rows(place, third_b)
    which = (lax.broadcasted_iota(jnp.int32, (256, 1), 0) % HALF - LOG_LANE) // PER_HALF
    delta_ref[...] = split_three(deltas * -0.25, which).astype(jnp.bfloat16)
    gw_pool[...] = (inner_rows(pooled_mean[:HALF], grad_pre_b[:HALF]) * scale).astype(jnp.bfloat16)
    gw_out[...] = (inner_rows(att[...], dmixed_b) * scale).astype(jnp.bfloat16)
    gb_pool[...] = jnp.sum(grad_pre[:HALF], axis=0, keepdims=True) * scale
    g_gain[...] = jnp.sum(slope_grad[:HALF] * pooled_normed[:HALF], axis=0, keepdims=True) * scale


def pool(scale, *arrays):
    half = jnp.bfloat16
    vmem = pl.BlockSpec(memory_space=pltpu.VMEM)
    return pl.pallas_call(
        functools.partial(pool_kernel, scale),
        out_shape=[
            jax.ShapeDtypeStruct((PATCH, 256), jnp.float32),
            jax.ShapeDtypeStruct((PATCH, 256), half),
            jax.ShapeDtypeStruct((256, PATCH), half),
            jax.ShapeDtypeStruct((256, PATCH), half),
            jax.ShapeDtypeStruct((256, 512), half),
            jax.ShapeDtypeStruct((256, 256), half),
            jax.ShapeDtypeStruct((1, 512), jnp.float32),
            jax.ShapeDtypeStruct((1, 512), jnp.float32),
        ],
        in_specs=[vmem] * 9,
        out_specs=[vmem] * 8,
        scratch_shapes=[
            pltpu.VMEM((8, 384), jnp.float32),
            pltpu.VMEM((8, 896), jnp.float32),
            pltpu.VMEM((8, 384), jnp.float32),
            pltpu.VMEM((8, 896), jnp.float32),
            pltpu.SemaphoreType.DMA((2, 2)),
        ],
        compiler_params=pltpu.CompilerParams(
            collective_id=2, has_side_effects=True, vmem_limit_bytes=32 * 1024 * 1024
        ),
        name="pooling",
    )(*arrays)


def backward_kernel(
    spans, q_ref, qt_ref, logs_ref, do_ref, dot_ref, deltas_ref, kg_ref, vg_ref,
    dq_ref, dk_ref, dv_ref, qt, dt, qn, dn, kt, dqt, dk_sum, dv_sum,
):
    tile = pl.program_id(1)
    start, size = spans[tile, 0], spans[tile, 1]
    q_both = jnp.concatenate([qt_ref[...], logs_ref[...]], axis=0)
    d_both = jnp.concatenate([dot_ref[...], deltas_ref[...]], axis=0)
    for h in range(PER_HALF):
        rows = head_mask(h, 0)
        qt[h] = q_both * rows
        dt[h] = d_both * rows
        lanes = head_mask(h, 1)[:, :HALF]
        qn[h] = q_ref[...] * lanes
        dn[h] = do_ref[...] * lanes

    @pl.when(tile == 0)
    def _():
        dk_sum[...] = jnp.zeros_like(dk_sum)
        dv_sum[...] = jnp.zeros_like(dv_sum)

    def run(span):
        rows = pl.ds(pl.multiple_of(start, 16), span)
        kt[:, :span] = kg_ref[rows, :HALF].astype(jnp.float32).T.astype(jnp.bfloat16)
        for h in range(PER_HALF):
            weights = jnp.exp(jnp.dot(kg_ref[rows, :], qt[h], preferred_element_type=jnp.float32))
            dweights = jnp.dot(vg_ref[rows, :], dt[h], preferred_element_type=jnp.float32)
            dscores = (weights * dweights).astype(jnp.bfloat16)
            dk_sum[rows, :] += jnp.dot(dscores, qn[h], preferred_element_type=jnp.float32)
            dv_sum[rows, :] += jnp.dot(
                weights.astype(jnp.bfloat16), dn[h], preferred_element_type=jnp.float32
            )
            own = slice(h * HEAD_SIZE, (h + 1) * HEAD_SIZE)
            dqt[own, :] = jnp.dot(kt[own, :span], dscores, preferred_element_type=jnp.float32)

    by_span(size, run)
    dq_ref[...] = dqt[...].T.astype(jnp.bfloat16)

    @pl.when(tile == 1)
    def _():
        dk_ref[...] = (dk_sum[...] * 4.0).astype(jnp.bfloat16)
        dv_ref[...] = (dv_sum[...] * 4.0).astype(jnp.bfloat16)


def attend_back(spans, queries, queries_t, logs, douts, douts_t, deltas, keys_g, values_g):
    tall = pl.BlockSpec((None, WINDOW, 2 * HALF), lambda g, t: (g, 0, 0))
    mine = pl.BlockSpec((TILE, HALF), lambda g, t: (t, g))
    turned = pl.BlockSpec((HALF, TILE), lambda g, t: (g, t))
    sums = pl.BlockSpec((WINDOW, HALF), lambda g, t: (0, g))
    half = jnp.bfloat16
    return pl.pallas_call(
        backward_kernel,
        grid=(2, 2),
        out_shape=[
            jax.ShapeDtypeStruct((PATCH, 256), half),
            jax.ShapeDtypeStruct((WINDOW, 256), half),
            jax.ShapeDtypeStruct((WINDOW, 256), half),
        ],
        in_specs=[pl.BlockSpec(memory_space=pltpu.SMEM)]
        + [mine, turned, turned, mine, turned, turned, tall, tall],
        out_specs=[mine, sums, sums],
        scratch_shapes=[
            pltpu.VMEM((PER_HALF, 2 * HALF, TILE), half),
            pltpu.VMEM((PER_HALF, 2 * HALF, TILE), half),
            pltpu.VMEM((PER_HALF, TILE, HALF), half),
            pltpu.VMEM((PER_HALF, TILE, HALF), half),
            pltpu.VMEM((HALF, SPANS[-1]), half),
            pltpu.VMEM((HALF, TILE), jnp.float32),
            pltpu.VMEM((WINDOW, HALF), jnp.float32),
            pltpu.VMEM((WINDOW, HALF), jnp.float32),
        ],
        compiler_params=pltpu.CompilerParams(vmem_limit_bytes=40 * 1024 * 1024),
        name="attention_back",
    )(spans, queries, queries_t, logs, douts, douts_t, deltas, keys_g, values_g)


UNIT = 128
EXTRA = 16
CORE_ROWS = 12 * UNIT
X_ROWS = CORE_ROWS // 4
Y_ROWS = X_ROWS // 8


def axes():
    me = lax.axis_index("pts")
    core, z, y, x = me % 2, (me // 2) % 8, (me // 16) % 8, me // 128
    return (
        (core, 2, lambda r: x * 128 + y * 16 + z * 2 + r),
        (x, 4, lambda r: r * 128 + y * 16 + z * 2 + core),
        (y, 8, lambda r: x * 128 + r * 16 + z * 2 + core),
        (z, 8, lambda r: x * 128 + y * 16 + r * 2 + core),
    )


def swap(axis, source, landing, sems, first):
    rank, size, device = axis
    copies = []
    for k in range(1, size):
        peer = (rank + k) % size
        copies.append(send(source(peer), landing(rank), sems, first + k - 1, device(peer)))
    return copies


def wait_all(copies):
    for copy in copies:
        copy.wait()


def slot_sum(ref, start, size):
    total = ref[0, start : start + size, :].astype(jnp.float32)
    for r in range(1, ref.shape[0]):
        total = total + ref[r, start : start + size, :].astype(jnp.float32)
    return total


def finish_kernel(
    scale, hidden, dq, dk, dv, dmixed, points, gain, w_qkv, gw_out, gw_pool, gb_pool, g_gain,
    grad_points, reduced, extras,
    low_k, low_v, high_k, high_v, send_c, recv_c, send_x, recv_x, send_y, recv_y, recv_z,
    gather_y, gather_x, gather_c, sems,
):
    me, before, after = neighbours()
    on_core, on_x, on_y, on_z = axes()
    barrier = pltpu.get_barrier_semaphore()
    greeted = [before, after]
    for rank, size, device in (on_core, on_x, on_y, on_z):
        greeted += [device((rank + k) % size) for k in range(1, size)]
    for device in greeted:
        pl.semaphore_signal(barrier, inc=1, device_id=(device,), device_id_type=MESH)

    def fill(block, first_unit):
        for column in range(block.shape[1] // UNIT):
            unit = first_unit + 2 * column
            start = unit % 12 * UNIT
            send_c[unit // 12, start : start + 2 * UNIT, :] = block[:, column * UNIT : (column + 1) * UNIT]

    fill(gw_out[...], 12)
    fill(gw_pool[...], 16)
    pieces = [gb_pool[:, i * UNIT : (i + 1) * UNIT] for i in range(4)]
    pieces += [g_gain[:, i * UNIT : (i + 1) * UNIT] for i in range(4)]
    pieces += [jnp.zeros((EXTRA - 8, UNIT), jnp.float32)]
    packed = jnp.concatenate(pieces, axis=0).astype(jnp.bfloat16)
    for r in range(2):
        send_c[r, CORE_ROWS:, :] = packed
    pl.semaphore_wait(barrier, len(greeted))
    rims = [
        send(dk.at[pl.ds(0, PATCH)], high_k, sems, 40, before),
        send(dv.at[pl.ds(0, PATCH)], high_v, sems, 41, before),
        send(dk.at[pl.ds(2 * PATCH, PATCH)], low_k, sems, 42, after),
        send(dv.at[pl.ds(2 * PATCH, PATCH)], low_v, sems, 43, after),
    ]
    own = slice(PATCH, 2 * PATCH)
    fill((inner_rows(hidden[own, :], dq[...]) * scale).astype(jnp.bfloat16), 0)
    fill((inner_rows(hidden[...], dk[...]) * scale).astype(jnp.bfloat16), 4)
    fill((inner_rows(hidden[...], dv[...]) * scale).astype(jnp.bfloat16), 8)

    copies = swap(on_core, lambda r: send_c.at[r], lambda r: recv_c, sems, 0)
    dhidden = against_rows(dq[...], w_qkv[:, :256])
    wait_all(copies)
    kept = send_c.at[on_core[0]]
    extra = (
        kept[CORE_ROWS:, :].astype(jnp.float32) + recv_c[CORE_ROWS:, :].astype(jnp.float32)
    ).astype(jnp.bfloat16)
    for r in range(4):
        rows = slice(r * X_ROWS, (r + 1) * X_ROWS)
        total = kept[rows, :].astype(jnp.float32) + recv_c[rows, :].astype(jnp.float32)
        send_x[r, :X_ROWS, :] = total.astype(jnp.bfloat16)
        send_x[r, X_ROWS:, :] = extra

    copies = swap(on_x, lambda r: send_x.at[r], lambda r: recv_x.at[r], sems, 1)
    recv_x[on_x[0]] = send_x[on_x[0]]
    wait_all(rims)
    for columns, mine, low, high in (
        (slice(256, 512), dk, low_k, high_k), (slice(512, 768), dv, low_v, high_v)
    ):
        total = mine[own, :].astype(jnp.float32) + low[...].astype(jnp.float32)
        total = (total + high[...].astype(jnp.float32)).astype(jnp.bfloat16)
        dhidden = dhidden + against_rows(total, w_qkv[:, columns])
    normed, inv_std = layer_stats(points[...].astype(jnp.float32))
    grad_points[...] = dmixed[...] + norm_back(dhidden * gain[...], normed, inv_std)
    wait_all(copies)
    extra = slot_sum(recv_x, X_ROWS, EXTRA).astype(jnp.bfloat16)
    for r in range(8):
        send_y[r, :Y_ROWS, :] = slot_sum(recv_x, r * Y_ROWS, Y_ROWS).astype(jnp.bfloat16)
        send_y[r, Y_ROWS:, :] = extra

    copies = swap(on_y, lambda r: send_y.at[r], lambda r: recv_y.at[r], sems, 4)
    recv_y[on_y[0]] = send_y[on_y[0]]
    wait_all(copies)
    recv_z[on_z[0]] = slot_sum(recv_y, 0, Y_ROWS + EXTRA).astype(jnp.bfloat16)

    wait_all(swap(on_z, lambda r: recv_z.at[on_z[0]], lambda r: recv_z.at[r], sems, 11))
    total = slot_sum(recv_z, 0, Y_ROWS + EXTRA)
    extras[...] = total[Y_ROWS:]
    gather_y[on_y[0]] = total[:Y_ROWS].astype(jnp.bfloat16)
    wait_all(swap(on_y, lambda r: gather_y.at[on_y[0]], lambda r: gather_y.at[r], sems, 18))
    gather_x[on_x[0]] = gather_y[...]
    copies = swap(on_x, lambda r: gather_y, lambda r: gather_x.at[r], sems, 25)
    wait_all(copies)
    gather_c[on_core[0]] = gather_x[...]
    wait_all(swap(on_core, lambda r: gather_x, lambda r: gather_c.at[r], sems, 28))
    for c in range(2):
        for r in range(4):
            for s in range(8):
                start = c * CORE_ROWS + r * X_ROWS + s * Y_ROWS
                reduced[start : start + Y_ROWS, :] = gather_c[c, r, s]
    weighted = jnp.zeros((256, UNIT), jnp.float32)
    for column in range(6):
        block = reduced[column * 256 : (column + 1) * 256, :].astype(jnp.float32)
        lanes = slice(column * UNIT, (column + 1) * UNIT)
        weighted = weighted + block * w_qkv[:, lanes].astype(jnp.float32)
    summed_gain = jnp.sum(weighted.T, axis=0, keepdims=True) / gain[...]
    for i in range(2):
        extras[8 + i : 9 + i, :] = summed_gain[:, i * UNIT : (i + 1) * UNIT]


def finish(scale, *arrays):
    half = jnp.bfloat16
    vmem = pl.BlockSpec(memory_space=pltpu.VMEM)
    return pl.pallas_call(
        functools.partial(finish_kernel, scale),
        out_shape=[
            jax.ShapeDtypeStruct((PATCH, 256), jnp.float32),
            jax.ShapeDtypeStruct((2 * CORE_ROWS, UNIT), half),
            jax.ShapeDtypeStruct((EXTRA, UNIT), jnp.float32),
        ],
        in_specs=[vmem] * 12,
        out_specs=[vmem] * 3,
        scratch_shapes=[pltpu.VMEM((PATCH, 256), half)] * 4
        + [
            pltpu.VMEM((2, CORE_ROWS + EXTRA, UNIT), half),
            pltpu.VMEM((CORE_ROWS + EXTRA, UNIT), half),
            pltpu.VMEM((4, X_ROWS + EXTRA, UNIT), half),
            pltpu.VMEM((4, X_ROWS + EXTRA, UNIT), half),
            pltpu.VMEM((8, Y_ROWS + EXTRA, UNIT), half),
            pltpu.VMEM((8, Y_ROWS + EXTRA, UNIT), half),
            pltpu.VMEM((8, Y_ROWS + EXTRA, UNIT), half),
            pltpu.VMEM((8, Y_ROWS, UNIT), half),
            pltpu.VMEM((4, 8, Y_ROWS, UNIT), half),
            pltpu.VMEM((2, 4, 8, Y_ROWS, UNIT), half),
            pltpu.SemaphoreType.DMA((2, 44)),
        ],
        compiler_params=pltpu.CompilerParams(
            collective_id=3, has_side_effects=True, vmem_limit_bytes=40 * 1024 * 1024
        ),
        name="finish",
    )(*arrays)


def unpack_kernel(reduced, extras, rows_in, gq, go, gn, gp, gb, gg, rows_out, sem):
    copy = pltpu.make_async_copy(rows_in, rows_out, sem)
    copy.start()
    for column in range(12):
        block = reduced[column * 256 : (column + 1) * 256, :].astype(jnp.float32)
        if column < 6:
            gq[:, column * UNIT : (column + 1) * UNIT] = block
        elif column < 8:
            go[:, (column - 6) * UNIT : (column - 5) * UNIT] = block
        else:
            gp[:, (column - 8) * UNIT : (column - 7) * UNIT] = block
    for i in range(2):
        gn[:, i * UNIT : (i + 1) * UNIT] = extras[8 + i : 9 + i, :]
    for i in range(4):
        gb[:, i * UNIT : (i + 1) * UNIT] = extras[i : i + 1, :]
        gg[:, i * UNIT : (i + 1) * UNIT] = extras[4 + i : 5 + i, :]
    copy.wait()


def unpack(reduced, extras, rows):
    vmem = pl.BlockSpec(memory_space=pltpu.VMEM)
    outside = pl.BlockSpec(memory_space=pl.ANY)
    shapes = ((256, 768), (256, 256), (1, 256), (256, 512), (1, 512), (1, 512), (PATCH, 256))
    return pl.pallas_call(
        unpack_kernel,
        out_shape=[jax.ShapeDtypeStruct(shape, jnp.float32) for shape in shapes],
        in_specs=[vmem, vmem, outside],
        out_specs=[vmem] * 6 + [outside],
        scratch_shapes=[pltpu.SemaphoreType.DMA],
        name="unpack",
    )(reduced, extras, rows)


def body(
    points, patch_ids, cell_ids, norm_gain, w_qkv, w_out, w_pool, b_pool, pool_gain, cotangent
):
    scale = 1.0 / math.sqrt(points.shape[0] * lax.axis_size("pts"))
    gain = norm_gain[None]
    cells = cell_ids.reshape(4, HALF)
    queries, queries_t, keys_g, values_g, marks_f, hidden, spans = prepare(
        points, patch_ids.reshape(4, HALF), gain, w_qkv
    )
    attended, logs, sums, counts = attend(
        spans, queries_t, marks_f, keys_g, values_g, points, w_out, cells
    )
    dmixed, datt, datt_t, deltas, gw_pool, gw_out, gb_pool, g_gain = pool(
        scale, sums, counts, cells, attended, w_out, w_pool, b_pool[None], pool_gain[None], cotangent
    )
    dq, dk, dv = attend_back(
        spans, queries, queries_t, logs, datt, datt_t, deltas, keys_g, values_g
    )
    grad_points, reduced, extras = finish(
        scale, hidden, dq, dk, dv, dmixed, points, gain, w_qkv, gw_out, gw_pool, gb_pool, g_gain
    )
    gq, go, gn, gp, gb, gg, grad_points = unpack(reduced, extras, grad_points)
    return (grad_points, gq, go, gn[0], gp, gb[0], gg[0])


def solution(mesh):
    in_specs = (P("pts", None), P("pts"), P("pts"), P(), P(), P(), P(), P(), P(), P("pts", None))
    out_specs = (P("pts", None), P(), P(), P(), P(), P(), P())
    return jax.shard_map(body, mesh=mesh, in_specs=in_specs, out_specs=out_specs, check_vma=False)
```

```python
import functools
import math

import jax
import jax.numpy as jnp
from jax import lax
from jax.experimental import pallas as pl
from jax.experimental.pallas import tpu as pltpu
from jax.sharding import PartitionSpec as P

PATCH = 512
MESH = pl.DeviceIdType.MESH


EPS = 1e-05
ROOT_HALF = 0.7071067811865476
ROOT_TWO_PI = 2.5066282746310002


def layer_stats(values):
    centered = values - jnp.mean(values, axis=-1, keepdims=True)
    inv_std = lax.rsqrt(jnp.mean(centered * centered, axis=-1, keepdims=True) + EPS)
    return (centered * inv_std, inv_std)


def norm_back(grad_normed, normed, inv_std):
    first_mean = jnp.mean(grad_normed, axis=-1, keepdims=True)
    second_mean = jnp.mean(grad_normed * normed, axis=-1, keepdims=True)
    return inv_std * (grad_normed - first_mean - normed * second_mean)


def gelu_slope(scaled):
    normal_cdf = 0.5 * (1.0 + lax.erf(scaled * ROOT_HALF))
    return normal_cdf + scaled * jnp.exp(-0.5 * scaled * scaled) / ROOT_TWO_PI


def inner_rows(left, right):
    return lax.dot_general(
        left, right, (((0,), (0,)), ((), ())), preferred_element_type=jnp.float32
    )


def against_rows(left, right):
    return lax.dot_general(
        left, right, (((1,), (1,)), ((), ())), preferred_element_type=jnp.float32
    )


HALF = 128
PER_HALF = 8
HEAD_SIZE = 16
TILE = 128
CHUNK = 528
TALL = 3 * CHUNK
TILES = PATCH // TILE
PAIR = 256 // TILE
WINDOW = 3 * PATCH
FAR = float(2**30)
DIGIT = 32
LOG_LANE = 64


def head_mask(h, axis):
    shape = (1, 2 * HALF) if axis else (2 * HALF, 1)
    place = lax.broadcasted_iota(jnp.int32, shape, axis)
    own = (place >= h * HEAD_SIZE) & (place < (h + 1) * HEAD_SIZE)
    marks = (place >= HALF) & (place < HALF + LOG_LANE)
    terms = (place >= HALF + LOG_LANE) & (place < HALF + LOG_LANE + 24) & (place % PER_HALF == h)
    return (own | marks | terms).astype(jnp.float32).astype(jnp.bfloat16)


def split_three(values, which):
    first = values.astype(jnp.bfloat16).astype(jnp.float32)
    second = (values - first).astype(jnp.bfloat16).astype(jnp.float32)
    third = values - first - second
    return jnp.where(which == 0, first, jnp.where(which == 1, second, third))


def neighbours():
    me = lax.axis_index("pts")
    count = lax.axis_size("pts")
    return me, (me + count - 1) % count, (me + 1) % count


def greet_neighbours(before, after):
    barrier = pltpu.get_barrier_semaphore()
    for device in (before, after):
        pl.semaphore_signal(barrier, inc=1, device_id=(device,), device_id_type=MESH)
    pl.semaphore_wait(barrier, 2)


def send(source, landing, sems, index, device):
    copy = pltpu.make_async_remote_copy(
        src_ref=source,
        dst_ref=landing,
        send_sem=sems.at[0, index],
        recv_sem=sems.at[1, index],
        device_id=(device,),
        device_id_type=MESH,
    )
    copy.start()
    return copy


def digit_columns(marks):
    row = lax.broadcasted_iota(jnp.int32, (HALF, HALF), 0)
    high, low = marks // DIGIT, marks % DIGIT
    hit = ((row < DIGIT) & (row == high)) | ((row >= DIGIT) & (row < LOG_LANE) & (row - DIGIT == low))
    return hit.astype(jnp.float32)


def prepare_kernel(
    points_hbm, ids_hbm, gain_hbm, w_hbm, q_ref, qt_ref, kg_ref, vg_ref, f_ref, hidden_ref, spans_ref,
    points, ids, gain, w_qkv, marks, marks_low, marks_high, rows_low, rows_high, sems, local_sems,
):
    me, before, after = neighbours()
    local = []
    for i, (source, target) in enumerate(
        ((ids_hbm, ids), (points_hbm, points), (w_hbm, w_qkv), (gain_hbm, gain))
    ):
        local.append(pltpu.make_async_copy(source, target, local_sems.at[i]))
        local[-1].start()
    marks[...] = jnp.zeros_like(marks)
    greet_neighbours(before, after)
    local[0].wait()
    marks[:4, :] = ids[...] + 1
    local[1].wait()
    copies = [
        send(points, rows_high, sems, 0, before),
        send(points, rows_low, sems, 1, after),
        send(marks, marks_high, sems, 2, before),
        send(marks, marks_low, sems, 3, after),
    ]
    local[2].wait()
    local[3].wait()

    def project(block, first, columns):
        normed, _ = layer_stats(block[...].astype(jnp.float32))
        hidden = (normed * gain[...]).astype(jnp.bfloat16)
        hidden_ref[first : first + PATCH, :] = hidden
        return jnp.dot(hidden, w_qkv[:, columns], preferred_element_type=jnp.float32)

    def place(first, keys, values):
        for g in range(2):
            lanes = slice(g * HALF, (g + 1) * HALF)
            kg_ref[g, first : first + PATCH, :HALF] = keys[:, lanes].astype(jnp.bfloat16)
            vg_ref[g, first : first + PATCH, :HALF] = values[:, lanes].astype(jnp.bfloat16)

    def place_marks(block, first, own):
        lane = lax.broadcasted_iota(jnp.int32, (HALF, HALF), 1)
        row = lax.broadcasted_iota(jnp.int32, (HALF, HALF), 0)
        terms = (lane >= LOG_LANE) & (lane < LOG_LANE + 24)
        for i in range(4):
            rows = slice(first + i * HALF, first + (i + 1) * HALF)
            digits = digit_columns(block[i : i + 1, :])
            both = jnp.where(terms, 1.0, digits.T).astype(jnp.bfloat16)
            for g in range(2):
                kg_ref[g, rows, HALF:] = both
                vg_ref[g, rows, HALF:] = both
            if own:
                away = jnp.where(row < LOG_LANE, (1.0 - digits) * -FAR, 0.0)
                f_ref[:, i * HALF : (i + 1) * HALF] = away.astype(jnp.bfloat16)

    qkv = project(points, PATCH, slice(None))
    queries = qkv[:, :256].astype(jnp.bfloat16).astype(jnp.float32) * 0.25
    q_ref[...] = queries.astype(jnp.bfloat16)
    qt_ref[...] = queries.T.astype(jnp.bfloat16)
    place(PATCH, qkv[:, 256:512], qkv[:, 512:])
    own = marks[...]
    place_marks(own, PATCH, True)
    lane = lax.broadcasted_iota(jnp.int32, (TALL - WINDOW, 2 * HALF), 1)
    nowhere = ((lane == HALF) | (lane == HALF + DIGIT)).astype(jnp.float32).astype(jnp.bfloat16)
    for g in range(2):
        kg_ref[g, WINDOW:, :] = nowhere
        vg_ref[g, WINDOW:, :] = nowhere
    for copy in copies[2:]:
        copy.wait()
    low = jnp.where(me == 0, 0, marks_low[...])
    high = jnp.where(me == lax.axis_size("pts") - 1, 0, marks_high[...])
    place_marks(low, 0, False)
    place_marks(high, 2 * PATCH, False)
    own_f, low_f, high_f = (block[:4].astype(jnp.float32) for block in (own, low, high))
    for t in range(TILES):
        ours = own_f[t * TILE // HALF : (t + 1) * TILE // HALF]
        first, last = jnp.min(ours), jnp.max(ours)
        lower = jnp.sum((low_f < first).astype(jnp.float32) + (own_f < first).astype(jnp.float32))
        upper = jnp.sum(
            ((high_f > 0) & (high_f <= last)).astype(jnp.float32) + (own_f <= last).astype(jnp.float32)
        )
        lower = lower.astype(jnp.int32) // 16 * 16
        count = (PATCH + upper.astype(jnp.int32) - lower + CHUNK - 1) // CHUNK
        spans_ref[t, 0] = jnp.minimum(lower, TALL - count * CHUNK)
        spans_ref[t, 1] = count
    for copy, block, first in ((copies[1], rows_low, 0), (copies[0], rows_high, 2 * PATCH)):
        copy.wait()
        kv = project(block, first, slice(256, 768))
        place(first, kv[:, :256], kv[:, 256:])


def prepare(points, ids, gain, w_qkv):
    half = jnp.bfloat16
    vmem = pl.BlockSpec(memory_space=pltpu.VMEM)
    return pl.pallas_call(
        prepare_kernel,
        out_shape=[
            jax.ShapeDtypeStruct((PATCH, 256), half),
            jax.ShapeDtypeStruct((256, PATCH), half),
            jax.ShapeDtypeStruct((2, TALL, 2 * HALF), half),
            jax.ShapeDtypeStruct((2, TALL, 2 * HALF), half),
            jax.ShapeDtypeStruct((HALF, PATCH), half),
            jax.ShapeDtypeStruct((WINDOW, 256), half),
            jax.ShapeDtypeStruct((TILES, 2), jnp.int32),
        ],
        in_specs=[pl.BlockSpec(memory_space=pl.ANY)] * 4,
        out_specs=[vmem] * 6 + [pl.BlockSpec(memory_space=pltpu.SMEM)],
        scratch_shapes=[
            pltpu.VMEM((PATCH, 256), half),
            pltpu.VMEM((4, HALF), jnp.int32),
            pltpu.VMEM((1, 256), jnp.float32),
            pltpu.VMEM((256, 768), half),
            pltpu.VMEM((8, HALF), jnp.int32),
            pltpu.VMEM((8, HALF), jnp.int32),
            pltpu.VMEM((8, HALF), jnp.int32),
            pltpu.VMEM((PATCH, 256), half),
            pltpu.VMEM((PATCH, 256), half),
            pltpu.SemaphoreType.DMA((2, 4)),
            pltpu.SemaphoreType.DMA((4,)),
        ],
        compiler_params=pltpu.CompilerParams(
            collective_id=1, has_side_effects=True, vmem_limit_bytes=32 * 1024 * 1024
        ),
        name="prepare",
    )(points, ids, gain, w_qkv)


SLOTS = 144


def membership(cells):
    local = cells - lax.axis_index("pts") * HALF
    local = jnp.where(local < 0, HALF, local)
    slot = lax.broadcasted_iota(jnp.int32, (SLOTS, HALF), 0)
    parts = [(slot == local[i : i + 1, :]).astype(jnp.float32) for i in range(4)]
    return jnp.concatenate(parts, axis=1)


def tall_max(scores):
    part = CHUNK // 6
    folded = scores[:part]
    for i in range(1, 6):
        folded = jnp.maximum(folded, scores[i * part : (i + 1) * part])
    return jnp.max(folded, axis=0, keepdims=True)


def forward_kernel(
    spans, qt_ref, f_ref, kg_ref, vg_ref, points_hbm, w_out_hbm, cells_hbm,
    att_ref, logs_ref, sums_ref, counts_ref, qt, kept, att_t, top_t, total_t, points, w_out, cells, sems,
):
    tile, half = pl.program_id(0), pl.program_id(1)
    start, count = spans[tile, 0], spans[tile, 1]
    late = [
        pltpu.make_async_copy(source, target, sems.at[i])
        for i, (source, target) in enumerate(
            ((points_hbm, points), (w_out_hbm, w_out), (cells_hbm, cells))
        )
    ]

    @pl.when((tile == 0) & (half == 0))
    def _():
        for copy in late:
            copy.start()

    both = jnp.concatenate([qt_ref[...], f_ref[...]], axis=0)
    for h in range(PER_HALF):
        qt[h // PAIR, :, h % PAIR * TILE : (h % PAIR + 1) * TILE] = both * head_mask(h, 0)
    top_t[...] = jnp.full_like(top_t, -3e38)
    total_t[...] = jnp.zeros_like(total_t)
    att_t[...] = jnp.zeros_like(att_t)

    def chunk(c, carry):
        rows = pl.ds(pl.multiple_of(start + c * CHUNK, 16), CHUNK)
        values_t = vg_ref[half, rows, :HALF].astype(jnp.float32).T.astype(jnp.bfloat16)
        ones = jnp.ones((16, CHUNK), jnp.bfloat16)
        tops = []
        for p in range(PER_HALF // PAIR):
            scores = jnp.dot(kg_ref[half, rows, :], qt[p], preferred_element_type=jnp.float32)
            kept[p] = scores
            tops.append(jnp.maximum(top_t[p : p + 1, :], tall_max(scores)))
        for p in range(PER_HALF // PAIR):
            before, top = top_t[p : p + 1, :], tops[p]
            weights = jnp.exp(kept[p] - top).astype(jnp.bfloat16)
            decay = jnp.exp(before - top)
            top_t[p : p + 1, :] = top
            own = slice(p * PAIR * HEAD_SIZE, (p + 1) * PAIR * HEAD_SIZE)
            left = jnp.concatenate([values_t[own], ones], axis=0)
            mixed = jnp.dot(left, weights, preferred_element_type=jnp.float32)
            count_rows = PAIR * HEAD_SIZE
            total_t[p : p + 1, :] = total_t[p : p + 1, :] * decay + mixed[count_rows : count_rows + 1]
            att_t[own, :] = att_t[own, :] * decay + mixed[:count_rows]
        return carry

    lax.fori_loop(0, count, chunk, 0)
    rows = pl.ds(pl.multiple_of(tile * TILE, TILE), TILE)
    logs_p = -(top_t[...] + jnp.log(total_t[...]))
    parts, logs = [], []
    for h in range(PER_HALF):
        p, columns = h // PAIR, slice(h % PAIR * TILE, (h % PAIR + 1) * TILE)
        mine = att_t[h * HEAD_SIZE : (h + 1) * HEAD_SIZE, columns]
        parts.append(mine / total_t[p : p + 1, columns])
        logs.append(logs_p[p : p + 1, columns])
    attended = jnp.concatenate(parts, axis=0).T.astype(jnp.bfloat16)
    for g in range(2):

        @pl.when(half == g)
        def _():
            att_ref[rows, g * HALF : (g + 1) * HALF] = attended

    logs = jnp.concatenate(logs, axis=0)
    terms = [split_three(logs, i) for i in range(3)]
    logs_ref[:LOG_LANE, :] = f_ref[:LOG_LANE, :]
    spare = jnp.zeros((HALF - LOG_LANE - 24, TILE), jnp.float32)
    logs_ref[LOG_LANE:, :] = jnp.concatenate(terms + [spare], axis=0).astype(jnp.bfloat16)

    @pl.when((tile == TILES - 1) & (half == 1))
    def _():
        for copy in late:
            copy.wait()
        mixed = points[...].astype(jnp.float32) + jnp.dot(
            att_ref[...], w_out[...], preferred_element_type=jnp.float32
        )
        member = membership(cells[...])
        sums_ref[...] = jnp.dot(
            member.astype(jnp.bfloat16), mixed.astype(jnp.bfloat16), preferred_element_type=jnp.float32
        )
        counts_ref[...] = jnp.broadcast_to(jnp.sum(member, axis=1, keepdims=True), (SLOTS, HALF))


def attend(spans, queries_t, marks_f, keys_g, values_g, points, w_out, cells):
    def whole(*shape):
        return pl.BlockSpec(shape, lambda t, g: (0,) * len(shape))

    outside = pl.BlockSpec(memory_space=pl.ANY)
    return pl.pallas_call(
        forward_kernel,
        grid=(TILES, 2),
        out_shape=[
            jax.ShapeDtypeStruct((PATCH, 256), jnp.bfloat16),
            jax.ShapeDtypeStruct((256, PATCH), jnp.bfloat16),
            jax.ShapeDtypeStruct((SLOTS, 256), jnp.float32),
            jax.ShapeDtypeStruct((SLOTS, HALF), jnp.float32),
        ],
        in_specs=[
            pl.BlockSpec(memory_space=pltpu.SMEM),
            pl.BlockSpec((HALF, TILE), lambda t, g: (g, t)),
            pl.BlockSpec((HALF, TILE), lambda t, g: (0, t)),
            whole(2, TALL, 2 * HALF),
            whole(2, TALL, 2 * HALF),
            outside,
            outside,
            outside,
        ],
        out_specs=[
            whole(PATCH, 256),
            pl.BlockSpec((HALF, TILE), lambda t, g: (g, t)),
            whole(SLOTS, 256),
            whole(SLOTS, HALF),
        ],
        scratch_shapes=[
            pltpu.VMEM((PER_HALF // PAIR, 2 * HALF, PAIR * TILE), jnp.bfloat16),
            pltpu.VMEM((PER_HALF // PAIR, CHUNK, PAIR * TILE), jnp.float32),
            pltpu.VMEM((HALF, PAIR * TILE), jnp.float32),
            pltpu.VMEM((PER_HALF // PAIR, PAIR * TILE), jnp.float32),
            pltpu.VMEM((PER_HALF // PAIR, PAIR * TILE), jnp.float32),
            pltpu.VMEM((PATCH, 256), jnp.bfloat16),
            pltpu.VMEM((256, 256), jnp.bfloat16),
            pltpu.VMEM((4, HALF), jnp.int32),
            pltpu.SemaphoreType.DMA((3,)),
        ],
        compiler_params=pltpu.CompilerParams(vmem_limit_bytes=40 * 1024 * 1024),
        name="attention",
    )(spans, queries_t, marks_f, keys_g, values_g, points, w_out, cells)


def pool_kernel(
    scale, sums, counts, cells, att, w_out, w_pool, b_pool, pool_gain, cotangent,
    dmixed_ref, datt_ref, datt_t_ref, delta_ref, gw_pool, gw_out, gb_pool, g_gain,
    back_pack, ahead_pack, from_after, from_before, sems,
):
    me, before, after = neighbours()
    back_pack[:, :256] = sums[HALF : HALF + 8, :]
    back_pack[:, 256:] = counts[HALF : HALF + 8, :]
    ahead_pack[:, :256] = sums[HALF - 8 : HALF, :]
    ahead_pack[:, 256:384] = counts[HALF - 8 : HALF, :]
    ahead_pack[:, 384:] = cotangent[HALF - 8 :, :]
    greet_neighbours(before, after)
    copies = [
        send(back_pack, from_after, sems, 0, before),
        send(ahead_pack, from_before, sems, 1, after),
    ]
    member = membership(cells[...]).astype(jnp.bfloat16)
    for copy in copies:
        copy.wait()
    row = lax.broadcasted_iota(jnp.int32, (8, 1), 0)
    late, early = from_after[0:1, :], from_before[7:8, :]
    last_sum = sums[HALF - 8 : HALF, :] + jnp.where(row == 7, late[:, :256], 0.0)
    lead_sum = jnp.where(row == 0, sums[HALF : HALF + 8, :] + early[:, :256], 0.0)
    last_count = counts[HALF - 8 : HALF, :] + jnp.where(row == 7, late[:, 256:], 0.0)
    lead_count = jnp.where(row == 0, counts[HALF : HALF + 8, :] + early[:, 256:384], 0.0)
    spare = jnp.zeros((8, 256), jnp.float32)
    all_sums = jnp.concatenate([sums[: HALF - 8, :], last_sum, lead_sum, spare], axis=0)
    all_counts = jnp.concatenate(
        [counts[: HALF - 8, :], last_count, lead_count, spare[:, :HALF]], axis=0
    )[:, :1]
    all_counts = jnp.maximum(all_counts, 1.0)
    lead_cot = jnp.where(row == 0, early[:, 384:], 0.0)
    all_cot = jnp.concatenate([cotangent[...], lead_cot, jnp.zeros((8, 512), jnp.float32)], axis=0)

    pooled_mean = (all_sums / all_counts).astype(jnp.bfloat16)
    pre_norm = jnp.dot(pooled_mean, w_pool[...], preferred_element_type=jnp.float32) + b_pool[...]
    pooled_normed, pooled_inv = layer_stats(pre_norm)
    slope_grad = all_cot * gelu_slope(pooled_normed * pool_gain[...])
    grad_pre = norm_back(slope_grad * pool_gain[...], pooled_normed, pooled_inv)
    grad_pre_b = grad_pre.astype(jnp.bfloat16)
    share = against_rows(grad_pre_b, w_pool[...]) / all_counts
    share_b = share.astype(jnp.bfloat16)
    rest_b = (share - share_b.astype(jnp.float32)).astype(jnp.bfloat16)
    dmixed_main = inner_rows(member, share_b)
    dmixed_ref[...] = dmixed_main + inner_rows(member, rest_b)
    dmixed_b = dmixed_main.astype(jnp.bfloat16)
    datt = against_rows(dmixed_b, w_out[...]).astype(jnp.bfloat16)
    datt_f = datt.astype(jnp.float32)
    datt_ref[...] = (datt_f * 0.25).astype(jnp.bfloat16)
    product = datt_f * att[...].astype(jnp.float32)
    datt_t = against_rows(w_out[...], dmixed_b).astype(jnp.bfloat16).astype(jnp.float32)
    datt_t_ref[...] = (datt_t * 0.25).astype(jnp.bfloat16)
    slot = lax.broadcasted_iota(jnp.int32, (256, 256), 0)
    channel = lax.broadcasted_iota(jnp.int32, (256, 256), 1)
    spot = slot % HALF - LOG_LANE
    place = (channel // HALF == slot // HALF) & (spot >= 0) & (spot < 24)
    place = (place & (spot % PER_HALF == channel % HALF // HEAD_SIZE)).astype(jnp.float32)
    place = place.astype(jnp.bfloat16)
    first = product.astype(jnp.bfloat16)
    second = product - first.astype(jnp.float32)
    second_b = second.astype(jnp.bfloat16)
    third_b = (second - second_b.astype(jnp.float32)).astype(jnp.bfloat16)
    deltas = against_rows(place, first) + against_rows(place, second_b) + against_rows(place, third_b)
    which = (lax.broadcasted_iota(jnp.int32, (256, 1), 0) % HALF - LOG_LANE) // PER_HALF
    delta_ref[...] = split_three(deltas * -0.25, which).astype(jnp.bfloat16)
    gw_pool[...] = (inner_rows(pooled_mean[:HALF], grad_pre_b[:HALF]) * scale).astype(jnp.bfloat16)
    gw_out[...] = (inner_rows(att[...], dmixed_b) * scale).astype(jnp.bfloat16)
    gb_pool[...] = jnp.sum(grad_pre[:HALF], axis=0, keepdims=True) * scale
    g_gain[...] = jnp.sum(slope_grad[:HALF] * pooled_normed[:HALF], axis=0, keepdims=True) * scale


def pool(scale, *arrays):
    half = jnp.bfloat16
    vmem = pl.BlockSpec(memory_space=pltpu.VMEM)
    return pl.pallas_call(
        functools.partial(pool_kernel, scale),
        out_shape=[
            jax.ShapeDtypeStruct((PATCH, 256), jnp.float32),
            jax.ShapeDtypeStruct((PATCH, 256), half),
            jax.ShapeDtypeStruct((256, PATCH), half),
            jax.ShapeDtypeStruct((256, PATCH), half),
            jax.ShapeDtypeStruct((256, 512), half),
            jax.ShapeDtypeStruct((256, 256), half),
            jax.ShapeDtypeStruct((1, 512), jnp.float32),
            jax.ShapeDtypeStruct((1, 512), jnp.float32),
        ],
        in_specs=[vmem] * 9,
        out_specs=[vmem] * 8,
        scratch_shapes=[
            pltpu.VMEM((8, 384), jnp.float32),
            pltpu.VMEM((8, 896), jnp.float32),
            pltpu.VMEM((8, 384), jnp.float32),
            pltpu.VMEM((8, 896), jnp.float32),
            pltpu.SemaphoreType.DMA((2, 2)),
        ],
        compiler_params=pltpu.CompilerParams(
            collective_id=2, has_side_effects=True, vmem_limit_bytes=32 * 1024 * 1024
        ),
        name="pooling",
    )(*arrays)


def backward_kernel(
    spans, q_ref, qt_ref, logs_ref, do_ref, dot_ref, deltas_ref, kg_ref, vg_ref,
    dq_ref, dk_ref, dv_ref, qt, dt, qn, dn, some, slopes, dqt, dk_sum, dv_sum,
):
    tile = pl.program_id(1)
    start, count = spans[tile, 0], spans[tile, 1]
    q_both = jnp.concatenate([qt_ref[...], logs_ref[...]], axis=0)
    d_both = jnp.concatenate([dot_ref[...], deltas_ref[...]], axis=0)
    for h in range(PER_HALF):
        p, place = h // PAIR, slice(h % PAIR * TILE, (h % PAIR + 1) * TILE)
        rows = head_mask(h, 0)
        qt[p, :, place] = q_both * rows
        dt[p, :, place] = d_both * rows
        lanes = head_mask(h, 1)[:, :HALF]
        qn[p, place, :] = q_ref[...] * lanes
        dn[p, place, :] = do_ref[...] * lanes
    dqt[...] = jnp.zeros_like(dqt)

    @pl.when(tile == 0)
    def _():
        dk_sum[...] = jnp.zeros_like(dk_sum)
        dv_sum[...] = jnp.zeros_like(dv_sum)

    def chunk(c, carry):
        rows = pl.ds(pl.multiple_of(start + c * CHUNK, 16), CHUNK)
        keys_t = kg_ref[rows, :HALF].astype(jnp.float32).T.astype(jnp.bfloat16)
        for p in range(PER_HALF // PAIR):
            weights = jnp.exp(jnp.dot(kg_ref[rows, :], qt[p], preferred_element_type=jnp.float32))
            dweights = jnp.dot(vg_ref[rows, :], dt[p], preferred_element_type=jnp.float32)
            place = slice(p * PAIR * TILE, (p + 1) * PAIR * TILE)
            some[:, place] = weights.astype(jnp.bfloat16)
            slopes[:, place] = (weights * dweights).astype(jnp.bfloat16)
        depth = PER_HALF * TILE
        dk = jnp.dot(slopes[...], qn[...].reshape(depth, HALF), preferred_element_type=jnp.float32)
        dv = jnp.dot(some[...], dn[...].reshape(depth, HALF), preferred_element_type=jnp.float32)
        for p in range(PER_HALF // PAIR):
            own = slice(p * PAIR * HEAD_SIZE, (p + 1) * PAIR * HEAD_SIZE)
            place = slice(p * PAIR * TILE, (p + 1) * PAIR * TILE)
            dqt[own, :] += jnp.dot(keys_t[own], slopes[:, place], preferred_element_type=jnp.float32)
        dk_sum[rows, :] += dk
        dv_sum[rows, :] += dv
        return carry

    lax.fori_loop(0, count, chunk, 0)
    parts = []
    for h in range(PER_HALF):
        place = slice(h % PAIR * TILE, (h % PAIR + 1) * TILE)
        parts.append(dqt[h * HEAD_SIZE : (h + 1) * HEAD_SIZE, place])
    dq_ref[...] = jnp.concatenate(parts, axis=0).T.astype(jnp.bfloat16)

    @pl.when(tile == TILES - 1)
    def _():
        dk_ref[...] = (dk_sum[:WINDOW] * 4.0).astype(jnp.bfloat16)
        dv_ref[...] = (dv_sum[:WINDOW] * 4.0).astype(jnp.bfloat16)


def attend_back(spans, queries, queries_t, logs, douts, douts_t, deltas, keys_g, values_g):
    tall = pl.BlockSpec((None, TALL, 2 * HALF), lambda g, t: (g, 0, 0))
    mine = pl.BlockSpec((TILE, HALF), lambda g, t: (t, g))
    turned = pl.BlockSpec((HALF, TILE), lambda g, t: (g, t))
    sums = pl.BlockSpec((WINDOW, HALF), lambda g, t: (0, g))
    half = jnp.bfloat16
    return pl.pallas_call(
        backward_kernel,
        grid=(2, TILES),
        out_shape=[
            jax.ShapeDtypeStruct((PATCH, 256), half),
            jax.ShapeDtypeStruct((WINDOW, 256), half),
            jax.ShapeDtypeStruct((WINDOW, 256), half),
        ],
        in_specs=[pl.BlockSpec(memory_space=pltpu.SMEM)]
        + [mine, turned, turned, mine, turned, turned, tall, tall],
        out_specs=[mine, sums, sums],
        scratch_shapes=[
            pltpu.VMEM((PER_HALF // PAIR, 2 * HALF, PAIR * TILE), half),
            pltpu.VMEM((PER_HALF // PAIR, 2 * HALF, PAIR * TILE), half),
            pltpu.VMEM((PER_HALF // PAIR, PAIR * TILE, HALF), half),
            pltpu.VMEM((PER_HALF // PAIR, PAIR * TILE, HALF), half),
            pltpu.VMEM((CHUNK, 256 * PER_HALF // PAIR), half),
            pltpu.VMEM((CHUNK, 256 * PER_HALF // PAIR), half),
            pltpu.VMEM((HALF, PAIR * TILE), jnp.float32),
            pltpu.VMEM((TALL, HALF), jnp.float32),
            pltpu.VMEM((TALL, HALF), jnp.float32),
        ],
        compiler_params=pltpu.CompilerParams(vmem_limit_bytes=40 * 1024 * 1024),
        name="attention_back",
    )(spans, queries, queries_t, logs, douts, douts_t, deltas, keys_g, values_g)


UNIT = 128
EXTRA = 16
CORE_ROWS = 12 * UNIT
X_ROWS = CORE_ROWS // 4
Y_ROWS = X_ROWS // 8


def axes():
    me = lax.axis_index("pts")
    core, z, y, x = me % 2, (me // 2) % 8, (me // 16) % 8, me // 128
    return (
        (core, 2, lambda r: x * 128 + y * 16 + z * 2 + r),
        (x, 4, lambda r: r * 128 + y * 16 + z * 2 + core),
        (y, 8, lambda r: x * 128 + r * 16 + z * 2 + core),
        (z, 8, lambda r: x * 128 + y * 16 + r * 2 + core),
    )


def swap(axis, source, landing, sems, first):
    rank, size, device = axis
    copies = []
    for k in range(1, size):
        peer = (rank + k) % size
        copies.append(send(source(peer), landing(rank), sems, first + k - 1, device(peer)))
    return copies


def wait_all(copies):
    for copy in copies:
        copy.wait()


def slot_sum(ref, start, size):
    total = ref[0, start : start + size, :].astype(jnp.float32)
    for r in range(1, ref.shape[0]):
        total = total + ref[r, start : start + size, :].astype(jnp.float32)
    return total


def finish_kernel(
    scale, hidden, dq, dk, dv, dmixed, points, gain, w_qkv, gw_out, gw_pool, gb_pool, g_gain,
    grad_points, reduced, extras,
    low_k, low_v, high_k, high_v, send_c, recv_c, send_x, recv_x, send_y, recv_y, recv_z,
    gather_y, gather_x, gather_c, sems,
):
    me, before, after = neighbours()
    on_core, on_x, on_y, on_z = axes()
    barrier = pltpu.get_barrier_semaphore()
    greeted = [before, after]
    for rank, size, device in (on_core, on_x, on_y, on_z):
        greeted += [device((rank + k) % size) for k in range(1, size)]
    for device in greeted:
        pl.semaphore_signal(barrier, inc=1, device_id=(device,), device_id_type=MESH)

    def fill(block, first_unit):
        for column in range(block.shape[1] // UNIT):
            unit = first_unit + 2 * column
            start = unit % 12 * UNIT
            send_c[unit // 12, start : start + 2 * UNIT, :] = block[:, column * UNIT : (column + 1) * UNIT]

    fill(gw_out[...], 12)
    fill(gw_pool[...], 16)
    pieces = [gb_pool[:, i * UNIT : (i + 1) * UNIT] for i in range(4)]
    pieces += [g_gain[:, i * UNIT : (i + 1) * UNIT] for i in range(4)]
    pieces += [jnp.zeros((EXTRA - 8, UNIT), jnp.float32)]
    packed = jnp.concatenate(pieces, axis=0).astype(jnp.bfloat16)
    for r in range(2):
        send_c[r, CORE_ROWS:, :] = packed
    pl.semaphore_wait(barrier, len(greeted))
    rims = [
        send(dk.at[pl.ds(0, PATCH)], high_k, sems, 40, before),
        send(dv.at[pl.ds(0, PATCH)], high_v, sems, 41, before),
        send(dk.at[pl.ds(2 * PATCH, PATCH)], low_k, sems, 42, after),
        send(dv.at[pl.ds(2 * PATCH, PATCH)], low_v, sems, 43, after),
    ]
    own = slice(PATCH, 2 * PATCH)
    fill((inner_rows(hidden[own, :], dq[...]) * scale).astype(jnp.bfloat16), 0)
    fill((inner_rows(hidden[...], dk[...]) * scale).astype(jnp.bfloat16), 4)
    fill((inner_rows(hidden[...], dv[...]) * scale).astype(jnp.bfloat16), 8)

    copies = swap(on_core, lambda r: send_c.at[r], lambda r: recv_c, sems, 0)
    dhidden = against_rows(dq[...], w_qkv[:, :256])
    wait_all(copies)
    kept = send_c.at[on_core[0]]
    extra = (
        kept[CORE_ROWS:, :].astype(jnp.float32) + recv_c[CORE_ROWS:, :].astype(jnp.float32)
    ).astype(jnp.bfloat16)
    for r in range(4):
        rows = slice(r * X_ROWS, (r + 1) * X_ROWS)
        total = kept[rows, :].astype(jnp.float32) + recv_c[rows, :].astype(jnp.float32)
        send_x[r, :X_ROWS, :] = total.astype(jnp.bfloat16)
        send_x[r, X_ROWS:, :] = extra

    copies = swap(on_x, lambda r: send_x.at[r], lambda r: recv_x.at[r], sems, 1)
    recv_x[on_x[0]] = send_x[on_x[0]]
    wait_all(rims)
    for columns, mine, low, high in (
        (slice(256, 512), dk, low_k, high_k), (slice(512, 768), dv, low_v, high_v)
    ):
        total = mine[own, :].astype(jnp.float32) + low[...].astype(jnp.float32)
        total = (total + high[...].astype(jnp.float32)).astype(jnp.bfloat16)
        dhidden = dhidden + against_rows(total, w_qkv[:, columns])
    normed, inv_std = layer_stats(points[...].astype(jnp.float32))
    grad_points[...] = dmixed[...] + norm_back(dhidden * gain[...], normed, inv_std)
    wait_all(copies)
    extra = slot_sum(recv_x, X_ROWS, EXTRA).astype(jnp.bfloat16)
    for r in range(8):
        send_y[r, :Y_ROWS, :] = slot_sum(recv_x, r * Y_ROWS, Y_ROWS).astype(jnp.bfloat16)
        send_y[r, Y_ROWS:, :] = extra

    copies = swap(on_y, lambda r: send_y.at[r], lambda r: recv_y.at[r], sems, 4)
    recv_y[on_y[0]] = send_y[on_y[0]]
    wait_all(copies)
    recv_z[on_z[0]] = slot_sum(recv_y, 0, Y_ROWS + EXTRA).astype(jnp.bfloat16)

    wait_all(swap(on_z, lambda r: recv_z.at[on_z[0]], lambda r: recv_z.at[r], sems, 11))
    total = slot_sum(recv_z, 0, Y_ROWS + EXTRA)
    extras[...] = total[Y_ROWS:]
    gather_y[on_y[0]] = total[:Y_ROWS].astype(jnp.bfloat16)
    wait_all(swap(on_y, lambda r: gather_y.at[on_y[0]], lambda r: gather_y.at[r], sems, 18))
    gather_x[on_x[0]] = gather_y[...]
    copies = swap(on_x, lambda r: gather_y, lambda r: gather_x.at[r], sems, 25)
    wait_all(copies)
    gather_c[on_core[0]] = gather_x[...]
    wait_all(swap(on_core, lambda r: gather_x, lambda r: gather_c.at[r], sems, 28))
    for c in range(2):
        for r in range(4):
            for s in range(8):
                start = c * CORE_ROWS + r * X_ROWS + s * Y_ROWS
                reduced[start : start + Y_ROWS, :] = gather_c[c, r, s]
    weighted = jnp.zeros((256, UNIT), jnp.float32)
    for column in range(6):
        block = reduced[column * 256 : (column + 1) * 256, :].astype(jnp.float32)
        lanes = slice(column * UNIT, (column + 1) * UNIT)
        weighted = weighted + block * w_qkv[:, lanes].astype(jnp.float32)
    summed_gain = jnp.sum(weighted.T, axis=0, keepdims=True) / gain[...]
    for i in range(2):
        extras[8 + i : 9 + i, :] = summed_gain[:, i * UNIT : (i + 1) * UNIT]


def finish(scale, *arrays):
    half = jnp.bfloat16
    vmem = pl.BlockSpec(memory_space=pltpu.VMEM)
    return pl.pallas_call(
        functools.partial(finish_kernel, scale),
        out_shape=[
            jax.ShapeDtypeStruct((PATCH, 256), jnp.float32),
            jax.ShapeDtypeStruct((2 * CORE_ROWS, UNIT), half),
            jax.ShapeDtypeStruct((EXTRA, UNIT), jnp.float32),
        ],
        in_specs=[vmem] * 12,
        out_specs=[vmem] * 3,
        scratch_shapes=[pltpu.VMEM((PATCH, 256), half)] * 4
        + [
            pltpu.VMEM((2, CORE_ROWS + EXTRA, UNIT), half),
            pltpu.VMEM((CORE_ROWS + EXTRA, UNIT), half),
            pltpu.VMEM((4, X_ROWS + EXTRA, UNIT), half),
            pltpu.VMEM((4, X_ROWS + EXTRA, UNIT), half),
            pltpu.VMEM((8, Y_ROWS + EXTRA, UNIT), half),
            pltpu.VMEM((8, Y_ROWS + EXTRA, UNIT), half),
            pltpu.VMEM((8, Y_ROWS + EXTRA, UNIT), half),
            pltpu.VMEM((8, Y_ROWS, UNIT), half),
            pltpu.VMEM((4, 8, Y_ROWS, UNIT), half),
            pltpu.VMEM((2, 4, 8, Y_ROWS, UNIT), half),
            pltpu.SemaphoreType.DMA((2, 44)),
        ],
        compiler_params=pltpu.CompilerParams(
            collective_id=3, has_side_effects=True, vmem_limit_bytes=40 * 1024 * 1024
        ),
        name="finish",
    )(*arrays)


def unpack_kernel(reduced, extras, rows_in, gq, go, gn, gp, gb, gg, rows_out, sem):
    copy = pltpu.make_async_copy(rows_in, rows_out, sem)
    copy.start()
    for column in range(12):
        block = reduced[column * 256 : (column + 1) * 256, :].astype(jnp.float32)
        if column < 6:
            gq[:, column * UNIT : (column + 1) * UNIT] = block
        elif column < 8:
            go[:, (column - 6) * UNIT : (column - 5) * UNIT] = block
        else:
            gp[:, (column - 8) * UNIT : (column - 7) * UNIT] = block
    for i in range(2):
        gn[:, i * UNIT : (i + 1) * UNIT] = extras[8 + i : 9 + i, :]
    for i in range(4):
        gb[:, i * UNIT : (i + 1) * UNIT] = extras[i : i + 1, :]
        gg[:, i * UNIT : (i + 1) * UNIT] = extras[4 + i : 5 + i, :]
    copy.wait()


def unpack(reduced, extras, rows):
    vmem = pl.BlockSpec(memory_space=pltpu.VMEM)
    outside = pl.BlockSpec(memory_space=pl.ANY)
    shapes = ((256, 768), (256, 256), (1, 256), (256, 512), (1, 512), (1, 512), (PATCH, 256))
    return pl.pallas_call(
        unpack_kernel,
        out_shape=[jax.ShapeDtypeStruct(shape, jnp.float32) for shape in shapes],
        in_specs=[vmem, vmem, vmem],
        out_specs=[vmem] * 6 + [outside],
        scratch_shapes=[pltpu.SemaphoreType.DMA],
        name="unpack",
    )(reduced, extras, rows)


def body(
    points, patch_ids, cell_ids, norm_gain, w_qkv, w_out, w_pool, b_pool, pool_gain, cotangent
):
    scale = 1.0 / math.sqrt(points.shape[0] * lax.axis_size("pts"))
    gain = norm_gain[None]
    cells = cell_ids.reshape(4, HALF)
    queries, queries_t, keys_g, values_g, marks_f, hidden, spans = prepare(
        points, patch_ids.reshape(4, HALF), gain, w_qkv
    )
    attended, logs, sums, counts = attend(
        spans, queries_t, marks_f, keys_g, values_g, points, w_out, cells
    )
    dmixed, datt, datt_t, deltas, gw_pool, gw_out, gb_pool, g_gain = pool(
        scale, sums, counts, cells, attended, w_out, w_pool, b_pool[None], pool_gain[None], cotangent
    )
    dq, dk, dv = attend_back(
        spans, queries, queries_t, logs, datt, datt_t, deltas, keys_g, values_g
    )
    grad_points, reduced, extras = finish(
        scale, hidden, dq, dk, dv, dmixed, points, gain, w_qkv, gw_out, gw_pool, gb_pool, g_gain
    )
    gq, go, gn, gp, gb, gg, grad_points = unpack(reduced, extras, grad_points)
    return (grad_points, gq, go, gn[0], gp, gb[0], gg[0])


def solution(mesh):
    in_specs = (P("pts", None), P("pts"), P("pts"), P(), P(), P(), P(), P(), P(), P("pts", None))
    out_specs = (P("pts", None), P(), P(), P(), P(), P(), P())
    return jax.shard_map(body, mesh=mesh, in_specs=in_specs, out_specs=out_specs, check_vma=False)
```

```python
import functools
import math

import jax
import jax.numpy as jnp
from jax import lax
from jax.experimental import pallas as pl
from jax.experimental.pallas import tpu as pltpu
from jax.sharding import PartitionSpec as P

PATCH = 512
MESH = pl.DeviceIdType.MESH


EPS = 1e-05
ROOT_HALF = 0.7071067811865476
ROOT_TWO_PI = 2.5066282746310002


def layer_stats(values):
    centered = values - jnp.mean(values, axis=-1, keepdims=True)
    inv_std = lax.rsqrt(jnp.mean(centered * centered, axis=-1, keepdims=True) + EPS)
    return (centered * inv_std, inv_std)


def norm_back(grad_normed, normed, inv_std):
    first_mean = jnp.mean(grad_normed, axis=-1, keepdims=True)
    second_mean = jnp.mean(grad_normed * normed, axis=-1, keepdims=True)
    return inv_std * (grad_normed - first_mean - normed * second_mean)


def gelu_slope(scaled):
    normal_cdf = 0.5 * (1.0 + lax.erf(scaled * ROOT_HALF))
    return normal_cdf + scaled * jnp.exp(-0.5 * scaled * scaled) / ROOT_TWO_PI


def inner_rows(left, right):
    return lax.dot_general(
        left, right, (((0,), (0,)), ((), ())), preferred_element_type=jnp.float32
    )


def against_rows(left, right):
    return lax.dot_general(
        left, right, (((1,), (1,)), ((), ())), preferred_element_type=jnp.float32
    )


HALF = 128
PER_HALF = 8
HEAD_SIZE = 16
TILE = 128
CHUNK = 528
TALL = 3 * CHUNK
TILES = PATCH // TILE
PAIR = 256 // TILE
WINDOW = 3 * PATCH
FAR = float(2**30)
DIGIT = 32
LOG_LANE = 64


def head_mask(h, axis):
    shape = (1, 2 * HALF) if axis else (2 * HALF, 1)
    place = lax.broadcasted_iota(jnp.int32, shape, axis)
    own = (place >= h * HEAD_SIZE) & (place < (h + 1) * HEAD_SIZE)
    marks = (place >= HALF) & (place < HALF + LOG_LANE)
    terms = (place >= HALF + LOG_LANE) & (place < HALF + LOG_LANE + 24) & (place % PER_HALF == h)
    return (own | marks | terms).astype(jnp.float32).astype(jnp.bfloat16)


def split_three(values, which):
    first = values.astype(jnp.bfloat16).astype(jnp.float32)
    second = (values - first).astype(jnp.bfloat16).astype(jnp.float32)
    third = values - first - second
    return jnp.where(which == 0, first, jnp.where(which == 1, second, third))


def neighbours():
    me = lax.axis_index("pts")
    count = lax.axis_size("pts")
    return me, (me + count - 1) % count, (me + 1) % count


def greet_neighbours(before, after):
    barrier = pltpu.get_barrier_semaphore()
    for device in (before, after):
        pl.semaphore_signal(barrier, inc=1, device_id=(device,), device_id_type=MESH)
    pl.semaphore_wait(barrier, 2)


def send(source, landing, sems, index, device):
    copy = pltpu.make_async_remote_copy(
        src_ref=source,
        dst_ref=landing,
        send_sem=sems.at[0, index],
        recv_sem=sems.at[1, index],
        device_id=(device,),
        device_id_type=MESH,
    )
    copy.start()
    return copy


def digit_columns(marks):
    row = lax.broadcasted_iota(jnp.int32, (HALF, HALF), 0)
    high, low = marks // DIGIT, marks % DIGIT
    hit = ((row < DIGIT) & (row == high)) | ((row >= DIGIT) & (row < LOG_LANE) & (row - DIGIT == low))
    return hit.astype(jnp.float32)


def prepare_kernel(
    points_hbm, ids_hbm, gain_hbm, w_hbm, q_ref, qt_ref, kg_ref, vg_ref, f_ref, hidden_ref, spans_ref,
    points, ids, gain, w_qkv, marks, marks_low, marks_high, rows_low, rows_high, sems, local_sems,
):
    me, before, after = neighbours()
    local = []
    for i, (source, target) in enumerate(
        ((ids_hbm, ids), (points_hbm, points), (w_hbm, w_qkv), (gain_hbm, gain))
    ):
        local.append(pltpu.make_async_copy(source, target, local_sems.at[i]))
        local[-1].start()
    marks[...] = jnp.zeros_like(marks)
    greet_neighbours(before, after)
    local[0].wait()
    marks[:4, :] = ids[...] + 1
    local[1].wait()
    copies = [
        send(points, rows_high, sems, 0, before),
        send(points, rows_low, sems, 1, after),
        send(marks, marks_high, sems, 2, before),
        send(marks, marks_low, sems, 3, after),
    ]
    local[2].wait()
    local[3].wait()

    def project(block, first, columns):
        normed, _ = layer_stats(block[...].astype(jnp.float32))
        hidden = (normed * gain[...]).astype(jnp.bfloat16)
        hidden_ref[first : first + PATCH, :] = hidden
        return jnp.dot(hidden, w_qkv[:, columns], preferred_element_type=jnp.float32)

    def place(first, keys, values):
        for g in range(2):
            lanes = slice(g * HALF, (g + 1) * HALF)
            kg_ref[g, first : first + PATCH, :HALF] = keys[:, lanes].astype(jnp.bfloat16)
            vg_ref[g, first : first + PATCH, :HALF] = values[:, lanes].astype(jnp.bfloat16)

    def place_marks(block, first, own):
        lane = lax.broadcasted_iota(jnp.int32, (HALF, HALF), 1)
        row = lax.broadcasted_iota(jnp.int32, (HALF, HALF), 0)
        terms = (lane >= LOG_LANE) & (lane < LOG_LANE + 24)
        for i in range(4):
            rows = slice(first + i * HALF, first + (i + 1) * HALF)
            digits = digit_columns(block[i : i + 1, :])
            both = jnp.where(terms, 1.0, digits.T).astype(jnp.bfloat16)
            for g in range(2):
                kg_ref[g, rows, HALF:] = both
                vg_ref[g, rows, HALF:] = both
            if own:
                away = jnp.where(row < LOG_LANE, (1.0 - digits) * -FAR, 0.0)
                f_ref[:, i * HALF : (i + 1) * HALF] = away.astype(jnp.bfloat16)

    qkv = project(points, PATCH, slice(None))
    queries = qkv[:, :256].astype(jnp.bfloat16).astype(jnp.float32) * 0.25
    q_ref[...] = queries.astype(jnp.bfloat16)
    qt_ref[...] = queries.T.astype(jnp.bfloat16)
    place(PATCH, qkv[:, 256:512], qkv[:, 512:])
    own = marks[...]
    place_marks(own, PATCH, True)
    lane = lax.broadcasted_iota(jnp.int32, (TALL - WINDOW, 2 * HALF), 1)
    nowhere = ((lane == HALF) | (lane == HALF + DIGIT)).astype(jnp.float32).astype(jnp.bfloat16)
    for g in range(2):
        kg_ref[g, WINDOW:, :] = nowhere
        vg_ref[g, WINDOW:, :] = nowhere
    for copy in copies[2:]:
        copy.wait()
    low = jnp.where(me == 0, 0, marks_low[...])
    high = jnp.where(me == lax.axis_size("pts") - 1, 0, marks_high[...])
    place_marks(low, 0, False)
    place_marks(high, 2 * PATCH, False)
    own_f, low_f, high_f = (block[:4].astype(jnp.float32) for block in (own, low, high))
    for t in range(TILES):
        ours = own_f[t * TILE // HALF : (t + 1) * TILE // HALF]
        first, last = jnp.min(ours), jnp.max(ours)
        lower = jnp.sum((low_f < first).astype(jnp.float32) + (own_f < first).astype(jnp.float32))
        upper = jnp.sum(
            ((high_f > 0) & (high_f <= last)).astype(jnp.float32) + (own_f <= last).astype(jnp.float32)
        )
        lower = lower.astype(jnp.int32) // 16 * 16
        count = (PATCH + upper.astype(jnp.int32) - lower + CHUNK - 1) // CHUNK
        spans_ref[t, 0] = jnp.minimum(lower, TALL - count * CHUNK)
        spans_ref[t, 1] = count
    for copy, block, first in ((copies[1], rows_low, 0), (copies[0], rows_high, 2 * PATCH)):
        copy.wait()
        kv = project(block, first, slice(256, 768))
        place(first, kv[:, :256], kv[:, 256:])


def prepare(points, ids, gain, w_qkv):
    half = jnp.bfloat16
    vmem = pl.BlockSpec(memory_space=pltpu.VMEM)
    return pl.pallas_call(
        prepare_kernel,
        out_shape=[
            jax.ShapeDtypeStruct((PATCH, 256), half),
            jax.ShapeDtypeStruct((256, PATCH), half),
            jax.ShapeDtypeStruct((2, TALL, 2 * HALF), half),
            jax.ShapeDtypeStruct((2, TALL, 2 * HALF), half),
            jax.ShapeDtypeStruct((HALF, PATCH), half),
            jax.ShapeDtypeStruct((WINDOW, 256), half),
            jax.ShapeDtypeStruct((TILES, 2), jnp.int32),
        ],
        in_specs=[pl.BlockSpec(memory_space=pltpu.HBM)] * 4,
        out_specs=[vmem] * 6 + [pl.BlockSpec(memory_space=pltpu.SMEM)],
        scratch_shapes=[
            pltpu.VMEM((PATCH, 256), half),
            pltpu.VMEM((4, HALF), jnp.int32),
            pltpu.VMEM((1, 256), jnp.float32),
            pltpu.VMEM((256, 768), half),
            pltpu.VMEM((8, HALF), jnp.int32),
            pltpu.VMEM((8, HALF), jnp.int32),
            pltpu.VMEM((8, HALF), jnp.int32),
            pltpu.VMEM((PATCH, 256), half),
            pltpu.VMEM((PATCH, 256), half),
            pltpu.SemaphoreType.DMA((2, 4)),
            pltpu.SemaphoreType.DMA((4,)),
        ],
        compiler_params=pltpu.CompilerParams(
            collective_id=1, has_side_effects=True, vmem_limit_bytes=32 * 1024 * 1024
        ),
        name="prepare",
    )(points, ids, gain, w_qkv)


SLOTS = 144


def membership(cells):
    local = cells - lax.axis_index("pts") * HALF
    local = jnp.where(local < 0, HALF, local)
    slot = lax.broadcasted_iota(jnp.int32, (SLOTS, HALF), 0)
    parts = [(slot == local[i : i + 1, :]).astype(jnp.float32) for i in range(4)]
    return jnp.concatenate(parts, axis=1)


def tall_max(scores):
    part = CHUNK // 6
    folded = scores[:part]
    for i in range(1, 6):
        folded = jnp.maximum(folded, scores[i * part : (i + 1) * part])
    return jnp.max(folded, axis=0, keepdims=True)


def forward_kernel(
    spans, qt_ref, f_ref, kg_ref, vg_ref, points_hbm, w_out_hbm, cells_hbm,
    att_ref, logs_ref, sums_ref, counts_ref, qt, kept, att_t, top_t, total_t, points, w_out, cells, sems,
):
    tile, half = pl.program_id(0), pl.program_id(1)
    start, count = spans[tile, 0], spans[tile, 1]
    late = [
        pltpu.make_async_copy(source, target, sems.at[i])
        for i, (source, target) in enumerate(
            ((points_hbm, points), (w_out_hbm, w_out), (cells_hbm, cells))
        )
    ]

    @pl.when((tile == 0) & (half == 0))
    def _():
        for copy in late:
            copy.start()

    both = jnp.concatenate([qt_ref[...], f_ref[...]], axis=0)
    for h in range(PER_HALF):
        qt[h // PAIR, :, h % PAIR * TILE : (h % PAIR + 1) * TILE] = both * head_mask(h, 0)
    top_t[...] = jnp.full_like(top_t, -3e38)
    total_t[...] = jnp.zeros_like(total_t)
    att_t[...] = jnp.zeros_like(att_t)

    def chunk(c, carry):
        rows = pl.ds(pl.multiple_of(start + c * CHUNK, 16), CHUNK)
        values_t = vg_ref[half, rows, :HALF].astype(jnp.float32).T.astype(jnp.bfloat16)
        ones = jnp.ones((16, CHUNK), jnp.bfloat16)
        tops = []
        for p in range(PER_HALF // PAIR):
            scores = jnp.dot(kg_ref[half, rows, :], qt[p], preferred_element_type=jnp.float32)
            kept[p] = scores
            tops.append(jnp.maximum(top_t[p : p + 1, :], tall_max(scores)))
        for p in range(PER_HALF // PAIR):
            before, top = top_t[p : p + 1, :], tops[p]
            weights = jnp.exp(kept[p] - top).astype(jnp.bfloat16)
            decay = jnp.exp(before - top)
            top_t[p : p + 1, :] = top
            own = slice(p * PAIR * HEAD_SIZE, (p + 1) * PAIR * HEAD_SIZE)
            left = jnp.concatenate([values_t[own], ones], axis=0)
            mixed = jnp.dot(left, weights, preferred_element_type=jnp.float32)
            count_rows = PAIR * HEAD_SIZE
            total_t[p : p + 1, :] = total_t[p : p + 1, :] * decay + mixed[count_rows : count_rows + 1]
            att_t[own, :] = att_t[own, :] * decay + mixed[:count_rows]
        return carry

    lax.fori_loop(0, count, chunk, 0)
    rows = pl.ds(pl.multiple_of(tile * TILE, TILE), TILE)
    logs_p = -(top_t[...] + jnp.log(total_t[...]))
    parts, logs = [], []
    for h in range(PER_HALF):
        p, columns = h // PAIR, slice(h % PAIR * TILE, (h % PAIR + 1) * TILE)
        mine = att_t[h * HEAD_SIZE : (h + 1) * HEAD_SIZE, columns]
        parts.append(mine / total_t[p : p + 1, columns])
        logs.append(logs_p[p : p + 1, columns])
    attended = jnp.concatenate(parts, axis=0).T.astype(jnp.bfloat16)
    for g in range(2):

        @pl.when(half == g)
        def _():
            att_ref[rows, g * HALF : (g + 1) * HALF] = attended

    logs = jnp.concatenate(logs, axis=0)
    terms = [split_three(logs, i) for i in range(3)]
    logs_ref[:LOG_LANE, :] = f_ref[:LOG_LANE, :]
    spare = jnp.zeros((HALF - LOG_LANE - 24, TILE), jnp.float32)
    logs_ref[LOG_LANE:, :] = jnp.concatenate(terms + [spare], axis=0).astype(jnp.bfloat16)

    @pl.when((tile == TILES - 1) & (half == 1))
    def _():
        for copy in late:
            copy.wait()
        mixed = points[...].astype(jnp.float32) + jnp.dot(
            att_ref[...], w_out[...], preferred_element_type=jnp.float32
        )
        member = membership(cells[...])
        sums_ref[...] = jnp.dot(
            member.astype(jnp.bfloat16), mixed.astype(jnp.bfloat16), preferred_element_type=jnp.float32
        )
        counts_ref[...] = jnp.broadcast_to(jnp.sum(member, axis=1, keepdims=True), (SLOTS, HALF))


def attend(spans, queries_t, marks_f, keys_g, values_g, points, w_out, cells):
    def whole(*shape):
        return pl.BlockSpec(shape, lambda t, g: (0,) * len(shape))

    outside = pl.BlockSpec(memory_space=pltpu.HBM)
    return pl.pallas_call(
        forward_kernel,
        grid=(TILES, 2),
        out_shape=[
            jax.ShapeDtypeStruct((PATCH, 256), jnp.bfloat16),
            jax.ShapeDtypeStruct((256, PATCH), jnp.bfloat16),
            jax.ShapeDtypeStruct((SLOTS, 256), jnp.float32),
            jax.ShapeDtypeStruct((SLOTS, HALF), jnp.float32),
        ],
        in_specs=[
            pl.BlockSpec(memory_space=pltpu.SMEM),
            pl.BlockSpec((HALF, TILE), lambda t, g: (g, t)),
            pl.BlockSpec((HALF, TILE), lambda t, g: (0, t)),
            whole(2, TALL, 2 * HALF),
            whole(2, TALL, 2 * HALF),
            outside,
            outside,
            outside,
        ],
        out_specs=[
            whole(PATCH, 256),
            pl.BlockSpec((HALF, TILE), lambda t, g: (g, t)),
            whole(SLOTS, 256),
            whole(SLOTS, HALF),
        ],
        scratch_shapes=[
            pltpu.VMEM((PER_HALF // PAIR, 2 * HALF, PAIR * TILE), jnp.bfloat16),
            pltpu.VMEM((PER_HALF // PAIR, CHUNK, PAIR * TILE), jnp.float32),
            pltpu.VMEM((HALF, PAIR * TILE), jnp.float32),
            pltpu.VMEM((PER_HALF // PAIR, PAIR * TILE), jnp.float32),
            pltpu.VMEM((PER_HALF // PAIR, PAIR * TILE), jnp.float32),
            pltpu.VMEM((PATCH, 256), jnp.bfloat16),
            pltpu.VMEM((256, 256), jnp.bfloat16),
            pltpu.VMEM((4, HALF), jnp.int32),
            pltpu.SemaphoreType.DMA((3,)),
        ],
        compiler_params=pltpu.CompilerParams(vmem_limit_bytes=40 * 1024 * 1024),
        name="attention",
    )(spans, queries_t, marks_f, keys_g, values_g, points, w_out, cells)


def pool_kernel(
    scale, sums, counts, cells, att, w_out, w_pool, b_pool, pool_gain, cotangent,
    dmixed_ref, datt_ref, datt_t_ref, delta_ref, gw_pool, gw_out, gb_pool, g_gain,
    back_pack, ahead_pack, from_after, from_before, sems,
):
    me, before, after = neighbours()
    back_pack[:, :256] = sums[HALF : HALF + 8, :]
    back_pack[:, 256:] = counts[HALF : HALF + 8, :]
    ahead_pack[:, :256] = sums[HALF - 8 : HALF, :]
    ahead_pack[:, 256:384] = counts[HALF - 8 : HALF, :]
    ahead_pack[:, 384:] = cotangent[HALF - 8 :, :]
    greet_neighbours(before, after)
    copies = [
        send(back_pack, from_after, sems, 0, before),
        send(ahead_pack, from_before, sems, 1, after),
    ]
    member = membership(cells[...]).astype(jnp.bfloat16)
    for copy in copies:
        copy.wait()
    row = lax.broadcasted_iota(jnp.int32, (8, 1), 0)
    late, early = from_after[0:1, :], from_before[7:8, :]
    last_sum = sums[HALF - 8 : HALF, :] + jnp.where(row == 7, late[:, :256], 0.0)
    lead_sum = jnp.where(row == 0, sums[HALF : HALF + 8, :] + early[:, :256], 0.0)
    last_count = counts[HALF - 8 : HALF, :] + jnp.where(row == 7, late[:, 256:], 0.0)
    lead_count = jnp.where(row == 0, counts[HALF : HALF + 8, :] + early[:, 256:384], 0.0)
    spare = jnp.zeros((8, 256), jnp.float32)
    all_sums = jnp.concatenate([sums[: HALF - 8, :], last_sum, lead_sum, spare], axis=0)
    all_counts = jnp.concatenate(
        [counts[: HALF - 8, :], last_count, lead_count, spare[:, :HALF]], axis=0
    )[:, :1]
    all_counts = jnp.maximum(all_counts, 1.0)
    lead_cot = jnp.where(row == 0, early[:, 384:], 0.0)
    all_cot = jnp.concatenate([cotangent[...], lead_cot, jnp.zeros((8, 512), jnp.float32)], axis=0)

    pooled_mean = (all_sums / all_counts).astype(jnp.bfloat16)
    pre_norm = jnp.dot(pooled_mean, w_pool[...], preferred_element_type=jnp.float32) + b_pool[...]
    pooled_normed, pooled_inv = layer_stats(pre_norm)
    slope_grad = all_cot * gelu_slope(pooled_normed * pool_gain[...])
    grad_pre = norm_back(slope_grad * pool_gain[...], pooled_normed, pooled_inv)
    grad_pre_b = grad_pre.astype(jnp.bfloat16)
    share = against_rows(grad_pre_b, w_pool[...]) / all_counts
    share_b = share.astype(jnp.bfloat16)
    rest_b = (share - share_b.astype(jnp.float32)).astype(jnp.bfloat16)
    dmixed_main = inner_rows(member, share_b)
    dmixed_ref[...] = dmixed_main + inner_rows(member, rest_b)
    dmixed_b = dmixed_main.astype(jnp.bfloat16)
    datt = against_rows(dmixed_b, w_out[...]).astype(jnp.bfloat16)
    datt_f = datt.astype(jnp.float32)
    datt_ref[...] = (datt_f * 0.25).astype(jnp.bfloat16)
    product = datt_f * att[...].astype(jnp.float32)
    datt_t = against_rows(w_out[...], dmixed_b).astype(jnp.bfloat16).astype(jnp.float32)
    datt_t_ref[...] = (datt_t * 0.25).astype(jnp.bfloat16)
    slot = lax.broadcasted_iota(jnp.int32, (256, 256), 0)
    channel = lax.broadcasted_iota(jnp.int32, (256, 256), 1)
    spot = slot % HALF - LOG_LANE
    place = (channel // HALF == slot // HALF) & (spot >= 0) & (spot < 24)
    place = (place & (spot % PER_HALF == channel % HALF // HEAD_SIZE)).astype(jnp.float32)
    place = place.astype(jnp.bfloat16)
    first = product.astype(jnp.bfloat16)
    second = product - first.astype(jnp.float32)
    second_b = second.astype(jnp.bfloat16)
    third_b = (second - second_b.astype(jnp.float32)).astype(jnp.bfloat16)
    deltas = against_rows(place, first) + against_rows(place, second_b) + against_rows(place, third_b)
    which = (lax.broadcasted_iota(jnp.int32, (256, 1), 0) % HALF - LOG_LANE) // PER_HALF
    delta_ref[...] = split_three(deltas * -0.25, which).astype(jnp.bfloat16)
    gw_pool[...] = (inner_rows(pooled_mean[:HALF], grad_pre_b[:HALF]) * scale).astype(jnp.bfloat16)
    gw_out[...] = (inner_rows(att[...], dmixed_b) * scale).astype(jnp.bfloat16)
    gb_pool[...] = jnp.sum(grad_pre[:HALF], axis=0, keepdims=True) * scale
    g_gain[...] = jnp.sum(slope_grad[:HALF] * pooled_normed[:HALF], axis=0, keepdims=True) * scale


def pool(scale, *arrays):
    half = jnp.bfloat16
    vmem = pl.BlockSpec(memory_space=pltpu.VMEM)
    return pl.pallas_call(
        functools.partial(pool_kernel, scale),
        out_shape=[
            jax.ShapeDtypeStruct((PATCH, 256), jnp.float32),
            jax.ShapeDtypeStruct((PATCH, 256), half),
            jax.ShapeDtypeStruct((256, PATCH), half),
            jax.ShapeDtypeStruct((256, PATCH), half),
            jax.ShapeDtypeStruct((256, 512), half),
            jax.ShapeDtypeStruct((256, 256), half),
            jax.ShapeDtypeStruct((1, 512), jnp.float32),
            jax.ShapeDtypeStruct((1, 512), jnp.float32),
        ],
        in_specs=[vmem] * 9,
        out_specs=[vmem] * 8,
        scratch_shapes=[
            pltpu.VMEM((8, 384), jnp.float32),
            pltpu.VMEM((8, 896), jnp.float32),
            pltpu.VMEM((8, 384), jnp.float32),
            pltpu.VMEM((8, 896), jnp.float32),
            pltpu.SemaphoreType.DMA((2, 2)),
        ],
        compiler_params=pltpu.CompilerParams(
            collective_id=2, has_side_effects=True, vmem_limit_bytes=32 * 1024 * 1024
        ),
        name="pooling",
    )(*arrays)


def backward_kernel(
    spans, q_ref, qt_ref, logs_ref, do_ref, dot_ref, deltas_ref, kg_ref, vg_ref,
    dq_ref, dk_ref, dv_ref, qt, dt, qn, dn, some, slopes, dqt, dk_sum, dv_sum,
):
    tile = pl.program_id(1)
    start, count = spans[tile, 0], spans[tile, 1]
    q_both = jnp.concatenate([qt_ref[...], logs_ref[...]], axis=0)
    d_both = jnp.concatenate([dot_ref[...], deltas_ref[...]], axis=0)
    for h in range(PER_HALF):
        p, place = h // PAIR, slice(h % PAIR * TILE, (h % PAIR + 1) * TILE)
        rows = head_mask(h, 0)
        qt[p, :, place] = q_both * rows
        dt[p, :, place] = d_both * rows
        lanes = head_mask(h, 1)[:, :HALF]
        qn[p, place, :] = q_ref[...] * lanes
        dn[p, place, :] = do_ref[...] * lanes
    dqt[...] = jnp.zeros_like(dqt)

    @pl.when(tile == 0)
    def _():
        dk_sum[...] = jnp.zeros_like(dk_sum)
        dv_sum[...] = jnp.zeros_like(dv_sum)

    def chunk(c, carry):
        rows = pl.ds(pl.multiple_of(start + c * CHUNK, 16), CHUNK)
        keys_t = kg_ref[rows, :HALF].astype(jnp.float32).T.astype(jnp.bfloat16)
        for p in range(PER_HALF // PAIR):
            weights = jnp.exp(jnp.dot(kg_ref[rows, :], qt[p], preferred_element_type=jnp.float32))
            dweights = jnp.dot(vg_ref[rows, :], dt[p], preferred_element_type=jnp.float32)
            place = slice(p * PAIR * TILE, (p + 1) * PAIR * TILE)
            some[:, place] = weights.astype(jnp.bfloat16)
            slopes[:, place] = (weights * dweights).astype(jnp.bfloat16)
        depth = PER_HALF * TILE
        dk = jnp.dot(slopes[...], qn[...].reshape(depth, HALF), preferred_element_type=jnp.float32)
        dv = jnp.dot(some[...], dn[...].reshape(depth, HALF), preferred_element_type=jnp.float32)
        for p in range(PER_HALF // PAIR):
            own = slice(p * PAIR * HEAD_SIZE, (p + 1) * PAIR * HEAD_SIZE)
            place = slice(p * PAIR * TILE, (p + 1) * PAIR * TILE)
            dqt[own, :] += jnp.dot(keys_t[own], slopes[:, place], preferred_element_type=jnp.float32)
        dk_sum[rows, :] += dk
        dv_sum[rows, :] += dv
        return carry

    lax.fori_loop(0, count, chunk, 0)
    parts = []
    for h in range(PER_HALF):
        place = slice(h % PAIR * TILE, (h % PAIR + 1) * TILE)
        parts.append(dqt[h * HEAD_SIZE : (h + 1) * HEAD_SIZE, place])
    dq_ref[...] = jnp.concatenate(parts, axis=0).T.astype(jnp.bfloat16)

    @pl.when(tile == TILES - 1)
    def _():
        dk_ref[...] = (dk_sum[:WINDOW] * 4.0).astype(jnp.bfloat16)
        dv_ref[...] = (dv_sum[:WINDOW] * 4.0).astype(jnp.bfloat16)


def attend_back(spans, queries, queries_t, logs, douts, douts_t, deltas, keys_g, values_g):
    tall = pl.BlockSpec((None, TALL, 2 * HALF), lambda g, t: (g, 0, 0))
    mine = pl.BlockSpec((TILE, HALF), lambda g, t: (t, g))
    turned = pl.BlockSpec((HALF, TILE), lambda g, t: (g, t))
    sums = pl.BlockSpec((WINDOW, HALF), lambda g, t: (0, g))
    half = jnp.bfloat16
    return pl.pallas_call(
        backward_kernel,
        grid=(2, TILES),
        out_shape=[
            jax.ShapeDtypeStruct((PATCH, 256), half),
            jax.ShapeDtypeStruct((WINDOW, 256), half),
            jax.ShapeDtypeStruct((WINDOW, 256), half),
        ],
        in_specs=[pl.BlockSpec(memory_space=pltpu.SMEM)]
        + [mine, turned, turned, mine, turned, turned, tall, tall],
        out_specs=[mine, sums, sums],
        scratch_shapes=[
            pltpu.VMEM((PER_HALF // PAIR, 2 * HALF, PAIR * TILE), half),
            pltpu.VMEM((PER_HALF // PAIR, 2 * HALF, PAIR * TILE), half),
            pltpu.VMEM((PER_HALF // PAIR, PAIR * TILE, HALF), half),
            pltpu.VMEM((PER_HALF // PAIR, PAIR * TILE, HALF), half),
            pltpu.VMEM((CHUNK, 256 * PER_HALF // PAIR), half),
            pltpu.VMEM((CHUNK, 256 * PER_HALF // PAIR), half),
            pltpu.VMEM((HALF, PAIR * TILE), jnp.float32),
            pltpu.VMEM((TALL, HALF), jnp.float32),
            pltpu.VMEM((TALL, HALF), jnp.float32),
        ],
        compiler_params=pltpu.CompilerParams(vmem_limit_bytes=40 * 1024 * 1024),
        name="attention_back",
    )(spans, queries, queries_t, logs, douts, douts_t, deltas, keys_g, values_g)


UNIT = 128
EXTRA = 16
CORE_ROWS = 12 * UNIT
X_ROWS = CORE_ROWS // 4
Y_ROWS = X_ROWS // 8


def axes():
    me = lax.axis_index("pts")
    core, z, y, x = me % 2, (me // 2) % 8, (me // 16) % 8, me // 128
    return (
        (core, 2, lambda r: x * 128 + y * 16 + z * 2 + r),
        (x, 4, lambda r: r * 128 + y * 16 + z * 2 + core),
        (y, 8, lambda r: x * 128 + r * 16 + z * 2 + core),
        (z, 8, lambda r: x * 128 + y * 16 + r * 2 + core),
    )


def swap(axis, source, landing, sems, first):
    rank, size, device = axis
    copies = []
    for k in range(1, size):
        peer = (rank + k) % size
        copies.append(send(source(peer), landing(rank), sems, first + k - 1, device(peer)))
    return copies


def wait_all(copies):
    for copy in copies:
        copy.wait()


def slot_sum(ref, start, size):
    total = ref[0, start : start + size, :].astype(jnp.float32)
    for r in range(1, ref.shape[0]):
        total = total + ref[r, start : start + size, :].astype(jnp.float32)
    return total


def finish_kernel(
    scale, hidden, dq, dk, dv, dmixed, points, gain, w_qkv, gw_out, gw_pool, gb_pool, g_gain,
    grad_points, reduced, extras,
    low_k, low_v, high_k, high_v, send_c, recv_c, send_x, recv_x, send_y, recv_y, recv_z,
    gather_y, gather_x, gather_c, sems,
):
    me, before, after = neighbours()
    on_core, on_x, on_y, on_z = axes()
    barrier = pltpu.get_barrier_semaphore()
    greeted = [before, after]
    for rank, size, device in (on_core, on_x, on_y, on_z):
        greeted += [device((rank + k) % size) for k in range(1, size)]
    for device in greeted:
        pl.semaphore_signal(barrier, inc=1, device_id=(device,), device_id_type=MESH)

    def fill(block, first_unit):
        for column in range(block.shape[1] // UNIT):
            unit = first_unit + 2 * column
            start = unit % 12 * UNIT
            send_c[unit // 12, start : start + 2 * UNIT, :] = block[:, column * UNIT : (column + 1) * UNIT]

    fill(gw_out[...], 12)
    fill(gw_pool[...], 16)
    pieces = [gb_pool[:, i * UNIT : (i + 1) * UNIT] for i in range(4)]
    pieces += [g_gain[:, i * UNIT : (i + 1) * UNIT] for i in range(4)]
    pieces += [jnp.zeros((EXTRA - 8, UNIT), jnp.float32)]
    packed = jnp.concatenate(pieces, axis=0).astype(jnp.bfloat16)
    for r in range(2):
        send_c[r, CORE_ROWS:, :] = packed
    own = slice(PATCH, 2 * PATCH)
    fill((inner_rows(hidden[own, :], dq[...]) * scale).astype(jnp.bfloat16), 0)
    fill((inner_rows(hidden[...], dk[...]) * scale).astype(jnp.bfloat16), 4)
    fill((inner_rows(hidden[...], dv[...]) * scale).astype(jnp.bfloat16), 8)

    pl.semaphore_wait(barrier, len(greeted))
    copies = swap(on_core, lambda r: send_c.at[r], lambda r: recv_c, sems, 0)
    rims = [
        send(dk.at[pl.ds(0, PATCH)], high_k, sems, 40, before),
        send(dv.at[pl.ds(0, PATCH)], high_v, sems, 41, before),
        send(dk.at[pl.ds(2 * PATCH, PATCH)], low_k, sems, 42, after),
        send(dv.at[pl.ds(2 * PATCH, PATCH)], low_v, sems, 43, after),
    ]
    dhidden = against_rows(dq[...], w_qkv[:, :256])
    wait_all(copies)
    kept = send_c.at[on_core[0]]
    extra = (
        kept[CORE_ROWS:, :].astype(jnp.float32) + recv_c[CORE_ROWS:, :].astype(jnp.float32)
    ).astype(jnp.bfloat16)
    for r in range(4):
        rows = slice(r * X_ROWS, (r + 1) * X_ROWS)
        total = kept[rows, :].astype(jnp.float32) + recv_c[rows, :].astype(jnp.float32)
        send_x[r, :X_ROWS, :] = total.astype(jnp.bfloat16)
        send_x[r, X_ROWS:, :] = extra

    copies = swap(on_x, lambda r: send_x.at[r], lambda r: recv_x.at[r], sems, 1)
    recv_x[on_x[0]] = send_x[on_x[0]]
    wait_all(rims)
    for columns, mine, low, high in (
        (slice(256, 512), dk, low_k, high_k), (slice(512, 768), dv, low_v, high_v)
    ):
        total = mine[own, :].astype(jnp.float32) + low[...].astype(jnp.float32)
        total = (total + high[...].astype(jnp.float32)).astype(jnp.bfloat16)
        dhidden = dhidden + against_rows(total, w_qkv[:, columns])
    normed, inv_std = layer_stats(points[...].astype(jnp.float32))
    grad_points[...] = dmixed[...] + norm_back(dhidden * gain[...], normed, inv_std)
    wait_all(copies)
    extra = slot_sum(recv_x, X_ROWS, EXTRA).astype(jnp.bfloat16)
    for r in range(8):
        send_y[r, :Y_ROWS, :] = slot_sum(recv_x, r * Y_ROWS, Y_ROWS).astype(jnp.bfloat16)
        send_y[r, Y_ROWS:, :] = extra

    copies = swap(on_y, lambda r: send_y.at[r], lambda r: recv_y.at[r], sems, 4)
    recv_y[on_y[0]] = send_y[on_y[0]]
    wait_all(copies)
    recv_z[on_z[0]] = slot_sum(recv_y, 0, Y_ROWS + EXTRA).astype(jnp.bfloat16)

    wait_all(swap(on_z, lambda r: recv_z.at[on_z[0]], lambda r: recv_z.at[r], sems, 11))
    total = slot_sum(recv_z, 0, Y_ROWS + EXTRA)
    extras[...] = total[Y_ROWS:]
    gather_y[on_y[0]] = total[:Y_ROWS].astype(jnp.bfloat16)
    wait_all(swap(on_y, lambda r: gather_y.at[on_y[0]], lambda r: gather_y.at[r], sems, 18))
    gather_x[on_x[0]] = gather_y[...]
    copies = swap(on_x, lambda r: gather_y, lambda r: gather_x.at[r], sems, 25)
    wait_all(copies)
    gather_c[on_core[0]] = gather_x[...]
    wait_all(swap(on_core, lambda r: gather_x, lambda r: gather_c.at[r], sems, 28))
    for c in range(2):
        for r in range(4):
            for s in range(8):
                start = c * CORE_ROWS + r * X_ROWS + s * Y_ROWS
                reduced[start : start + Y_ROWS, :] = gather_c[c, r, s]
    weighted = jnp.zeros((256, UNIT), jnp.float32)
    for column in range(6):
        block = reduced[column * 256 : (column + 1) * 256, :].astype(jnp.float32)
        lanes = slice(column * UNIT, (column + 1) * UNIT)
        weighted = weighted + block * w_qkv[:, lanes].astype(jnp.float32)
    summed_gain = jnp.sum(weighted.T, axis=0, keepdims=True) / gain[...]
    for i in range(2):
        extras[8 + i : 9 + i, :] = summed_gain[:, i * UNIT : (i + 1) * UNIT]


def finish(scale, *arrays):
    half = jnp.bfloat16
    vmem = pl.BlockSpec(memory_space=pltpu.VMEM)
    return pl.pallas_call(
        functools.partial(finish_kernel, scale),
        out_shape=[
            jax.ShapeDtypeStruct((PATCH, 256), jnp.float32),
            jax.ShapeDtypeStruct((2 * CORE_ROWS, UNIT), half),
            jax.ShapeDtypeStruct((EXTRA, UNIT), jnp.float32),
        ],
        in_specs=[vmem] * 12,
        out_specs=[vmem] * 3,
        scratch_shapes=[pltpu.VMEM((PATCH, 256), half)] * 4
        + [
            pltpu.VMEM((2, CORE_ROWS + EXTRA, UNIT), half),
            pltpu.VMEM((CORE_ROWS + EXTRA, UNIT), half),
            pltpu.VMEM((4, X_ROWS + EXTRA, UNIT), half),
            pltpu.VMEM((4, X_ROWS + EXTRA, UNIT), half),
            pltpu.VMEM((8, Y_ROWS + EXTRA, UNIT), half),
            pltpu.VMEM((8, Y_ROWS + EXTRA, UNIT), half),
            pltpu.VMEM((8, Y_ROWS + EXTRA, UNIT), half),
            pltpu.VMEM((8, Y_ROWS, UNIT), half),
            pltpu.VMEM((4, 8, Y_ROWS, UNIT), half),
            pltpu.VMEM((2, 4, 8, Y_ROWS, UNIT), half),
            pltpu.SemaphoreType.DMA((2, 44)),
        ],
        compiler_params=pltpu.CompilerParams(
            collective_id=3, has_side_effects=True, vmem_limit_bytes=40 * 1024 * 1024
        ),
        name="finish",
    )(*arrays)


def unpack_kernel(reduced, extras, rows_in, gq, go, gn, gp, gb, gg, rows_out, sem):
    copy = pltpu.make_async_copy(rows_in, rows_out, sem)
    copy.start()
    for column in range(12):
        block = reduced[column * 256 : (column + 1) * 256, :].astype(jnp.float32)
        if column < 6:
            gq[:, column * UNIT : (column + 1) * UNIT] = block
        elif column < 8:
            go[:, (column - 6) * UNIT : (column - 5) * UNIT] = block
        else:
            gp[:, (column - 8) * UNIT : (column - 7) * UNIT] = block
    for i in range(2):
        gn[:, i * UNIT : (i + 1) * UNIT] = extras[8 + i : 9 + i, :]
    for i in range(4):
        gb[:, i * UNIT : (i + 1) * UNIT] = extras[i : i + 1, :]
        gg[:, i * UNIT : (i + 1) * UNIT] = extras[4 + i : 5 + i, :]
    copy.wait()


def unpack(reduced, extras, rows):
    vmem = pl.BlockSpec(memory_space=pltpu.VMEM)
    outside = pl.BlockSpec(memory_space=pl.ANY)
    shapes = ((256, 768), (256, 256), (1, 256), (256, 512), (1, 512), (1, 512), (PATCH, 256))
    return pl.pallas_call(
        unpack_kernel,
        out_shape=[jax.ShapeDtypeStruct(shape, jnp.float32) for shape in shapes],
        in_specs=[vmem, vmem, vmem],
        out_specs=[vmem] * 6 + [outside],
        scratch_shapes=[pltpu.SemaphoreType.DMA],
        compiler_params=pltpu.CompilerParams(vmem_limit_bytes=16 * 1024 * 1024),
        name="unpack",
    )(reduced, extras, rows)


def body(
    points, patch_ids, cell_ids, norm_gain, w_qkv, w_out, w_pool, b_pool, pool_gain, cotangent
):
    scale = 1.0 / math.sqrt(points.shape[0] * lax.axis_size("pts"))
    gain = norm_gain[None]
    cells = cell_ids.reshape(4, HALF)
    far = [
        pltpu.with_memory_space_constraint(array, pltpu.HBM)
        for array in (points, patch_ids.reshape(4, HALF), gain, w_qkv, w_out, cells)
    ]
    queries, queries_t, keys_g, values_g, marks_f, hidden, spans = prepare(*far[:4])
    attended, logs, sums, counts = attend(
        spans, queries_t, marks_f, keys_g, values_g, far[0], far[4], far[5]
    )
    dmixed, datt, datt_t, deltas, gw_pool, gw_out, gb_pool, g_gain = pool(
        scale, sums, counts, cells, attended, w_out, w_pool, b_pool[None], pool_gain[None], cotangent
    )
    dq, dk, dv = attend_back(
        spans, queries, queries_t, logs, datt, datt_t, deltas, keys_g, values_g
    )
    grad_points, reduced, extras = finish(
        scale, hidden, dq, dk, dv, dmixed, points, gain, w_qkv, gw_out, gw_pool, gb_pool, g_gain
    )
    gq, go, gn, gp, gb, gg, grad_points = unpack(reduced, extras, grad_points)
    return (grad_points, gq, go, gn[0], gp, gb[0], gg[0])


def solution(mesh):
    in_specs = (P("pts", None), P("pts"), P("pts"), P(), P(), P(), P(), P(), P(), P("pts", None))
    out_specs = (P("pts", None), P(), P(), P(), P(), P(), P())
    return jax.shard_map(body, mesh=mesh, in_specs=in_specs, out_specs=out_specs, check_vma=False)
```

```python
import functools
import math

import jax
import jax.numpy as jnp
from jax import lax
from jax.experimental import pallas as pl
from jax.experimental.pallas import tpu as pltpu
from jax.sharding import PartitionSpec as P

PATCH = 512
MESH = pl.DeviceIdType.MESH


EPS = 1e-05
ROOT_HALF = 0.7071067811865476
ROOT_TWO_PI = 2.5066282746310002


def layer_stats(values):
    centered = values - jnp.mean(values, axis=-1, keepdims=True)
    inv_std = lax.rsqrt(jnp.mean(centered * centered, axis=-1, keepdims=True) + EPS)
    return (centered * inv_std, inv_std)


def norm_back(grad_normed, normed, inv_std):
    first_mean = jnp.mean(grad_normed, axis=-1, keepdims=True)
    second_mean = jnp.mean(grad_normed * normed, axis=-1, keepdims=True)
    return inv_std * (grad_normed - first_mean - normed * second_mean)


def gelu_slope(scaled):
    normal_cdf = 0.5 * (1.0 + lax.erf(scaled * ROOT_HALF))
    return normal_cdf + scaled * jnp.exp(-0.5 * scaled * scaled) / ROOT_TWO_PI


def inner_rows(left, right):
    return lax.dot_general(
        left, right, (((0,), (0,)), ((), ())), preferred_element_type=jnp.float32
    )


def against_rows(left, right):
    return lax.dot_general(
        left, right, (((1,), (1,)), ((), ())), preferred_element_type=jnp.float32
    )


HALF = 128
PER_HALF = 8
HEAD_SIZE = 16
TILE = 128
CHUNK = 528
TALL = 3 * CHUNK
TILES = PATCH // TILE
PAIR = 256 // TILE
WINDOW = 3 * PATCH
FAR = float(2**30)
DIGIT = 32
LOG_LANE = 64


def head_mask(h, axis):
    shape = (1, 2 * HALF) if axis else (2 * HALF, 1)
    place = lax.broadcasted_iota(jnp.int32, shape, axis)
    own = (place >= h * HEAD_SIZE) & (place < (h + 1) * HEAD_SIZE)
    marks = (place >= HALF) & (place < HALF + LOG_LANE)
    terms = (place >= HALF + LOG_LANE) & (place < HALF + LOG_LANE + 24) & (place % PER_HALF == h)
    return (own | marks | terms).astype(jnp.float32).astype(jnp.bfloat16)


def split_three(values, which):
    first = values.astype(jnp.bfloat16).astype(jnp.float32)
    second = (values - first).astype(jnp.bfloat16).astype(jnp.float32)
    third = values - first - second
    return jnp.where(which == 0, first, jnp.where(which == 1, second, third))


def neighbours():
    me = lax.axis_index("pts")
    count = lax.axis_size("pts")
    return me, (me + count - 1) % count, (me + 1) % count


def greet_neighbours(before, after):
    barrier = pltpu.get_barrier_semaphore()
    for device in (before, after):
        pl.semaphore_signal(barrier, inc=1, device_id=(device,), device_id_type=MESH)
    pl.semaphore_wait(barrier, 2)


def send(source, landing, sems, index, device):
    copy = pltpu.make_async_remote_copy(
        src_ref=source,
        dst_ref=landing,
        send_sem=sems.at[0, index],
        recv_sem=sems.at[1, index],
        device_id=(device,),
        device_id_type=MESH,
    )
    copy.start()
    return copy


def digit_columns(marks):
    row = lax.broadcasted_iota(jnp.int32, (HALF, HALF), 0)
    high, low = marks // DIGIT, marks % DIGIT
    hit = ((row < DIGIT) & (row == high)) | ((row >= DIGIT) & (row < LOG_LANE) & (row - DIGIT == low))
    return hit.astype(jnp.float32)


def prepare_kernel(
    points_hbm, ids_hbm, gain_hbm, w_hbm, q_ref, qt_ref, kg_ref, vg_ref, f_ref, hidden_ref, spans_ref,
    points, ids, gain, w_qkv, marks, marks_low, marks_high, rows_low, rows_high, sems, local_sems,
):
    me, before, after = neighbours()
    local = []
    for i, (source, target) in enumerate(
        ((ids_hbm, ids), (points_hbm, points), (w_hbm, w_qkv), (gain_hbm, gain))
    ):
        local.append(pltpu.make_async_copy(source, target, local_sems.at[i]))
        local[-1].start()
    marks[...] = jnp.zeros_like(marks)
    greet_neighbours(before, after)
    local[0].wait()
    marks[:4, :] = ids[...] + 1
    local[1].wait()
    copies = [
        send(points, rows_high, sems, 0, before),
        send(points, rows_low, sems, 1, after),
        send(marks, marks_high, sems, 2, before),
        send(marks, marks_low, sems, 3, after),
    ]
    local[2].wait()
    local[3].wait()

    def project(block, first, columns):
        normed, _ = layer_stats(block[...].astype(jnp.float32))
        hidden = (normed * gain[...]).astype(jnp.bfloat16)
        hidden_ref[first : first + PATCH, :] = hidden
        return jnp.dot(hidden, w_qkv[:, columns], preferred_element_type=jnp.float32)

    def place(first, keys, values):
        for g in range(2):
            lanes = slice(g * HALF, (g + 1) * HALF)
            kg_ref[g, first : first + PATCH, :HALF] = keys[:, lanes].astype(jnp.bfloat16)
            vg_ref[g, first : first + PATCH, :HALF] = values[:, lanes].astype(jnp.bfloat16)

    def place_marks(block, first, own):
        lane = lax.broadcasted_iota(jnp.int32, (HALF, HALF), 1)
        row = lax.broadcasted_iota(jnp.int32, (HALF, HALF), 0)
        terms = (lane >= LOG_LANE) & (lane < LOG_LANE + 24)
        for i in range(4):
            rows = slice(first + i * HALF, first + (i + 1) * HALF)
            digits = digit_columns(block[i : i + 1, :])
            both = jnp.where(terms, 1.0, digits.T).astype(jnp.bfloat16)
            for g in range(2):
                kg_ref[g, rows, HALF:] = both
                vg_ref[g, rows, HALF:] = both
            if own:
                away = jnp.where(row < LOG_LANE, (1.0 - digits) * -FAR, 0.0)
                f_ref[:, i * HALF : (i + 1) * HALF] = away.astype(jnp.bfloat16)

    qkv = project(points, PATCH, slice(None))
    queries = qkv[:, :256].astype(jnp.bfloat16).astype(jnp.float32) * 0.25
    q_ref[...] = queries.astype(jnp.bfloat16)
    qt_ref[...] = queries.T.astype(jnp.bfloat16)
    place(PATCH, qkv[:, 256:512], qkv[:, 512:])
    own = marks[...]
    place_marks(own, PATCH, True)
    lane = lax.broadcasted_iota(jnp.int32, (TALL - WINDOW, 2 * HALF), 1)
    nowhere = ((lane == HALF) | (lane == HALF + DIGIT)).astype(jnp.float32).astype(jnp.bfloat16)
    for g in range(2):
        kg_ref[g, WINDOW:, :] = nowhere
        vg_ref[g, WINDOW:, :] = nowhere
    for copy in copies[2:]:
        copy.wait()
    low = jnp.where(me == 0, 0, marks_low[...])
    high = jnp.where(me == lax.axis_size("pts") - 1, 0, marks_high[...])
    place_marks(low, 0, False)
    place_marks(high, 2 * PATCH, False)
    own_f, low_f, high_f = (block[:4].astype(jnp.float32) for block in (own, low, high))
    for t in range(TILES):
        ours = own_f[t * TILE // HALF : (t + 1) * TILE // HALF]
        first, last = jnp.min(ours), jnp.max(ours)
        lower = jnp.sum((low_f < first).astype(jnp.float32) + (own_f < first).astype(jnp.float32))
        upper = jnp.sum(
            ((high_f > 0) & (high_f <= last)).astype(jnp.float32) + (own_f <= last).astype(jnp.float32)
        )
        lower = lower.astype(jnp.int32) // 16 * 16
        count = (PATCH + upper.astype(jnp.int32) - lower + CHUNK - 1) // CHUNK
        spans_ref[t, 0] = jnp.minimum(lower, TALL - count * CHUNK)
        spans_ref[t, 1] = count
    for copy, block, first in ((copies[1], rows_low, 0), (copies[0], rows_high, 2 * PATCH)):
        copy.wait()
        kv = project(block, first, slice(256, 768))
        place(first, kv[:, :256], kv[:, 256:])


def prepare(points, ids, gain, w_qkv):
    half = jnp.bfloat16
    vmem = pl.BlockSpec(memory_space=pltpu.VMEM)
    return pl.pallas_call(
        prepare_kernel,
        out_shape=[
            jax.ShapeDtypeStruct((PATCH, 256), half),
            jax.ShapeDtypeStruct((256, PATCH), half),
            jax.ShapeDtypeStruct((2, TALL, 2 * HALF), half),
            jax.ShapeDtypeStruct((2, TALL, 2 * HALF), half),
            jax.ShapeDtypeStruct((HALF, PATCH), half),
            jax.ShapeDtypeStruct((WINDOW, 256), half),
            jax.ShapeDtypeStruct((TILES, 2), jnp.int32),
        ],
        in_specs=[pl.BlockSpec(memory_space=pltpu.HBM)] * 4,
        out_specs=[vmem] * 6 + [pl.BlockSpec(memory_space=pltpu.SMEM)],
        scratch_shapes=[
            pltpu.VMEM((PATCH, 256), half),
            pltpu.VMEM((4, HALF), jnp.int32),
            pltpu.VMEM((1, 256), jnp.float32),
            pltpu.VMEM((256, 768), half),
            pltpu.VMEM((8, HALF), jnp.int32),
            pltpu.VMEM((8, HALF), jnp.int32),
            pltpu.VMEM((8, HALF), jnp.int32),
            pltpu.VMEM((PATCH, 256), half),
            pltpu.VMEM((PATCH, 256), half),
            pltpu.SemaphoreType.DMA((2, 4)),
            pltpu.SemaphoreType.DMA((4,)),
        ],
        compiler_params=pltpu.CompilerParams(
            collective_id=1, has_side_effects=True, vmem_limit_bytes=32 * 1024 * 1024
        ),
        name="prepare",
    )(points, ids, gain, w_qkv)


SLOTS = 144


def membership(cells):
    local = cells - lax.axis_index("pts") * HALF
    local = jnp.where(local < 0, HALF, local)
    slot = lax.broadcasted_iota(jnp.int32, (SLOTS, HALF), 0)
    parts = [(slot == local[i : i + 1, :]).astype(jnp.float32) for i in range(4)]
    return jnp.concatenate(parts, axis=1)


def tall_max(scores):
    part = CHUNK // 6
    folded = scores[:part]
    for i in range(1, 6):
        folded = jnp.maximum(folded, scores[i * part : (i + 1) * part])
    return jnp.max(folded, axis=0, keepdims=True)


def block_of(index, size):
    return pl.ds(pl.multiple_of(index * size, size), size)


def forward_kernel(
    spans, qt_ref, f_ref, kg_ref, vg_ref, points_hbm, w_out_hbm, cells_hbm,
    att_ref, logs_ref, sums_ref, counts_ref, qt, kept, att_t, top_t, total_t, points, w_out, cells, sems,
):
    late = [
        pltpu.make_async_copy(source, target, sems.at[i])
        for i, (source, target) in enumerate(
            ((points_hbm, points), (w_out_hbm, w_out), (cells_hbm, cells))
        )
    ]
    for copy in late:
        copy.start()
    qt[...] = jnp.zeros_like(qt)

    def step(index, carry):
        forward_step(
            index // 2, index % 2, spans, qt_ref, f_ref, kg_ref, vg_ref, att_ref, logs_ref,
            qt, kept, att_t, top_t, total_t,
        )
        return carry

    lax.fori_loop(0, 2 * TILES, step, 0)
    for copy in late:
        copy.wait()
    mixed = points[...].astype(jnp.float32) + jnp.dot(
        att_ref[...], w_out[...], preferred_element_type=jnp.float32
    )
    member = membership(cells[...])
    sums_ref[...] = jnp.dot(
        member.astype(jnp.bfloat16), mixed.astype(jnp.bfloat16), preferred_element_type=jnp.float32
    )
    counts_ref[...] = jnp.broadcast_to(jnp.sum(member, axis=1, keepdims=True), (SLOTS, HALF))


def forward_step(
    tile, half, spans, qt_ref, f_ref, kg_ref, vg_ref, att_ref, logs_ref, qt, kept, att_t, top_t, total_t
):
    start, count = spans[tile, 0], spans[tile, 1]
    mine, turned = block_of(tile, TILE), block_of(half, HALF)
    queries_t, marks = qt_ref[turned, mine], f_ref[:LOG_LANE, mine]
    for h in range(PER_HALF):
        place = slice(h % PAIR * TILE, (h % PAIR + 1) * TILE)
        own = slice(h * HEAD_SIZE, (h + 1) * HEAD_SIZE)
        qt[h // PAIR, own, place] = queries_t[own]
        qt[h // PAIR, HALF : HALF + LOG_LANE, place] = marks
    top_t[...] = jnp.full_like(top_t, -3e38)
    total_t[...] = jnp.zeros_like(total_t)
    att_t[...] = jnp.zeros_like(att_t)

    def chunk(c, carry):
        rows = pl.ds(pl.multiple_of(start + c * CHUNK, 16), CHUNK)
        values_t = vg_ref[half, rows, :HALF].astype(jnp.float32).T.astype(jnp.bfloat16)
        ones = jnp.ones((16, CHUNK), jnp.bfloat16)
        tops = []
        for p in range(PER_HALF // PAIR):
            scores = jnp.dot(kg_ref[half, rows, :], qt[p], preferred_element_type=jnp.float32)
            kept[p] = scores
            tops.append(jnp.maximum(top_t[p : p + 1, :], tall_max(scores)))
        for p in range(PER_HALF // PAIR):
            before, top = top_t[p : p + 1, :], tops[p]
            weights = jnp.exp(kept[p] - top).astype(jnp.bfloat16)
            decay = jnp.exp(before - top)
            top_t[p : p + 1, :] = top
            own = slice(p * PAIR * HEAD_SIZE, (p + 1) * PAIR * HEAD_SIZE)
            left = jnp.concatenate([values_t[own], ones], axis=0)
            mixed = jnp.dot(left, weights, preferred_element_type=jnp.float32)
            count_rows = PAIR * HEAD_SIZE
            total_t[p : p + 1, :] = total_t[p : p + 1, :] * decay + mixed[count_rows : count_rows + 1]
            att_t[own, :] = att_t[own, :] * decay + mixed[:count_rows]
        return carry

    lax.fori_loop(0, count, chunk, 0)
    logs_p = -(top_t[...] + jnp.log(total_t[...]))
    parts, logs = [], []
    for h in range(PER_HALF):
        p, columns = h // PAIR, slice(h % PAIR * TILE, (h % PAIR + 1) * TILE)
        piece = att_t[h * HEAD_SIZE : (h + 1) * HEAD_SIZE, columns]
        parts.append(piece / total_t[p : p + 1, columns])
        logs.append(logs_p[p : p + 1, columns])
    attended = jnp.concatenate(parts, axis=0).T.astype(jnp.bfloat16)
    att_ref[mine, turned] = attended
    logs = jnp.concatenate(logs, axis=0)
    terms = [split_three(logs, i) for i in range(3)]
    spare = jnp.zeros((HALF - LOG_LANE - 24, TILE), jnp.float32)
    ending = jnp.concatenate(terms + [spare], axis=0).astype(jnp.bfloat16)
    logs_ref[turned, mine] = jnp.concatenate([marks, ending], axis=0)


def attend(spans, queries_t, marks_f, keys_g, values_g, points, w_out, cells):
    vmem = pl.BlockSpec(memory_space=pltpu.VMEM)
    outside = pl.BlockSpec(memory_space=pltpu.HBM)
    return pl.pallas_call(
        forward_kernel,
        out_shape=[
            jax.ShapeDtypeStruct((PATCH, 256), jnp.bfloat16),
            jax.ShapeDtypeStruct((256, PATCH), jnp.bfloat16),
            jax.ShapeDtypeStruct((SLOTS, 256), jnp.float32),
            jax.ShapeDtypeStruct((SLOTS, HALF), jnp.float32),
        ],
        in_specs=[pl.BlockSpec(memory_space=pltpu.SMEM)] + [vmem] * 4 + [outside] * 3,
        out_specs=[vmem] * 4,
        scratch_shapes=[
            pltpu.VMEM((PER_HALF // PAIR, 2 * HALF, PAIR * TILE), jnp.bfloat16),
            pltpu.VMEM((PER_HALF // PAIR, CHUNK, PAIR * TILE), jnp.float32),
            pltpu.VMEM((HALF, PAIR * TILE), jnp.float32),
            pltpu.VMEM((PER_HALF // PAIR, PAIR * TILE), jnp.float32),
            pltpu.VMEM((PER_HALF // PAIR, PAIR * TILE), jnp.float32),
            pltpu.VMEM((PATCH, 256), jnp.bfloat16),
            pltpu.VMEM((256, 256), jnp.bfloat16),
            pltpu.VMEM((4, HALF), jnp.int32),
            pltpu.SemaphoreType.DMA((3,)),
        ],
        compiler_params=pltpu.CompilerParams(vmem_limit_bytes=24 * 1024 * 1024),
        name="attention",
    )(spans, queries_t, marks_f, keys_g, values_g, points, w_out, cells)


def pool_kernel(
    scale, sums, counts, cells, att, w_out, w_pool, b_pool, pool_gain, cotangent,
    dmixed_ref, datt_ref, datt_t_ref, delta_ref, gw_pool, gw_out, gb_pool, g_gain,
    back_pack, ahead_pack, from_after, from_before, sems,
):
    me, before, after = neighbours()
    back_pack[:, :256] = sums[HALF : HALF + 8, :]
    back_pack[:, 256:] = counts[HALF : HALF + 8, :]
    ahead_pack[:, :256] = sums[HALF - 8 : HALF, :]
    ahead_pack[:, 256:384] = counts[HALF - 8 : HALF, :]
    ahead_pack[:, 384:] = cotangent[HALF - 8 :, :]
    greet_neighbours(before, after)
    copies = [
        send(back_pack, from_after, sems, 0, before),
        send(ahead_pack, from_before, sems, 1, after),
    ]
    member = membership(cells[...]).astype(jnp.bfloat16)
    for copy in copies:
        copy.wait()
    row = lax.broadcasted_iota(jnp.int32, (8, 1), 0)
    late, early = from_after[0:1, :], from_before[7:8, :]
    last_sum = sums[HALF - 8 : HALF, :] + jnp.where(row == 7, late[:, :256], 0.0)
    lead_sum = jnp.where(row == 0, sums[HALF : HALF + 8, :] + early[:, :256], 0.0)
    last_count = counts[HALF - 8 : HALF, :] + jnp.where(row == 7, late[:, 256:], 0.0)
    lead_count = jnp.where(row == 0, counts[HALF : HALF + 8, :] + early[:, 256:384], 0.0)
    spare = jnp.zeros((8, 256), jnp.float32)
    all_sums = jnp.concatenate([sums[: HALF - 8, :], last_sum, lead_sum, spare], axis=0)
    all_counts = jnp.concatenate(
        [counts[: HALF - 8, :], last_count, lead_count, spare[:, :HALF]], axis=0
    )[:, :1]
    all_counts = jnp.maximum(all_counts, 1.0)
    lead_cot = jnp.where(row == 0, early[:, 384:], 0.0)
    all_cot = jnp.concatenate([cotangent[...], lead_cot, jnp.zeros((8, 512), jnp.float32)], axis=0)

    pooled_mean = (all_sums / all_counts).astype(jnp.bfloat16)
    pre_norm = jnp.dot(pooled_mean, w_pool[...], preferred_element_type=jnp.float32) + b_pool[...]
    pooled_normed, pooled_inv = layer_stats(pre_norm)
    slope_grad = all_cot * gelu_slope(pooled_normed * pool_gain[...])
    grad_pre = norm_back(slope_grad * pool_gain[...], pooled_normed, pooled_inv)
    grad_pre_b = grad_pre.astype(jnp.bfloat16)
    share = against_rows(grad_pre_b, w_pool[...]) / all_counts
    share_b = share.astype(jnp.bfloat16)
    rest_b = (share - share_b.astype(jnp.float32)).astype(jnp.bfloat16)
    dmixed_main = inner_rows(member, share_b)
    dmixed_ref[...] = dmixed_main + inner_rows(member, rest_b)
    dmixed_b = dmixed_main.astype(jnp.bfloat16)
    datt = against_rows(dmixed_b, w_out[...]).astype(jnp.bfloat16)
    datt_f = datt.astype(jnp.float32)
    datt_ref[...] = (datt_f * 0.25).astype(jnp.bfloat16)
    product = datt_f * att[...].astype(jnp.float32)
    datt_t = against_rows(w_out[...], dmixed_b).astype(jnp.bfloat16).astype(jnp.float32)
    datt_t_ref[...] = (datt_t * 0.25).astype(jnp.bfloat16)
    slot = lax.broadcasted_iota(jnp.int32, (256, 256), 0)
    channel = lax.broadcasted_iota(jnp.int32, (256, 256), 1)
    spot = slot % HALF - LOG_LANE
    place = (channel // HALF == slot // HALF) & (spot >= 0) & (spot < 24)
    place = (place & (spot % PER_HALF == channel % HALF // HEAD_SIZE)).astype(jnp.float32)
    place = place.astype(jnp.bfloat16)
    first = product.astype(jnp.bfloat16)
    second = product - first.astype(jnp.float32)
    second_b = second.astype(jnp.bfloat16)
    third_b = (second - second_b.astype(jnp.float32)).astype(jnp.bfloat16)
    deltas = against_rows(place, first) + against_rows(place, second_b) + against_rows(place, third_b)
    which = (lax.broadcasted_iota(jnp.int32, (256, 1), 0) % HALF - LOG_LANE) // PER_HALF
    delta_ref[...] = split_three(deltas * -0.25, which).astype(jnp.bfloat16)
    gw_pool[...] = (inner_rows(pooled_mean[:HALF], grad_pre_b[:HALF]) * scale).astype(jnp.bfloat16)
    gw_out[...] = (inner_rows(att[...], dmixed_b) * scale).astype(jnp.bfloat16)
    gb_pool[...] = jnp.sum(grad_pre[:HALF], axis=0, keepdims=True) * scale
    g_gain[...] = jnp.sum(slope_grad[:HALF] * pooled_normed[:HALF], axis=0, keepdims=True) * scale


def pool(scale, *arrays):
    half = jnp.bfloat16
    vmem = pl.BlockSpec(memory_space=pltpu.VMEM)
    return pl.pallas_call(
        functools.partial(pool_kernel, scale),
        out_shape=[
            jax.ShapeDtypeStruct((PATCH, 256), jnp.float32),
            jax.ShapeDtypeStruct((PATCH, 256), half),
            jax.ShapeDtypeStruct((256, PATCH), half),
            jax.ShapeDtypeStruct((256, PATCH), half),
            jax.ShapeDtypeStruct((256, 512), half),
            jax.ShapeDtypeStruct((256, 256), half),
            jax.ShapeDtypeStruct((1, 512), jnp.float32),
            jax.ShapeDtypeStruct((1, 512), jnp.float32),
        ],
        in_specs=[vmem] * 9,
        out_specs=[vmem] * 8,
        scratch_shapes=[
            pltpu.VMEM((8, 384), jnp.float32),
            pltpu.VMEM((8, 896), jnp.float32),
            pltpu.VMEM((8, 384), jnp.float32),
            pltpu.VMEM((8, 896), jnp.float32),
            pltpu.SemaphoreType.DMA((2, 2)),
        ],
        compiler_params=pltpu.CompilerParams(
            collective_id=2, has_side_effects=True, vmem_limit_bytes=32 * 1024 * 1024
        ),
        name="pooling",
    )(*arrays)


def backward_kernel(
    spans, q_ref, qt_ref, logs_ref, do_ref, dot_ref, deltas_ref, kg_ref, vg_ref,
    dq_ref, dk_ref, dv_ref, qt, dt, qn, dn, some, slopes, dqt, dk_sum, dv_sum,
):
    qt[...] = jnp.zeros_like(qt)
    dt[...] = jnp.zeros_like(dt)

    def step(index, carry):
        tile, half = index % TILES, index // TILES

        @pl.when(tile == 0)
        def _():
            dk_sum[...] = jnp.zeros_like(dk_sum)
            dv_sum[...] = jnp.zeros_like(dv_sum)

        backward_step(
            tile, half, spans, q_ref, qt_ref, logs_ref, do_ref, dot_ref, deltas_ref, kg_ref, vg_ref,
            dq_ref, qt, dt, qn, dn, some, slopes, dqt, dk_sum, dv_sum,
        )

        @pl.when(tile == TILES - 1)
        def _():
            lanes = block_of(half, HALF)
            dk_ref[:, lanes] = (dk_sum[:WINDOW] * 4.0).astype(jnp.bfloat16)
            dv_ref[:, lanes] = (dv_sum[:WINDOW] * 4.0).astype(jnp.bfloat16)

        return carry

    lax.fori_loop(0, 2 * TILES, step, 0)


def backward_step(
    tile, half, spans, q_ref, qt_ref, logs_ref, do_ref, dot_ref, deltas_ref, kg_ref, vg_ref,
    dq_ref, qt, dt, qn, dn, some, slopes, dqt, dk_sum, dv_sum,
):
    start, count = spans[tile, 0], spans[tile, 1]
    mine, turned = block_of(tile, TILE), block_of(half, HALF)
    queries, douts = q_ref[mine, turned], do_ref[mine, turned]
    queries_t, douts_t = qt_ref[turned, mine], dot_ref[turned, mine]
    logs, deltas = logs_ref[turned, mine], deltas_ref[turned, mine]
    after = HALF + LOG_LANE
    for h in range(PER_HALF):
        p, place = h // PAIR, slice(h % PAIR * TILE, (h % PAIR + 1) * TILE)
        own = slice(h * HEAD_SIZE, (h + 1) * HEAD_SIZE)
        terms = head_mask(h, 0)[after : after + 32]
        qt[p, own, place] = queries_t[own]
        qt[p, HALF:after, place] = logs[:LOG_LANE]
        qt[p, after : after + 32, place] = logs[LOG_LANE : LOG_LANE + 32] * terms
        dt[p, own, place] = douts_t[own]
        dt[p, after : after + 32, place] = deltas[LOG_LANE : LOG_LANE + 32] * terms
        lanes = head_mask(h, 1)[:, :HALF]
        qn[p, place, :] = queries * lanes
        dn[p, place, :] = douts * lanes
    dqt[...] = jnp.zeros_like(dqt)

    def chunk(c, carry):
        rows = pl.ds(pl.multiple_of(start + c * CHUNK, 16), CHUNK)
        keys_t = kg_ref[half, rows, :HALF].astype(jnp.float32).T.astype(jnp.bfloat16)
        for p in range(PER_HALF // PAIR):
            weights = jnp.exp(jnp.dot(kg_ref[half, rows, :], qt[p], preferred_element_type=jnp.float32))
            dweights = jnp.dot(vg_ref[half, rows, :], dt[p], preferred_element_type=jnp.float32)
            place = slice(p * PAIR * TILE, (p + 1) * PAIR * TILE)
            some[:, place] = weights.astype(jnp.bfloat16)
            slopes[:, place] = (weights * dweights).astype(jnp.bfloat16)
        depth = PER_HALF * TILE
        dk = jnp.dot(slopes[...], qn[...].reshape(depth, HALF), preferred_element_type=jnp.float32)
        dv = jnp.dot(some[...], dn[...].reshape(depth, HALF), preferred_element_type=jnp.float32)
        for p in range(PER_HALF // PAIR):
            own = slice(p * PAIR * HEAD_SIZE, (p + 1) * PAIR * HEAD_SIZE)
            place = slice(p * PAIR * TILE, (p + 1) * PAIR * TILE)
            dqt[own, :] += jnp.dot(keys_t[own], slopes[:, place], preferred_element_type=jnp.float32)
        dk_sum[rows, :] += dk
        dv_sum[rows, :] += dv
        return carry

    lax.fori_loop(0, count, chunk, 0)
    parts = []
    for h in range(PER_HALF):
        place = slice(h % PAIR * TILE, (h % PAIR + 1) * TILE)
        parts.append(dqt[h * HEAD_SIZE : (h + 1) * HEAD_SIZE, place])
    dq_ref[mine, turned] = jnp.concatenate(parts, axis=0).T.astype(jnp.bfloat16)


def attend_back(spans, queries, queries_t, logs, douts, douts_t, deltas, keys_g, values_g):
    vmem = pl.BlockSpec(memory_space=pltpu.VMEM)
    half = jnp.bfloat16
    return pl.pallas_call(
        backward_kernel,
        out_shape=[
            jax.ShapeDtypeStruct((PATCH, 256), half),
            jax.ShapeDtypeStruct((WINDOW, 256), half),
            jax.ShapeDtypeStruct((WINDOW, 256), half),
        ],
        in_specs=[pl.BlockSpec(memory_space=pltpu.SMEM)] + [vmem] * 8,
        out_specs=[vmem] * 3,
        scratch_shapes=[
            pltpu.VMEM((PER_HALF // PAIR, 2 * HALF, PAIR * TILE), half),
            pltpu.VMEM((PER_HALF // PAIR, 2 * HALF, PAIR * TILE), half),
            pltpu.VMEM((PER_HALF // PAIR, PAIR * TILE, HALF), half),
            pltpu.VMEM((PER_HALF // PAIR, PAIR * TILE, HALF), half),
            pltpu.VMEM((CHUNK, 256 * PER_HALF // PAIR), half),
            pltpu.VMEM((CHUNK, 256 * PER_HALF // PAIR), half),
            pltpu.VMEM((HALF, PAIR * TILE), jnp.float32),
            pltpu.VMEM((TALL, HALF), jnp.float32),
            pltpu.VMEM((TALL, HALF), jnp.float32),
        ],
        compiler_params=pltpu.CompilerParams(vmem_limit_bytes=24 * 1024 * 1024),
        name="attention_back",
    )(spans, queries, queries_t, logs, douts, douts_t, deltas, keys_g, values_g)


UNIT = 128
EXTRA = 16
CORE_ROWS = 12 * UNIT
X_ROWS = CORE_ROWS // 4
Y_ROWS = X_ROWS // 8


def axes():
    me = lax.axis_index("pts")
    core, z, y, x = me % 2, (me // 2) % 8, (me // 16) % 8, me // 128
    return (
        (core, 2, lambda r: x * 128 + y * 16 + z * 2 + r),
        (x, 4, lambda r: r * 128 + y * 16 + z * 2 + core),
        (y, 8, lambda r: x * 128 + r * 16 + z * 2 + core),
        (z, 8, lambda r: x * 128 + y * 16 + r * 2 + core),
    )


def swap(axis, source, landing, sems, first):
    rank, size, device = axis
    copies = []
    for k in range(1, size):
        peer = (rank + k) % size
        copies.append(send(source(peer), landing(rank), sems, first + k - 1, device(peer)))
    return copies


def wait_all(copies):
    for copy in copies:
        copy.wait()


def slot_sum(ref, start, size):
    total = ref[0, start : start + size, :].astype(jnp.float32)
    for r in range(1, ref.shape[0]):
        total = total + ref[r, start : start + size, :].astype(jnp.float32)
    return total


def finish_kernel(
    scale, hidden, dq, dk, dv, dmixed, points, gain, w_qkv, gw_out, gw_pool, gb_pool, g_gain,
    grad_points, reduced, extras,
    low_k, low_v, high_k, high_v, send_c, recv_c, extra_own, extra_in,
    send_x, recv_x, send_y, recv_y, recv_z, gather_c, sems,
):
    me, before, after = neighbours()
    on_core, on_x, on_y, on_z = axes()
    barrier = pltpu.get_barrier_semaphore()
    greeted = [before, after]
    for rank, size, device in (on_core, on_x, on_y, on_z):
        greeted += [device((rank + k) % size) for k in range(1, size)]
    for device in greeted:
        pl.semaphore_signal(barrier, inc=1, device_id=(device,), device_id_type=MESH)

    def fill(block, first_unit):
        for column in range(block.shape[1] // UNIT):
            unit = first_unit + 2 * column
            start = unit % 12 * UNIT
            for part in range(2):
                at = start + part * UNIT
                rows = slice(at % X_ROWS, at % X_ROWS + UNIT)
                send_c[unit // 12, at // X_ROWS, rows, :] = block[
                    part * UNIT : (part + 1) * UNIT, column * UNIT : (column + 1) * UNIT
                ]

    fill(gw_out[...], 12)
    fill(gw_pool[...], 16)
    pieces = [gb_pool[:, i * UNIT : (i + 1) * UNIT] for i in range(4)]
    pieces += [g_gain[:, i * UNIT : (i + 1) * UNIT] for i in range(4)]
    pieces += [jnp.zeros((EXTRA - 8, UNIT), jnp.float32)]
    packed = jnp.concatenate(pieces, axis=0).astype(jnp.bfloat16)
    extra_own[...] = packed
    own = slice(PATCH, 2 * PATCH)
    fill((inner_rows(hidden[own, :], dq[...]) * scale).astype(jnp.bfloat16), 0)
    fill((inner_rows(hidden[...], dk[...]) * scale).astype(jnp.bfloat16), 4)
    fill((inner_rows(hidden[...], dv[...]) * scale).astype(jnp.bfloat16), 8)

    pl.semaphore_wait(barrier, len(greeted))
    core, core_device = on_core[0], on_core[2](1 - on_core[0])
    x, x_device = on_x[0], on_x[2]
    quarters = [(x + k) % 4 for k in (1, 2, 3, 0)]
    extra_copy = send(extra_own, extra_in, sems, 4, core_device)
    core_copies = [
        send(send_c.at[1 - core, q], recv_c.at[q], sems, k, core_device) for k, q in enumerate(quarters)
    ]
    rims = [
        send(dk.at[pl.ds(0, PATCH)], high_k, sems, 60, before),
        send(dv.at[pl.ds(0, PATCH)], high_v, sems, 61, before),
        send(dk.at[pl.ds(2 * PATCH, PATCH)], low_k, sems, 62, after),
        send(dv.at[pl.ds(2 * PATCH, PATCH)], low_v, sems, 63, after),
    ]
    extra_copy.wait()
    extra = (extra_own[...].astype(jnp.float32) + extra_in[...].astype(jnp.float32)).astype(jnp.bfloat16)
    copies = []
    for k, q in enumerate(quarters):
        core_copies[k].wait()
        total = send_c[core, q].astype(jnp.float32) + recv_c[q].astype(jnp.float32)
        if k < 3:
            send_x[q, :X_ROWS, :] = total.astype(jnp.bfloat16)
            send_x[q, X_ROWS:, :] = extra
            copies.append(send(send_x.at[q], recv_x.at[x], sems, 5 + k, x_device(q)))
        else:
            recv_x[x, :X_ROWS, :] = total.astype(jnp.bfloat16)
            recv_x[x, X_ROWS:, :] = extra
    dhidden = against_rows(dq[...], w_qkv[:, :256])
    normed, inv_std = layer_stats(points[...].astype(jnp.float32))
    wait_all(copies)
    extra = slot_sum(recv_x, X_ROWS, EXTRA).astype(jnp.bfloat16)
    for r in range(8):
        send_y[r, :Y_ROWS, :] = slot_sum(recv_x, r * Y_ROWS, Y_ROWS).astype(jnp.bfloat16)
        send_y[r, Y_ROWS:, :] = extra

    copies = swap(on_y, lambda r: send_y.at[r], lambda r: recv_y.at[r], sems, 8)
    recv_y[on_y[0]] = send_y[on_y[0]]
    wait_all(rims)
    for columns, mine, low, high in (
        (slice(256, 512), dk, low_k, high_k), (slice(512, 768), dv, low_v, high_v)
    ):
        total = mine[own, :].astype(jnp.float32) + low[...].astype(jnp.float32)
        total = (total + high[...].astype(jnp.float32)).astype(jnp.bfloat16)
        dhidden = dhidden + against_rows(total, w_qkv[:, columns])
    grad_points[...] = dmixed[...] + norm_back(dhidden * gain[...], normed, inv_std)
    wait_all(copies)
    recv_z[on_z[0]] = slot_sum(recv_y, 0, Y_ROWS + EXTRA).astype(jnp.bfloat16)

    wait_all(swap(on_z, lambda r: recv_z.at[on_z[0]], lambda r: recv_z.at[r], sems, 15))
    total = slot_sum(recv_z, 0, Y_ROWS + EXTRA)
    extras[...] = total[Y_ROWS:]
    y, y_device = on_y[0], on_y[2]
    gather_c[core, x, y] = total[:Y_ROWS].astype(jnp.bfloat16)
    order = (1, 7, 2, 6, 3, 5, 4)

    def pass_on(k):
        piece = gather_c.at[core, x, (y + 8 - k) % 8]
        return [send(piece, piece, sems, 29 + 3 * k + i - 1, x_device((x + i) % 4)) for i in range(1, 4)]

    mine = gather_c.at[core, x, y]
    y_copies = {k: send(mine, mine, sems, 22 + k - 1, y_device((y + k) % 8)) for k in order}
    x_copies = {0: pass_on(0)}
    for k in order:
        y_copies[k].wait()
        x_copies[k] = pass_on(k)
    core_copies = [send(gather_c.at[core, x], gather_c.at[core, x], sems, 53, core_device)]
    for i in range(1, 4):
        for k in (0,) + order:
            x_copies[k][i - 1].wait()
        slot = gather_c.at[core, (x + 4 - i) % 4]
        core_copies.append(send(slot, slot, sems, 53 + i, core_device))
    wait_all(core_copies)
    for c in range(2):
        for r in range(4):
            for s in range(8):
                start = c * CORE_ROWS + r * X_ROWS + s * Y_ROWS
                reduced[start : start + Y_ROWS, :] = gather_c[c, r, s]
    weighted = jnp.zeros((256, UNIT), jnp.float32)
    for column in range(6):
        block = reduced[column * 256 : (column + 1) * 256, :].astype(jnp.float32)
        lanes = slice(column * UNIT, (column + 1) * UNIT)
        weighted = weighted + block * w_qkv[:, lanes].astype(jnp.float32)
    summed_gain = jnp.sum(weighted.T, axis=0, keepdims=True) / gain[...]
    for i in range(2):
        extras[8 + i : 9 + i, :] = summed_gain[:, i * UNIT : (i + 1) * UNIT]


def finish(scale, *arrays):
    half = jnp.bfloat16
    vmem = pl.BlockSpec(memory_space=pltpu.VMEM)
    return pl.pallas_call(
        functools.partial(finish_kernel, scale),
        out_shape=[
            jax.ShapeDtypeStruct((PATCH, 256), jnp.float32),
            jax.ShapeDtypeStruct((2 * CORE_ROWS, UNIT), half),
            jax.ShapeDtypeStruct((EXTRA, UNIT), jnp.float32),
        ],
        in_specs=[vmem] * 12,
        out_specs=[vmem] * 3,
        scratch_shapes=[pltpu.VMEM((PATCH, 256), half)] * 4
        + [
            pltpu.VMEM((2, 4, X_ROWS, UNIT), half),
            pltpu.VMEM((4, X_ROWS, UNIT), half),
            pltpu.VMEM((EXTRA, UNIT), half),
            pltpu.VMEM((EXTRA, UNIT), half),
            pltpu.VMEM((4, X_ROWS + EXTRA, UNIT), half),
            pltpu.VMEM((4, X_ROWS + EXTRA, UNIT), half),
            pltpu.VMEM((8, Y_ROWS + EXTRA, UNIT), half),
            pltpu.VMEM((8, Y_ROWS + EXTRA, UNIT), half),
            pltpu.VMEM((8, Y_ROWS + EXTRA, UNIT), half),
            pltpu.VMEM((2, 4, 8, Y_ROWS, UNIT), half),
            pltpu.SemaphoreType.DMA((2, 64)),
        ],
        compiler_params=pltpu.CompilerParams(
            collective_id=3, has_side_effects=True, vmem_limit_bytes=40 * 1024 * 1024
        ),
        name="finish",
    )(*arrays)


def unpack_kernel(reduced, extras, rows_in, gq, go, gn, gp, gb, gg, rows_out, sem):
    copy = pltpu.make_async_copy(rows_in, rows_out, sem)
    copy.start()
    for column in range(12):
        block = reduced[column * 256 : (column + 1) * 256, :].astype(jnp.float32)
        if column < 6:
            gq[:, column * UNIT : (column + 1) * UNIT] = block
        elif column < 8:
            go[:, (column - 6) * UNIT : (column - 5) * UNIT] = block
        else:
            gp[:, (column - 8) * UNIT : (column - 7) * UNIT] = block
    for i in range(2):
        gn[:, i * UNIT : (i + 1) * UNIT] = extras[8 + i : 9 + i, :]
    for i in range(4):
        gb[:, i * UNIT : (i + 1) * UNIT] = extras[i : i + 1, :]
        gg[:, i * UNIT : (i + 1) * UNIT] = extras[4 + i : 5 + i, :]
    copy.wait()


def unpack(reduced, extras, rows):
    vmem = pl.BlockSpec(memory_space=pltpu.VMEM)
    outside = pl.BlockSpec(memory_space=pl.ANY)
    shapes = ((256, 768), (256, 256), (1, 256), (256, 512), (1, 512), (1, 512), (PATCH, 256))
    return pl.pallas_call(
        unpack_kernel,
        out_shape=[jax.ShapeDtypeStruct(shape, jnp.float32) for shape in shapes],
        in_specs=[vmem, vmem, vmem],
        out_specs=[vmem] * 6 + [outside],
        scratch_shapes=[pltpu.SemaphoreType.DMA],
        compiler_params=pltpu.CompilerParams(vmem_limit_bytes=16 * 1024 * 1024),
        name="unpack",
    )(reduced, extras, rows)


def body(
    points, patch_ids, cell_ids, norm_gain, w_qkv, w_out, w_pool, b_pool, pool_gain, cotangent
):
    scale = 1.0 / math.sqrt(points.shape[0] * lax.axis_size("pts"))
    gain = norm_gain[None]
    cells = cell_ids.reshape(4, HALF)
    far = [
        pltpu.with_memory_space_constraint(array, pltpu.HBM)
        for array in (points, patch_ids.reshape(4, HALF), gain, w_qkv, w_out, cells)
    ]
    queries, queries_t, keys_g, values_g, marks_f, hidden, spans = prepare(*far[:4])
    attended, logs, sums, counts = attend(
        spans, queries_t, marks_f, keys_g, values_g, far[0], far[4], far[5]
    )
    dmixed, datt, datt_t, deltas, gw_pool, gw_out, gb_pool, g_gain = pool(
        scale, sums, counts, cells, attended, w_out, w_pool, b_pool[None], pool_gain[None], cotangent
    )
    dq, dk, dv = attend_back(
        spans, queries, queries_t, logs, datt, datt_t, deltas, keys_g, values_g
    )
    grad_points, reduced, extras = finish(
        scale, hidden, dq, dk, dv, dmixed, points, gain, w_qkv, gw_out, gw_pool, gb_pool, g_gain
    )
    gq, go, gn, gp, gb, gg, grad_points = unpack(reduced, extras, grad_points)
    return (grad_points, gq, go, gn[0], gp, gb[0], gg[0])


def solution(mesh):
    in_specs = (P("pts", None), P("pts"), P("pts"), P(), P(), P(), P(), P(), P(), P("pts", None))
    out_specs = (P("pts", None), P(), P(), P(), P(), P(), P())
    return jax.shard_map(body, mesh=mesh, in_specs=in_specs, out_specs=out_specs, check_vma=False)
```

```python
import functools
import math

import jax
import jax.numpy as jnp
from jax import lax
from jax.experimental import pallas as pl
from jax.experimental.pallas import tpu as pltpu
from jax.sharding import PartitionSpec as P

PATCH = 512
MESH = pl.DeviceIdType.MESH


EPS = 1e-05
ROOT_HALF = 0.7071067811865476
ROOT_TWO_PI = 2.5066282746310002


def layer_stats(values):
    centered = values - jnp.mean(values, axis=-1, keepdims=True)
    inv_std = lax.rsqrt(jnp.mean(centered * centered, axis=-1, keepdims=True) + EPS)
    return (centered * inv_std, inv_std)


def norm_back(grad_normed, normed, inv_std):
    first_mean = jnp.mean(grad_normed, axis=-1, keepdims=True)
    second_mean = jnp.mean(grad_normed * normed, axis=-1, keepdims=True)
    return inv_std * (grad_normed - first_mean - normed * second_mean)


def gelu_slope(scaled):
    normal_cdf = 0.5 * (1.0 + lax.erf(scaled * ROOT_HALF))
    return normal_cdf + scaled * jnp.exp(-0.5 * scaled * scaled) / ROOT_TWO_PI


def inner_rows(left, right):
    return lax.dot_general(
        left, right, (((0,), (0,)), ((), ())), preferred_element_type=jnp.float32
    )


def against_rows(left, right):
    return lax.dot_general(
        left, right, (((1,), (1,)), ((), ())), preferred_element_type=jnp.float32
    )


HALF = 128
PER_HALF = 8
HEAD_SIZE = 16
TILE = 128
CHUNK = 528
TALL = 3 * CHUNK
TILES = PATCH // TILE
PAIR = 256 // TILE
WINDOW = 3 * PATCH
FAR = float(2**30)
DIGIT = 32
LOG_LANE = 64


def head_mask(h, axis):
    shape = (1, 2 * HALF) if axis else (2 * HALF, 1)
    place = lax.broadcasted_iota(jnp.int32, shape, axis)
    own = (place >= h * HEAD_SIZE) & (place < (h + 1) * HEAD_SIZE)
    marks = (place >= HALF) & (place < HALF + LOG_LANE)
    terms = (place >= HALF + LOG_LANE) & (place < HALF + LOG_LANE + 24) & (place % PER_HALF == h)
    return (own | marks | terms).astype(jnp.float32).astype(jnp.bfloat16)


def split_three(values, which):
    first = values.astype(jnp.bfloat16).astype(jnp.float32)
    second = (values - first).astype(jnp.bfloat16).astype(jnp.float32)
    third = values - first - second
    return jnp.where(which == 0, first, jnp.where(which == 1, second, third))


def neighbours():
    me = lax.axis_index("pts")
    count = lax.axis_size("pts")
    return me, (me + count - 1) % count, (me + 1) % count


def greet_neighbours(before, after):
    barrier = pltpu.get_barrier_semaphore()
    for device in (before, after):
        pl.semaphore_signal(barrier, inc=1, device_id=(device,), device_id_type=MESH)
    pl.semaphore_wait(barrier, 2)


def send(source, landing, sems, index, device):
    copy = pltpu.make_async_remote_copy(
        src_ref=source,
        dst_ref=landing,
        send_sem=sems.at[0, index],
        recv_sem=sems.at[1, index],
        device_id=(device,),
        device_id_type=MESH,
    )
    copy.start()
    return copy


def digit_columns(marks):
    row = lax.broadcasted_iota(jnp.int32, (HALF, HALF), 0)
    high, low = marks // DIGIT, marks % DIGIT
    hit = ((row < DIGIT) & (row == high)) | ((row >= DIGIT) & (row < LOG_LANE) & (row - DIGIT == low))
    return hit.astype(jnp.float32)


def prepare_kernel(
    points_hbm, ids_hbm, gain_hbm, w_hbm, q_ref, qt_ref, kg_ref, vg_ref, f_ref, hidden_ref, spans_ref,
    points, ids, gain, w_qkv, marks, marks_low, marks_high, rows_low, rows_high, sems, local_sems,
):
    me, before, after = neighbours()
    local = []
    for i, (source, target) in enumerate(
        ((ids_hbm, ids), (points_hbm, points), (w_hbm, w_qkv), (gain_hbm, gain))
    ):
        local.append(pltpu.make_async_copy(source, target, local_sems.at[i]))
        local[-1].start()
    marks[...] = jnp.zeros_like(marks)
    greet_neighbours(before, after)
    local[0].wait()
    marks[:4, :] = ids[...] + 1
    local[1].wait()
    copies = [
        send(points, rows_high, sems, 0, before),
        send(points, rows_low, sems, 1, after),
        send(marks, marks_high, sems, 2, before),
        send(marks, marks_low, sems, 3, after),
    ]
    local[2].wait()
    local[3].wait()

    def project(block, first, columns):
        normed, _ = layer_stats(block[...].astype(jnp.float32))
        hidden = (normed * gain[...]).astype(jnp.bfloat16)
        hidden_ref[first : first + PATCH, :] = hidden
        return jnp.dot(hidden, w_qkv[:, columns], preferred_element_type=jnp.float32)

    def place(first, keys, values):
        for g in range(2):
            lanes = slice(g * HALF, (g + 1) * HALF)
            kg_ref[g, first : first + PATCH, :HALF] = keys[:, lanes].astype(jnp.bfloat16)
            vg_ref[g, first : first + PATCH, :HALF] = values[:, lanes].astype(jnp.bfloat16)

    def place_marks(block, first, own):
        lane = lax.broadcasted_iota(jnp.int32, (HALF, HALF), 1)
        row = lax.broadcasted_iota(jnp.int32, (HALF, HALF), 0)
        terms = (lane >= LOG_LANE) & (lane < LOG_LANE + 24)
        for i in range(4):
            rows = slice(first + i * HALF, first + (i + 1) * HALF)
            digits = digit_columns(block[i : i + 1, :])
            both = jnp.where(terms, 1.0, digits.T).astype(jnp.bfloat16)
            for g in range(2):
                kg_ref[g, rows, HALF:] = both
                vg_ref[g, rows, HALF:] = both
            if own:
                away = jnp.where(row < LOG_LANE, (1.0 - digits) * -FAR, 0.0)
                f_ref[:, i * HALF : (i + 1) * HALF] = away.astype(jnp.bfloat16)

    qkv = project(points, PATCH, slice(None))
    queries = qkv[:, :256].astype(jnp.bfloat16).astype(jnp.float32) * 0.25
    q_ref[...] = queries.astype(jnp.bfloat16)
    qt_ref[...] = queries.T.astype(jnp.bfloat16)
    place(PATCH, qkv[:, 256:512], qkv[:, 512:])
    own = marks[...]
    place_marks(own, PATCH, True)
    lane = lax.broadcasted_iota(jnp.int32, (TALL - WINDOW, 2 * HALF), 1)
    nowhere = ((lane == HALF) | (lane == HALF + DIGIT)).astype(jnp.float32).astype(jnp.bfloat16)
    for g in range(2):
        kg_ref[g, WINDOW:, :] = nowhere
        vg_ref[g, WINDOW:, :] = nowhere
    for copy in copies[2:]:
        copy.wait()
    low = jnp.where(me == 0, 0, marks_low[...])
    high = jnp.where(me == lax.axis_size("pts") - 1, 0, marks_high[...])
    place_marks(low, 0, False)
    place_marks(high, 2 * PATCH, False)
    own_f, low_f, high_f = (block[:4].astype(jnp.float32) for block in (own, low, high))
    for t in range(TILES):
        ours = own_f[t * TILE // HALF : (t + 1) * TILE // HALF]
        first, last = jnp.min(ours), jnp.max(ours)
        lower = jnp.sum((low_f < first).astype(jnp.float32) + (own_f < first).astype(jnp.float32))
        upper = jnp.sum(
            ((high_f > 0) & (high_f <= last)).astype(jnp.float32) + (own_f <= last).astype(jnp.float32)
        )
        lower = lower.astype(jnp.int32) // 16 * 16
        count = (PATCH + upper.astype(jnp.int32) - lower + CHUNK - 1) // CHUNK
        spans_ref[t, 0] = jnp.minimum(lower, TALL - count * CHUNK)
        spans_ref[t, 1] = count
    for copy, block, first in ((copies[1], rows_low, 0), (copies[0], rows_high, 2 * PATCH)):
        copy.wait()
        kv = project(block, first, slice(256, 768))
        place(first, kv[:, :256], kv[:, 256:])


def prepare(points, ids, gain, w_qkv):
    half = jnp.bfloat16
    vmem = pl.BlockSpec(memory_space=pltpu.VMEM)
    return pl.pallas_call(
        prepare_kernel,
        out_shape=[
            jax.ShapeDtypeStruct((PATCH, 256), half),
            jax.ShapeDtypeStruct((256, PATCH), half),
            jax.ShapeDtypeStruct((2, TALL, 2 * HALF), half),
            jax.ShapeDtypeStruct((2, TALL, 2 * HALF), half),
            jax.ShapeDtypeStruct((HALF, PATCH), half),
            jax.ShapeDtypeStruct((WINDOW, 256), half),
            jax.ShapeDtypeStruct((TILES, 2), jnp.int32),
        ],
        in_specs=[pl.BlockSpec(memory_space=pltpu.HBM)] * 4,
        out_specs=[vmem] * 6 + [pl.BlockSpec(memory_space=pltpu.SMEM)],
        scratch_shapes=[
            pltpu.VMEM((PATCH, 256), half),
            pltpu.VMEM((4, HALF), jnp.int32),
            pltpu.VMEM((1, 256), jnp.float32),
            pltpu.VMEM((256, 768), half),
            pltpu.VMEM((8, HALF), jnp.int32),
            pltpu.VMEM((8, HALF), jnp.int32),
            pltpu.VMEM((8, HALF), jnp.int32),
            pltpu.VMEM((PATCH, 256), half),
            pltpu.VMEM((PATCH, 256), half),
            pltpu.SemaphoreType.DMA((2, 4)),
            pltpu.SemaphoreType.DMA((4,)),
        ],
        compiler_params=pltpu.CompilerParams(
            collective_id=1, has_side_effects=True, vmem_limit_bytes=32 * 1024 * 1024
        ),
        name="prepare",
    )(points, ids, gain, w_qkv)


SLOTS = 144


def membership(cells):
    local = cells - lax.axis_index("pts") * HALF
    local = jnp.where(local < 0, HALF, local)
    slot = lax.broadcasted_iota(jnp.int32, (SLOTS, HALF), 0)
    parts = [(slot == local[i : i + 1, :]).astype(jnp.float32) for i in range(4)]
    return jnp.concatenate(parts, axis=1)


def tall_max(scores):
    part = CHUNK // 6
    folded = scores[:part]
    for i in range(1, 6):
        folded = jnp.maximum(folded, scores[i * part : (i + 1) * part])
    return jnp.max(folded, axis=0, keepdims=True)


def block_of(index, size):
    return pl.ds(pl.multiple_of(index * size, size), size)


def forward_kernel(
    spans, qt_ref, f_ref, kg_ref, vg_ref, points_hbm, w_out_hbm, cells_hbm,
    att_ref, logs_ref, sums_ref, counts_ref, qt, kept, att_t, top_t, total_t, points, w_out, cells, sems,
):
    late = [
        pltpu.make_async_copy(source, target, sems.at[i])
        for i, (source, target) in enumerate(
            ((points_hbm, points), (w_out_hbm, w_out), (cells_hbm, cells))
        )
    ]
    for copy in late:
        copy.start()
    qt[...] = jnp.zeros_like(qt)

    def step(index, carry):
        forward_step(
            index, spans, qt_ref, f_ref, kg_ref, vg_ref, att_ref, logs_ref,
            qt, kept, att_t, top_t, total_t,
        )
        return carry

    lax.fori_loop(0, TILES, step, 0)
    for copy in late:
        copy.wait()
    mixed = points[...].astype(jnp.float32) + jnp.dot(
        att_ref[...], w_out[...], preferred_element_type=jnp.float32
    )
    member = membership(cells[...])
    sums_ref[...] = jnp.dot(
        member.astype(jnp.bfloat16), mixed.astype(jnp.bfloat16), preferred_element_type=jnp.float32
    )
    counts_ref[...] = jnp.broadcast_to(jnp.sum(member, axis=1, keepdims=True), (SLOTS, HALF))


PAIRS = PER_HALF // PAIR


def forward_step(
    tile, spans, qt_ref, f_ref, kg_ref, vg_ref, att_ref, logs_ref, qt, kept, att_t, top_t, total_t
):
    start, count = spans[tile, 0], spans[tile, 1]
    mine = block_of(tile, TILE)
    marks = f_ref[:LOG_LANE, mine]
    for half in range(2):
        queries_t = qt_ref[half * HALF : (half + 1) * HALF, mine]
        for h in range(PER_HALF):
            p, place = half * PAIRS + h // PAIR, slice(h % PAIR * TILE, (h % PAIR + 1) * TILE)
            own = slice(h * HEAD_SIZE, (h + 1) * HEAD_SIZE)
            qt[p, own, place] = queries_t[own]
            qt[p, HALF : HALF + LOG_LANE, place] = marks
    top_t[...] = jnp.full_like(top_t, -3e38)
    total_t[...] = jnp.zeros_like(total_t)
    att_t[...] = jnp.zeros_like(att_t)

    def chunk(c, carry):
        rows = pl.ds(pl.multiple_of(start + c * CHUNK, 16), CHUNK)
        ones = jnp.ones((16, CHUNK), jnp.bfloat16)
        tops, values_t = [], []
        for half in range(2):
            values_t.append(vg_ref[half, rows, :HALF].astype(jnp.float32).T.astype(jnp.bfloat16))
            for p in range(half * PAIRS, (half + 1) * PAIRS):
                scores = jnp.dot(kg_ref[half, rows, :], qt[p], preferred_element_type=jnp.float32)
                kept[p] = scores
                tops.append(jnp.maximum(top_t[p : p + 1, :], tall_max(scores)))
        for p in range(2 * PAIRS):
            before, top = top_t[p : p + 1, :], tops[p]
            weights = jnp.exp(kept[p] - top).astype(jnp.bfloat16)
            decay = jnp.exp(before - top)
            top_t[p : p + 1, :] = top
            size = PAIR * HEAD_SIZE
            own, inner = slice(p * size, (p + 1) * size), slice(p % PAIRS * size, (p % PAIRS + 1) * size)
            left = jnp.concatenate([values_t[p // PAIRS][inner], ones], axis=0)
            mixed = jnp.dot(left, weights, preferred_element_type=jnp.float32)
            total_t[p : p + 1, :] = total_t[p : p + 1, :] * decay + mixed[size : size + 1]
            att_t[own, :] = att_t[own, :] * decay + mixed[:size]
        return carry

    lax.fori_loop(0, count, chunk, 0)
    logs_p = -(top_t[...] + jnp.log(total_t[...]))
    spare = jnp.zeros((HALF - LOG_LANE - 24, TILE), jnp.float32)
    for half in range(2):
        parts, logs = [], []
        for h in range(half * PER_HALF, (half + 1) * PER_HALF):
            p, columns = h // PAIR, slice(h % PAIR * TILE, (h % PAIR + 1) * TILE)
            piece = att_t[h * HEAD_SIZE : (h + 1) * HEAD_SIZE, columns]
            parts.append(piece / total_t[p : p + 1, columns])
            logs.append(logs_p[p : p + 1, columns])
        lanes = slice(half * HALF, (half + 1) * HALF)
        att_ref[mine, lanes] = jnp.concatenate(parts, axis=0).T.astype(jnp.bfloat16)
        logs = jnp.concatenate(logs, axis=0)
        terms = [split_three(logs, i) for i in range(3)]
        ending = jnp.concatenate(terms + [spare], axis=0).astype(jnp.bfloat16)
        logs_ref[lanes, mine] = jnp.concatenate([marks, ending], axis=0)


def attend(spans, queries_t, marks_f, keys_g, values_g, points, w_out, cells):
    vmem = pl.BlockSpec(memory_space=pltpu.VMEM)
    outside = pl.BlockSpec(memory_space=pltpu.HBM)
    return pl.pallas_call(
        forward_kernel,
        out_shape=[
            jax.ShapeDtypeStruct((PATCH, 256), jnp.bfloat16),
            jax.ShapeDtypeStruct((256, PATCH), jnp.bfloat16),
            jax.ShapeDtypeStruct((SLOTS, 256), jnp.float32),
            jax.ShapeDtypeStruct((SLOTS, HALF), jnp.float32),
        ],
        in_specs=[pl.BlockSpec(memory_space=pltpu.SMEM)] + [vmem] * 4 + [outside] * 3,
        out_specs=[vmem] * 4,
        scratch_shapes=[
            pltpu.VMEM((2 * PAIRS, 2 * HALF, PAIR * TILE), jnp.bfloat16),
            pltpu.VMEM((2 * PAIRS, CHUNK, PAIR * TILE), jnp.float32),
            pltpu.VMEM((2 * HALF, PAIR * TILE), jnp.float32),
            pltpu.VMEM((2 * PAIRS, PAIR * TILE), jnp.float32),
            pltpu.VMEM((2 * PAIRS, PAIR * TILE), jnp.float32),
            pltpu.VMEM((PATCH, 256), jnp.bfloat16),
            pltpu.VMEM((256, 256), jnp.bfloat16),
            pltpu.VMEM((4, HALF), jnp.int32),
            pltpu.SemaphoreType.DMA((3,)),
        ],
        compiler_params=pltpu.CompilerParams(vmem_limit_bytes=24 * 1024 * 1024),
        name="attention",
    )(spans, queries_t, marks_f, keys_g, values_g, points, w_out, cells)


def pool_kernel(
    scale, sums, counts, cells, att, w_out, w_pool, b_pool, pool_gain, cotangent,
    dmixed_ref, datt_ref, datt_t_ref, delta_ref, gw_pool, gw_out, gb_pool, g_gain,
    back_pack, ahead_pack, from_after, from_before, sems,
):
    me, before, after = neighbours()
    back_pack[:, :256] = sums[HALF : HALF + 8, :]
    back_pack[:, 256:] = counts[HALF : HALF + 8, :]
    ahead_pack[:, :256] = sums[HALF - 8 : HALF, :]
    ahead_pack[:, 256:384] = counts[HALF - 8 : HALF, :]
    ahead_pack[:, 384:] = cotangent[HALF - 8 :, :]
    greet_neighbours(before, after)
    copies = [
        send(back_pack, from_after, sems, 0, before),
        send(ahead_pack, from_before, sems, 1, after),
    ]
    member = membership(cells[...]).astype(jnp.bfloat16)
    for copy in copies:
        copy.wait()
    row = lax.broadcasted_iota(jnp.int32, (8, 1), 0)
    late, early = from_after[0:1, :], from_before[7:8, :]
    last_sum = sums[HALF - 8 : HALF, :] + jnp.where(row == 7, late[:, :256], 0.0)
    lead_sum = jnp.where(row == 0, sums[HALF : HALF + 8, :] + early[:, :256], 0.0)
    last_count = counts[HALF - 8 : HALF, :] + jnp.where(row == 7, late[:, 256:], 0.0)
    lead_count = jnp.where(row == 0, counts[HALF : HALF + 8, :] + early[:, 256:384], 0.0)
    spare = jnp.zeros((8, 256), jnp.float32)
    all_sums = jnp.concatenate([sums[: HALF - 8, :], last_sum, lead_sum, spare], axis=0)
    all_counts = jnp.concatenate(
        [counts[: HALF - 8, :], last_count, lead_count, spare[:, :HALF]], axis=0
    )[:, :1]
    all_counts = jnp.maximum(all_counts, 1.0)
    lead_cot = jnp.where(row == 0, early[:, 384:], 0.0)
    all_cot = jnp.concatenate([cotangent[...], lead_cot, jnp.zeros((8, 512), jnp.float32)], axis=0)

    pooled_mean = (all_sums / all_counts).astype(jnp.bfloat16)
    pre_norm = jnp.dot(pooled_mean, w_pool[...], preferred_element_type=jnp.float32) + b_pool[...]
    pooled_normed, pooled_inv = layer_stats(pre_norm)
    slope_grad = all_cot * gelu_slope(pooled_normed * pool_gain[...])
    grad_pre = norm_back(slope_grad * pool_gain[...], pooled_normed, pooled_inv)
    grad_pre_b = grad_pre.astype(jnp.bfloat16)
    share = against_rows(grad_pre_b, w_pool[...]) / all_counts
    share_b = share.astype(jnp.bfloat16)
    rest_b = (share - share_b.astype(jnp.float32)).astype(jnp.bfloat16)
    dmixed_main = inner_rows(member, share_b)
    dmixed_ref[...] = dmixed_main + inner_rows(member, rest_b)
    dmixed_b = dmixed_main.astype(jnp.bfloat16)
    datt = against_rows(dmixed_b, w_out[...]).astype(jnp.bfloat16)
    datt_f = datt.astype(jnp.float32)
    datt_ref[...] = (datt_f * 0.25).astype(jnp.bfloat16)
    product = datt_f * att[...].astype(jnp.float32)
    datt_t = against_rows(w_out[...], dmixed_b).astype(jnp.bfloat16).astype(jnp.float32)
    datt_t_ref[...] = (datt_t * 0.25).astype(jnp.bfloat16)
    slot = lax.broadcasted_iota(jnp.int32, (256, 256), 0)
    channel = lax.broadcasted_iota(jnp.int32, (256, 256), 1)
    spot = slot % HALF - LOG_LANE
    place = (channel // HALF == slot // HALF) & (spot >= 0) & (spot < 24)
    place = (place & (spot % PER_HALF == channel % HALF // HEAD_SIZE)).astype(jnp.float32)
    place = place.astype(jnp.bfloat16)
    first = product.astype(jnp.bfloat16)
    second = product - first.astype(jnp.float32)
    second_b = second.astype(jnp.bfloat16)
    third_b = (second - second_b.astype(jnp.float32)).astype(jnp.bfloat16)
    deltas = against_rows(place, first) + against_rows(place, second_b) + against_rows(place, third_b)
    which = (lax.broadcasted_iota(jnp.int32, (256, 1), 0) % HALF - LOG_LANE) // PER_HALF
    delta_ref[...] = split_three(deltas * -0.25, which).astype(jnp.bfloat16)
    gw_pool[...] = (inner_rows(pooled_mean[:HALF], grad_pre_b[:HALF]) * scale).astype(jnp.bfloat16)
    gw_out[...] = (inner_rows(att[...], dmixed_b) * scale).astype(jnp.bfloat16)
    gb_pool[...] = jnp.sum(grad_pre[:HALF], axis=0, keepdims=True) * scale
    g_gain[...] = jnp.sum(slope_grad[:HALF] * pooled_normed[:HALF], axis=0, keepdims=True) * scale


def pool(scale, *arrays):
    half = jnp.bfloat16
    vmem = pl.BlockSpec(memory_space=pltpu.VMEM)
    return pl.pallas_call(
        functools.partial(pool_kernel, scale),
        out_shape=[
            jax.ShapeDtypeStruct((PATCH, 256), jnp.float32),
            jax.ShapeDtypeStruct((PATCH, 256), half),
            jax.ShapeDtypeStruct((256, PATCH), half),
            jax.ShapeDtypeStruct((256, PATCH), half),
            jax.ShapeDtypeStruct((256, 512), half),
            jax.ShapeDtypeStruct((256, 256), half),
            jax.ShapeDtypeStruct((1, 512), jnp.float32),
            jax.ShapeDtypeStruct((1, 512), jnp.float32),
        ],
        in_specs=[vmem] * 9,
        out_specs=[vmem] * 8,
        scratch_shapes=[
            pltpu.VMEM((8, 384), jnp.float32),
            pltpu.VMEM((8, 896), jnp.float32),
            pltpu.VMEM((8, 384), jnp.float32),
            pltpu.VMEM((8, 896), jnp.float32),
            pltpu.SemaphoreType.DMA((2, 2)),
        ],
        compiler_params=pltpu.CompilerParams(
            collective_id=2, has_side_effects=True, vmem_limit_bytes=32 * 1024 * 1024
        ),
        name="pooling",
    )(*arrays)


def backward_kernel(
    spans, q_ref, qt_ref, logs_ref, do_ref, dot_ref, deltas_ref, kg_ref, vg_ref,
    dq_ref, dk_ref, dv_ref, qt, dt, qn, dn, some, slopes, dqt, dk_sum, dv_sum,
):
    qt[...] = jnp.zeros_like(qt)
    dt[...] = jnp.zeros_like(dt)
    dk_sum[...] = jnp.zeros_like(dk_sum)
    dv_sum[...] = jnp.zeros_like(dv_sum)

    def step(tile, carry):
        backward_step(
            tile, spans, q_ref, qt_ref, logs_ref, do_ref, dot_ref, deltas_ref, kg_ref, vg_ref,
            dq_ref, qt, dt, qn, dn, some, slopes, dqt, dk_sum, dv_sum,
        )
        return carry

    lax.fori_loop(0, TILES, step, 0)
    dk_ref[...] = (dk_sum[:WINDOW] * 4.0).astype(jnp.bfloat16)
    dv_ref[...] = (dv_sum[:WINDOW] * 4.0).astype(jnp.bfloat16)


def backward_step(
    tile, spans, q_ref, qt_ref, logs_ref, do_ref, dot_ref, deltas_ref, kg_ref, vg_ref,
    dq_ref, qt, dt, qn, dn, some, slopes, dqt, dk_sum, dv_sum,
):
    start, count = spans[tile, 0], spans[tile, 1]
    mine = block_of(tile, TILE)
    after = HALF + LOG_LANE
    halves = [slice(half * HALF, (half + 1) * HALF) for half in range(2)]
    for half, turned in enumerate(halves):
        queries, douts = q_ref[mine, turned], do_ref[mine, turned]
        queries_t, douts_t = qt_ref[turned, mine], dot_ref[turned, mine]
        logs, deltas = logs_ref[turned, mine], deltas_ref[turned, mine]
        for h in range(PER_HALF):
            p, place = half * PAIRS + h // PAIR, slice(h % PAIR * TILE, (h % PAIR + 1) * TILE)
            own = slice(h * HEAD_SIZE, (h + 1) * HEAD_SIZE)
            terms = head_mask(h, 0)[after : after + 32]
            qt[p, own, place] = queries_t[own]
            qt[p, HALF:after, place] = logs[:LOG_LANE]
            qt[p, after : after + 32, place] = logs[LOG_LANE : LOG_LANE + 32] * terms
            dt[p, own, place] = douts_t[own]
            dt[p, after : after + 32, place] = deltas[LOG_LANE : LOG_LANE + 32] * terms
            lanes = head_mask(h, 1)[:, :HALF]
            qn[p, place, :] = queries * lanes
            dn[p, place, :] = douts * lanes
    dqt[...] = jnp.zeros_like(dqt)
    width = PAIR * TILE

    def chunk(c, carry):
        rows = pl.ds(pl.multiple_of(start + c * CHUNK, 16), CHUNK)
        keys_t = []
        for half in range(2):
            keys_t.append(kg_ref[half, rows, :HALF].astype(jnp.float32).T.astype(jnp.bfloat16))
            for p in range(half * PAIRS, (half + 1) * PAIRS):
                weights = jnp.exp(
                    jnp.dot(kg_ref[half, rows, :], qt[p], preferred_element_type=jnp.float32)
                )
                dweights = jnp.dot(vg_ref[half, rows, :], dt[p], preferred_element_type=jnp.float32)
                place = slice(p * width, (p + 1) * width)
                some[:, place] = weights.astype(jnp.bfloat16)
                slopes[:, place] = (weights * dweights).astype(jnp.bfloat16)
        depth = PAIRS * width
        for half, lanes in enumerate(halves):
            place, pairs = slice(half * depth, (half + 1) * depth), slice(half * PAIRS, (half + 1) * PAIRS)
            dk_sum[rows, lanes] += jnp.dot(
                slopes[:, place], qn[pairs].reshape(depth, HALF), preferred_element_type=jnp.float32
            )
            dv_sum[rows, lanes] += jnp.dot(
                some[:, place], dn[pairs].reshape(depth, HALF), preferred_element_type=jnp.float32
            )
        size = PAIR * HEAD_SIZE
        for p in range(2 * PAIRS):
            inner = slice(p % PAIRS * size, (p % PAIRS + 1) * size)
            dqt[p * size : (p + 1) * size, :] += jnp.dot(
                keys_t[p // PAIRS][inner],
                slopes[:, p * width : (p + 1) * width],
                preferred_element_type=jnp.float32,
            )
        return carry

    lax.fori_loop(0, count, chunk, 0)
    for half, turned in enumerate(halves):
        parts = []
        for h in range(half * PER_HALF, (half + 1) * PER_HALF):
            place = slice(h % PAIR * TILE, (h % PAIR + 1) * TILE)
            parts.append(dqt[h * HEAD_SIZE : (h + 1) * HEAD_SIZE, place])
        dq_ref[mine, turned] = jnp.concatenate(parts, axis=0).T.astype(jnp.bfloat16)


def attend_back(spans, queries, queries_t, logs, douts, douts_t, deltas, keys_g, values_g):
    vmem = pl.BlockSpec(memory_space=pltpu.VMEM)
    half = jnp.bfloat16
    return pl.pallas_call(
        backward_kernel,
        out_shape=[
            jax.ShapeDtypeStruct((PATCH, 256), half),
            jax.ShapeDtypeStruct((WINDOW, 256), half),
            jax.ShapeDtypeStruct((WINDOW, 256), half),
        ],
        in_specs=[pl.BlockSpec(memory_space=pltpu.SMEM)] + [vmem] * 8,
        out_specs=[vmem] * 3,
        scratch_shapes=[
            pltpu.VMEM((2 * PAIRS, 2 * HALF, PAIR * TILE), half),
            pltpu.VMEM((2 * PAIRS, 2 * HALF, PAIR * TILE), half),
            pltpu.VMEM((2 * PAIRS, PAIR * TILE, HALF), half),
            pltpu.VMEM((2 * PAIRS, PAIR * TILE, HALF), half),
            pltpu.VMEM((CHUNK, 2 * PAIRS * PAIR * TILE), half),
            pltpu.VMEM((CHUNK, 2 * PAIRS * PAIR * TILE), half),
            pltpu.VMEM((2 * HALF, PAIR * TILE), jnp.float32),
            pltpu.VMEM((TALL, 2 * HALF), jnp.float32),
            pltpu.VMEM((TALL, 2 * HALF), jnp.float32),
        ],
        compiler_params=pltpu.CompilerParams(vmem_limit_bytes=24 * 1024 * 1024),
        name="attention_back",
    )(spans, queries, queries_t, logs, douts, douts_t, deltas, keys_g, values_g)


UNIT = 128
EXTRA = 16
CORE_ROWS = 12 * UNIT
X_ROWS = CORE_ROWS // 4
Y_ROWS = X_ROWS // 8


def axes():
    me = lax.axis_index("pts")
    core, z, y, x = me % 2, (me // 2) % 8, (me // 16) % 8, me // 128
    return (
        (core, 2, lambda r: x * 128 + y * 16 + z * 2 + r),
        (x, 4, lambda r: r * 128 + y * 16 + z * 2 + core),
        (y, 8, lambda r: x * 128 + r * 16 + z * 2 + core),
        (z, 8, lambda r: x * 128 + y * 16 + r * 2 + core),
    )


def far_first(size):
    return sorted(range(1, size), key=lambda k: -min(k, size - k))


def swap(axis, source, landing, sems, first):
    rank, size, device = axis
    copies = []
    for k in far_first(size):
        peer = (rank + k) % size
        copies.append(send(source(peer), landing(rank), sems, first + k - 1, device(peer)))
    return copies[::-1]


def wait_all(copies):
    for copy in copies:
        copy.wait()


def slot_sum(ref, start, size):
    total = ref[0, start : start + size, :].astype(jnp.float32)
    for r in range(1, ref.shape[0]):
        total = total + ref[r, start : start + size, :].astype(jnp.float32)
    return total


def finish_kernel(
    scale, hidden, dq, dk, dv, dmixed, points, gain, w_qkv, gw_out, gw_pool, gb_pool, g_gain,
    grad_points, reduced, extras,
    low_k, low_v, high_k, high_v, send_c, recv_c, extra_own, extra_in,
    send_x, recv_x, send_y, recv_y, recv_z, gather_c, sems,
):
    me, before, after = neighbours()
    on_core, on_x, on_y, on_z = axes()
    barrier = pltpu.get_barrier_semaphore()
    greeted = []
    for rank, size, device in (on_z, on_y, on_x, on_core):
        greeted += [device((rank + k) % size) for k in far_first(size)]
    greeted += [before, after]
    for device in greeted:
        pl.semaphore_signal(barrier, inc=1, device_id=(device,), device_id_type=MESH)

    def fill(block, first_unit):
        for column in range(block.shape[1] // UNIT):
            unit = first_unit + 2 * column
            start = unit % 12 * UNIT
            for part in range(2):
                at = start + part * UNIT
                rows = slice(at % X_ROWS, at % X_ROWS + UNIT)
                send_c[unit // 12, at // X_ROWS, rows, :] = block[
                    part * UNIT : (part + 1) * UNIT, column * UNIT : (column + 1) * UNIT
                ]

    fill(gw_out[...], 12)
    fill(gw_pool[...], 16)
    pieces = [gb_pool[:, i * UNIT : (i + 1) * UNIT] for i in range(4)]
    pieces += [g_gain[:, i * UNIT : (i + 1) * UNIT] for i in range(4)]
    pieces += [jnp.zeros((EXTRA - 8, UNIT), jnp.float32)]
    packed = jnp.concatenate(pieces, axis=0).astype(jnp.bfloat16)
    extra_own[...] = packed
    own = slice(PATCH, 2 * PATCH)
    fill((inner_rows(hidden[own, :], dq[...]) * scale).astype(jnp.bfloat16), 0)
    fill((inner_rows(hidden[...], dk[...]) * scale).astype(jnp.bfloat16), 4)
    fill((inner_rows(hidden[...], dv[...]) * scale).astype(jnp.bfloat16), 8)

    pl.semaphore_wait(barrier, len(greeted))
    core, core_device = on_core[0], on_core[2](1 - on_core[0])
    x, x_device = on_x[0], on_x[2]
    steps = (2, 1, 3, 0)
    quarters = [(x + k) % 4 for k in steps]
    extra_copy = send(extra_own, extra_in, sems, 57, core_device)
    core_copies = [
        send(send_c.at[1 - core, q], recv_c.at[q], sems, k, core_device) for k, q in enumerate(quarters)
    ]
    rims = [
        send(dk.at[pl.ds(0, PATCH)], high_k, sems, 60, before),
        send(dv.at[pl.ds(0, PATCH)], high_v, sems, 61, before),
        send(dk.at[pl.ds(2 * PATCH, PATCH)], low_k, sems, 62, after),
        send(dv.at[pl.ds(2 * PATCH, PATCH)], low_v, sems, 63, after),
    ]
    extra_copy.wait()
    extra = (extra_own[...].astype(jnp.float32) + extra_in[...].astype(jnp.float32)).astype(jnp.bfloat16)
    copies = []
    for k, q in enumerate(quarters):
        core_copies[k].wait()
        total = send_c[core, q].astype(jnp.float32) + recv_c[q].astype(jnp.float32)
        if k < 3:
            send_x[q, :X_ROWS, :] = total.astype(jnp.bfloat16)
            send_x[q, X_ROWS:, :] = extra
            copies.append(send(send_x.at[q], recv_x.at[x], sems, 4 + steps[k], x_device(q)))
        else:
            recv_x[x, :X_ROWS, :] = total.astype(jnp.bfloat16)
            recv_x[x, X_ROWS:, :] = extra
    dhidden = against_rows(dq[...], w_qkv[:, :256])
    normed, inv_std = layer_stats(points[...].astype(jnp.float32))
    wait_all(copies)
    extra = slot_sum(recv_x, X_ROWS, EXTRA).astype(jnp.bfloat16)
    for r in range(8):
        send_y[r, :Y_ROWS, :] = slot_sum(recv_x, r * Y_ROWS, Y_ROWS).astype(jnp.bfloat16)
        send_y[r, Y_ROWS:, :] = extra

    copies = swap(on_y, lambda r: send_y.at[r], lambda r: recv_y.at[r], sems, 8)
    recv_y[on_y[0]] = send_y[on_y[0]]
    wait_all(rims)
    for columns, mine, low, high in (
        (slice(256, 512), dk, low_k, high_k), (slice(512, 768), dv, low_v, high_v)
    ):
        total = mine[own, :].astype(jnp.float32) + low[...].astype(jnp.float32)
        total = (total + high[...].astype(jnp.float32)).astype(jnp.bfloat16)
        dhidden = dhidden + against_rows(total, w_qkv[:, columns])
    grad_points[...] = dmixed[...] + norm_back(dhidden * gain[...], normed, inv_std)
    wait_all(copies)
    recv_z[on_z[0]] = slot_sum(recv_y, 0, Y_ROWS + EXTRA).astype(jnp.bfloat16)

    wait_all(swap(on_z, lambda r: recv_z.at[on_z[0]], lambda r: recv_z.at[r], sems, 15))
    total = slot_sum(recv_z, 0, Y_ROWS + EXTRA)
    extras[...] = total[Y_ROWS:]
    y, y_device = on_y[0], on_y[2]
    gather_c[core, x, y] = total[:Y_ROWS].astype(jnp.bfloat16)
    order = (1, 7, 2, 6, 3, 5, 4)

    def pass_on(k):
        piece = gather_c.at[core, x, (y + 8 - k) % 8]
        return {i: send(piece, piece, sems, 28 + 3 * k + i, x_device((x + i) % 4)) for i in (2, 1, 3)}

    mine = gather_c.at[core, x, y]
    y_copies = {k: send(mine, mine, sems, 22 + k - 1, y_device((y + k) % 8)) for k in order[::-1]}
    x_copies = {0: pass_on(0)}
    for k in order:
        y_copies[k].wait()
        x_copies[k] = pass_on(k)
    core_copies = [send(gather_c.at[core, x], gather_c.at[core, x], sems, 53, core_device)]
    for i in (1, 3, 2):
        for k in (0,) + order:
            x_copies[k][i].wait()
        slot = gather_c.at[core, (x + 4 - i) % 4]
        core_copies.append(send(slot, slot, sems, 53 + i, core_device))
    wait_all(core_copies)
    for c in range(2):
        for r in range(4):
            for s in range(8):
                start = c * CORE_ROWS + r * X_ROWS + s * Y_ROWS
                reduced[start : start + Y_ROWS, :] = gather_c[c, r, s]
    weighted = jnp.zeros((256, UNIT), jnp.float32)
    for column in range(6):
        block = reduced[column * 256 : (column + 1) * 256, :].astype(jnp.float32)
        lanes = slice(column * UNIT, (column + 1) * UNIT)
        weighted = weighted + block * w_qkv[:, lanes].astype(jnp.float32)
    summed_gain = jnp.sum(weighted.T, axis=0, keepdims=True) / gain[...]
    for i in range(2):
        extras[8 + i : 9 + i, :] = summed_gain[:, i * UNIT : (i + 1) * UNIT]


def finish(scale, *arrays):
    half = jnp.bfloat16
    vmem = pl.BlockSpec(memory_space=pltpu.VMEM)
    return pl.pallas_call(
        functools.partial(finish_kernel, scale),
        out_shape=[
            jax.ShapeDtypeStruct((PATCH, 256), jnp.float32),
            jax.ShapeDtypeStruct((2 * CORE_ROWS, UNIT), half),
            jax.ShapeDtypeStruct((EXTRA, UNIT), jnp.float32),
        ],
        in_specs=[vmem] * 12,
        out_specs=[vmem] * 3,
        scratch_shapes=[pltpu.VMEM((PATCH, 256), half)] * 4
        + [
            pltpu.VMEM((2, 4, X_ROWS, UNIT), half),
            pltpu.VMEM((4, X_ROWS, UNIT), half),
            pltpu.VMEM((EXTRA, UNIT), half),
            pltpu.VMEM((EXTRA, UNIT), half),
            pltpu.VMEM((4, X_ROWS + EXTRA, UNIT), half),
            pltpu.VMEM((4, X_ROWS + EXTRA, UNIT), half),
            pltpu.VMEM((8, Y_ROWS + EXTRA, UNIT), half),
            pltpu.VMEM((8, Y_ROWS + EXTRA, UNIT), half),
            pltpu.VMEM((8, Y_ROWS + EXTRA, UNIT), half),
            pltpu.VMEM((2, 4, 8, Y_ROWS, UNIT), half),
            pltpu.SemaphoreType.DMA((2, 64)),
        ],
        compiler_params=pltpu.CompilerParams(
            collective_id=3, has_side_effects=True, vmem_limit_bytes=40 * 1024 * 1024
        ),
        name="finish",
    )(*arrays)


def unpack_kernel(reduced, extras, rows_in, gq, go, gn, gp, gb, gg, rows_out, sem):
    copy = pltpu.make_async_copy(rows_in, rows_out, sem)
    copy.start()
    for column in range(12):
        block = reduced[column * 256 : (column + 1) * 256, :].astype(jnp.float32)
        if column < 6:
            gq[:, column * UNIT : (column + 1) * UNIT] = block
        elif column < 8:
            go[:, (column - 6) * UNIT : (column - 5) * UNIT] = block
        else:
            gp[:, (column - 8) * UNIT : (column - 7) * UNIT] = block
    for i in range(2):
        gn[:, i * UNIT : (i + 1) * UNIT] = extras[8 + i : 9 + i, :]
    for i in range(4):
        gb[:, i * UNIT : (i + 1) * UNIT] = extras[i : i + 1, :]
        gg[:, i * UNIT : (i + 1) * UNIT] = extras[4 + i : 5 + i, :]
    copy.wait()


def unpack(reduced, extras, rows):
    vmem = pl.BlockSpec(memory_space=pltpu.VMEM)
    outside = pl.BlockSpec(memory_space=pl.ANY)
    shapes = ((256, 768), (256, 256), (1, 256), (256, 512), (1, 512), (1, 512), (PATCH, 256))
    return pl.pallas_call(
        unpack_kernel,
        out_shape=[jax.ShapeDtypeStruct(shape, jnp.float32) for shape in shapes],
        in_specs=[vmem, vmem, vmem],
        out_specs=[vmem] * 6 + [outside],
        scratch_shapes=[pltpu.SemaphoreType.DMA],
        compiler_params=pltpu.CompilerParams(vmem_limit_bytes=16 * 1024 * 1024),
        name="unpack",
    )(reduced, extras, rows)


def body(
    points, patch_ids, cell_ids, norm_gain, w_qkv, w_out, w_pool, b_pool, pool_gain, cotangent
):
    scale = 1.0 / math.sqrt(points.shape[0] * lax.axis_size("pts"))
    gain = norm_gain[None]
    cells = cell_ids.reshape(4, HALF)
    far = [
        pltpu.with_memory_space_constraint(array, pltpu.HBM)
        for array in (points, patch_ids.reshape(4, HALF), gain, w_qkv, w_out, cells)
    ]
    queries, queries_t, keys_g, values_g, marks_f, hidden, spans = prepare(*far[:4])
    attended, logs, sums, counts = attend(
        spans, queries_t, marks_f, keys_g, values_g, far[0], far[4], far[5]
    )
    dmixed, datt, datt_t, deltas, gw_pool, gw_out, gb_pool, g_gain = pool(
        scale, sums, counts, cells, attended, w_out, w_pool, b_pool[None], pool_gain[None], cotangent
    )
    dq, dk, dv = attend_back(
        spans, queries, queries_t, logs, datt, datt_t, deltas, keys_g, values_g
    )
    grad_points, reduced, extras = finish(
        scale, hidden, dq, dk, dv, dmixed, points, gain, w_qkv, gw_out, gw_pool, gb_pool, g_gain
    )
    gq, go, gn, gp, gb, gg, grad_points = unpack(reduced, extras, grad_points)
    return (grad_points, gq, go, gn[0], gp, gb[0], gg[0])


def solution(mesh):
    in_specs = (P("pts", None), P("pts"), P("pts"), P(), P(), P(), P(), P(), P(), P("pts", None))
    out_specs = (P("pts", None), P(), P(), P(), P(), P(), P())
    return jax.shard_map(body, mesh=mesh, in_specs=in_specs, out_specs=out_specs, check_vma=False)
```

```python
import functools
import math

import jax
import jax.numpy as jnp
from jax import lax
from jax.experimental import pallas as pl
from jax.experimental.pallas import tpu as pltpu
from jax.sharding import PartitionSpec as P

PATCH = 512
MESH = pl.DeviceIdType.MESH


EPS = 1e-05
ROOT_HALF = 0.7071067811865476
ROOT_TWO_PI = 2.5066282746310002


def layer_stats(values):
    centered = values - jnp.mean(values, axis=-1, keepdims=True)
    inv_std = lax.rsqrt(jnp.mean(centered * centered, axis=-1, keepdims=True) + EPS)
    return (centered * inv_std, inv_std)


def norm_back(grad_normed, normed, inv_std):
    first_mean = jnp.mean(grad_normed, axis=-1, keepdims=True)
    second_mean = jnp.mean(grad_normed * normed, axis=-1, keepdims=True)
    return inv_std * (grad_normed - first_mean - normed * second_mean)


def gelu_slope(scaled):
    normal_cdf = 0.5 * (1.0 + lax.erf(scaled * ROOT_HALF))
    return normal_cdf + scaled * jnp.exp(-0.5 * scaled * scaled) / ROOT_TWO_PI


def inner_rows(left, right):
    return lax.dot_general(
        left, right, (((0,), (0,)), ((), ())), preferred_element_type=jnp.float32
    )


def against_rows(left, right):
    return lax.dot_general(
        left, right, (((1,), (1,)), ((), ())), preferred_element_type=jnp.float32
    )


HALF = 128
PER_HALF = 8
HEAD_SIZE = 16
TILE = 128
CHUNK = 528
TALL = 3 * CHUNK
TILES = PATCH // TILE
PAIR = 256 // TILE
WINDOW = 3 * PATCH
FAR = float(2**30)
DIGIT = 32
LOG_LANE = 64


def head_mask(h, axis):
    shape = (1, 2 * HALF) if axis else (2 * HALF, 1)
    place = lax.broadcasted_iota(jnp.int32, shape, axis)
    own = (place >= h * HEAD_SIZE) & (place < (h + 1) * HEAD_SIZE)
    marks = (place >= HALF) & (place < HALF + LOG_LANE)
    terms = (place >= HALF + LOG_LANE) & (place < HALF + LOG_LANE + 24) & (place % PER_HALF == h)
    return (own | marks | terms).astype(jnp.float32).astype(jnp.bfloat16)


def split_three(values, which):
    first = values.astype(jnp.bfloat16).astype(jnp.float32)
    second = (values - first).astype(jnp.bfloat16).astype(jnp.float32)
    third = values - first - second
    return jnp.where(which == 0, first, jnp.where(which == 1, second, third))


def neighbours():
    me = lax.axis_index("pts")
    count = lax.axis_size("pts")
    return me, (me + count - 1) % count, (me + 1) % count


def greet_neighbours(before, after):
    barrier = pltpu.get_barrier_semaphore()
    for device in (before, after):
        pl.semaphore_signal(barrier, inc=1, device_id=(device,), device_id_type=MESH)
    pl.semaphore_wait(barrier, 2)


def send(source, landing, sems, index, device):
    copy = pltpu.make_async_remote_copy(
        src_ref=source,
        dst_ref=landing,
        send_sem=sems.at[0, index],
        recv_sem=sems.at[1, index],
        device_id=(device,),
        device_id_type=MESH,
    )
    copy.start()
    return copy


def digit_columns(marks):
    row = lax.broadcasted_iota(jnp.int32, (HALF, HALF), 0)
    high, low = marks // DIGIT, marks % DIGIT
    hit = ((row < DIGIT) & (row == high)) | ((row >= DIGIT) & (row < LOG_LANE) & (row - DIGIT == low))
    return hit.astype(jnp.float32)


def prepare_kernel(
    points_hbm, ids_hbm, gain_hbm, w_hbm, q_ref, qt_ref, kg_ref, vg_ref, f_ref, hidden_ref, spans_ref,
    points, ids, gain, w_qkv, marks, marks_low, marks_high, rows_low, rows_high, sems, local_sems,
):
    me, before, after = neighbours()
    local = []
    for i, (source, target) in enumerate(
        ((ids_hbm, ids), (points_hbm, points), (w_hbm, w_qkv), (gain_hbm, gain))
    ):
        local.append(pltpu.make_async_copy(source, target, local_sems.at[i]))
        local[-1].start()
    marks[...] = jnp.zeros_like(marks)
    greet_neighbours(before, after)
    local[0].wait()
    marks[:4, :] = ids[...] + 1
    local[1].wait()
    copies = [send(marks, marks_high, sems, 0, before), send(marks, marks_low, sems, 1, after)]
    parts = [pl.ds(i * TILE * 2, TILE * 2) for i in range(2)]
    halo = []
    for i, part in enumerate(parts):
        halo.append(
            (
                send(points.at[part], rows_high.at[part], sems, 2 + 2 * i, before),
                send(points.at[part], rows_low.at[part], sems, 3 + 2 * i, after),
            )
        )
    local[2].wait()
    local[3].wait()

    def project(block, first, columns):
        normed, _ = layer_stats(block.astype(jnp.float32))
        hidden = (normed * gain[...]).astype(jnp.bfloat16)
        hidden_ref[first : first + block.shape[0], :] = hidden
        return jnp.dot(hidden, w_qkv[:, columns], preferred_element_type=jnp.float32)

    def place(first, keys, values):
        for g in range(2):
            lanes = slice(g * HALF, (g + 1) * HALF)
            rows = slice(first, first + keys.shape[0])
            kg_ref[g, rows, :HALF] = keys[:, lanes].astype(jnp.bfloat16)
            vg_ref[g, rows, :HALF] = values[:, lanes].astype(jnp.bfloat16)

    def place_marks(block, first, own):
        lane = lax.broadcasted_iota(jnp.int32, (HALF, HALF), 1)
        row = lax.broadcasted_iota(jnp.int32, (HALF, HALF), 0)
        terms = (lane >= LOG_LANE) & (lane < LOG_LANE + 24)
        for i in range(4):
            rows = slice(first + i * HALF, first + (i + 1) * HALF)
            digits = digit_columns(block[i : i + 1, :])
            both = jnp.where(terms, 1.0, digits.T).astype(jnp.bfloat16)
            for g in range(2):
                kg_ref[g, rows, HALF:] = both
                vg_ref[g, rows, HALF:] = both
            if own:
                away = jnp.where(row < LOG_LANE, (1.0 - digits) * -FAR, 0.0)
                f_ref[:, i * HALF : (i + 1) * HALF] = away.astype(jnp.bfloat16)

    qkv = project(points[...], PATCH, slice(None))
    queries = qkv[:, :256].astype(jnp.bfloat16).astype(jnp.float32) * 0.25
    q_ref[...] = queries.astype(jnp.bfloat16)
    qt_ref[...] = queries.T.astype(jnp.bfloat16)
    place(PATCH, qkv[:, 256:512], qkv[:, 512:])
    own = marks[...]
    place_marks(own, PATCH, True)
    lane = lax.broadcasted_iota(jnp.int32, (TALL - WINDOW, 2 * HALF), 1)
    nowhere = ((lane == HALF) | (lane == HALF + DIGIT)).astype(jnp.float32).astype(jnp.bfloat16)
    for g in range(2):
        kg_ref[g, WINDOW:, :] = nowhere
        vg_ref[g, WINDOW:, :] = nowhere
    for copy in copies:
        copy.wait()
    low = jnp.where(me == 0, 0, marks_low[...])
    high = jnp.where(me == lax.axis_size("pts") - 1, 0, marks_high[...])
    place_marks(low, 0, False)
    place_marks(high, 2 * PATCH, False)
    own_f, low_f, high_f = (block[:4].astype(jnp.float32) for block in (own, low, high))
    for t in range(TILES):
        ours = own_f[t * TILE // HALF : (t + 1) * TILE // HALF]
        first, last = jnp.min(ours), jnp.max(ours)
        lower = jnp.sum((low_f < first).astype(jnp.float32) + (own_f < first).astype(jnp.float32))
        upper = jnp.sum(
            ((high_f > 0) & (high_f <= last)).astype(jnp.float32) + (own_f <= last).astype(jnp.float32)
        )
        lower = lower.astype(jnp.int32) // 16 * 16
        count = (PATCH + upper.astype(jnp.int32) - lower + CHUNK - 1) // CHUNK
        spans_ref[t, 0] = jnp.minimum(lower, TALL - count * CHUNK)
        spans_ref[t, 1] = count
    for part, (high_copy, low_copy) in zip(parts, halo):
        for copy, block, first in ((low_copy, rows_low, 0), (high_copy, rows_high, 2 * PATCH)):
            copy.wait()
            kv = project(block[part, :], first + part.start, slice(256, 768))
            place(first + part.start, kv[:, :256], kv[:, 256:])


def prepare(points, ids, gain, w_qkv):
    half = jnp.bfloat16
    vmem = pl.BlockSpec(memory_space=pltpu.VMEM)
    return pl.pallas_call(
        prepare_kernel,
        out_shape=[
            jax.ShapeDtypeStruct((PATCH, 256), half),
            jax.ShapeDtypeStruct((256, PATCH), half),
            jax.ShapeDtypeStruct((2, TALL, 2 * HALF), half),
            jax.ShapeDtypeStruct((2, TALL, 2 * HALF), half),
            jax.ShapeDtypeStruct((HALF, PATCH), half),
            jax.ShapeDtypeStruct((WINDOW, 256), half),
            jax.ShapeDtypeStruct((TILES, 2), jnp.int32),
        ],
        in_specs=[pl.BlockSpec(memory_space=pltpu.HBM)] * 4,
        out_specs=[vmem] * 6 + [pl.BlockSpec(memory_space=pltpu.SMEM)],
        scratch_shapes=[
            pltpu.VMEM((PATCH, 256), half),
            pltpu.VMEM((4, HALF), jnp.int32),
            pltpu.VMEM((1, 256), jnp.float32),
            pltpu.VMEM((256, 768), half),
            pltpu.VMEM((8, HALF), jnp.int32),
            pltpu.VMEM((8, HALF), jnp.int32),
            pltpu.VMEM((8, HALF), jnp.int32),
            pltpu.VMEM((PATCH, 256), half),
            pltpu.VMEM((PATCH, 256), half),
            pltpu.SemaphoreType.DMA((2, 6)),
            pltpu.SemaphoreType.DMA((4,)),
        ],
        compiler_params=pltpu.CompilerParams(
            collective_id=1, has_side_effects=True, vmem_limit_bytes=32 * 1024 * 1024
        ),
        name="prepare",
    )(points, ids, gain, w_qkv)


SLOTS = 144


def membership(cells):
    local = cells - lax.axis_index("pts") * HALF
    local = jnp.where(local < 0, HALF, local)
    slot = lax.broadcasted_iota(jnp.int32, (SLOTS, HALF), 0)
    parts = [(slot == local[i : i + 1, :]).astype(jnp.float32) for i in range(4)]
    return jnp.concatenate(parts, axis=1)


def tall_max(scores):
    part = CHUNK // 6
    folded = scores[:part]
    for i in range(1, 6):
        folded = jnp.maximum(folded, scores[i * part : (i + 1) * part])
    return jnp.max(folded, axis=0, keepdims=True)


def block_of(index, size):
    return pl.ds(pl.multiple_of(index * size, size), size)


def forward_kernel(
    spans, qt_ref, f_ref, kg_ref, vg_ref, points_hbm, w_out_hbm, cells_hbm,
    att_ref, logs_ref, sums_ref, counts_ref, qt, kept, att_t, top_t, total_t, points, w_out, cells, sems,
):
    late = [
        pltpu.make_async_copy(source, target, sems.at[i])
        for i, (source, target) in enumerate(
            ((points_hbm, points), (w_out_hbm, w_out), (cells_hbm, cells))
        )
    ]
    for copy in late:
        copy.start()
    qt[...] = jnp.zeros_like(qt)

    def step(index, carry):
        forward_step(
            index, spans, qt_ref, f_ref, kg_ref, vg_ref, att_ref, logs_ref,
            qt, kept, att_t, top_t, total_t,
        )
        return carry

    lax.fori_loop(0, TILES, step, 0)
    for copy in late:
        copy.wait()
    mixed = points[...].astype(jnp.float32) + jnp.dot(
        att_ref[...], w_out[...], preferred_element_type=jnp.float32
    )
    member = membership(cells[...])
    sums_ref[...] = jnp.dot(
        member.astype(jnp.bfloat16), mixed.astype(jnp.bfloat16), preferred_element_type=jnp.float32
    )
    counts_ref[...] = jnp.broadcast_to(jnp.sum(member, axis=1, keepdims=True), (SLOTS, HALF))


PAIRS = PER_HALF // PAIR


def forward_step(
    tile, spans, qt_ref, f_ref, kg_ref, vg_ref, att_ref, logs_ref, qt, kept, att_t, top_t, total_t
):
    start, count = spans[tile, 0], spans[tile, 1]
    mine = block_of(tile, TILE)
    marks = f_ref[:LOG_LANE, mine]
    for half in range(2):
        queries_t = qt_ref[half * HALF : (half + 1) * HALF, mine]
        for h in range(PER_HALF):
            p, place = half * PAIRS + h // PAIR, slice(h % PAIR * TILE, (h % PAIR + 1) * TILE)
            own = slice(h * HEAD_SIZE, (h + 1) * HEAD_SIZE)
            qt[p, own, place] = queries_t[own]
            qt[p, HALF : HALF + LOG_LANE, place] = marks
    top_t[...] = jnp.full_like(top_t, -3e38)
    total_t[...] = jnp.zeros_like(total_t)
    att_t[...] = jnp.zeros_like(att_t)

    def chunk(c, carry):
        rows = pl.ds(pl.multiple_of(start + c * CHUNK, 16), CHUNK)
        ones = jnp.ones((16, CHUNK), jnp.bfloat16)
        tops, values_t = [], []
        for half in range(2):
            values_t.append(vg_ref[half, rows, :HALF].astype(jnp.float32).T.astype(jnp.bfloat16))
            for p in range(half * PAIRS, (half + 1) * PAIRS):
                scores = jnp.dot(kg_ref[half, rows, :], qt[p], preferred_element_type=jnp.float32)
                kept[p] = scores
                tops.append(jnp.maximum(top_t[p : p + 1, :], tall_max(scores)))
        for p in range(2 * PAIRS):
            before, top = top_t[p : p + 1, :], tops[p]
            weights = jnp.exp(kept[p] - top).astype(jnp.bfloat16)
            decay = jnp.exp(before - top)
            top_t[p : p + 1, :] = top
            size = PAIR * HEAD_SIZE
            own, inner = slice(p * size, (p + 1) * size), slice(p % PAIRS * size, (p % PAIRS + 1) * size)
            left = jnp.concatenate([values_t[p // PAIRS][inner], ones], axis=0)
            mixed = jnp.dot(left, weights, preferred_element_type=jnp.float32)
            total_t[p : p + 1, :] = total_t[p : p + 1, :] * decay + mixed[size : size + 1]
            att_t[own, :] = att_t[own, :] * decay + mixed[:size]
        return carry

    lax.fori_loop(0, count, chunk, 0)
    logs_p = -(top_t[...] + jnp.log(total_t[...]))
    spare = jnp.zeros((HALF - LOG_LANE - 24, TILE), jnp.float32)
    for half in range(2):
        parts, logs = [], []
        for h in range(half * PER_HALF, (half + 1) * PER_HALF):
            p, columns = h // PAIR, slice(h % PAIR * TILE, (h % PAIR + 1) * TILE)
            piece = att_t[h * HEAD_SIZE : (h + 1) * HEAD_SIZE, columns]
            parts.append(piece / total_t[p : p + 1, columns])
            logs.append(logs_p[p : p + 1, columns])
        lanes = slice(half * HALF, (half + 1) * HALF)
        att_ref[mine, lanes] = jnp.concatenate(parts, axis=0).T.astype(jnp.bfloat16)
        logs = jnp.concatenate(logs, axis=0)
        terms = [split_three(logs, i) for i in range(3)]
        ending = jnp.concatenate(terms + [spare], axis=0).astype(jnp.bfloat16)
        logs_ref[lanes, mine] = jnp.concatenate([marks, ending], axis=0)


def attend(spans, queries_t, marks_f, keys_g, values_g, points, w_out, cells):
    vmem = pl.BlockSpec(memory_space=pltpu.VMEM)
    outside = pl.BlockSpec(memory_space=pltpu.HBM)
    return pl.pallas_call(
        forward_kernel,
        out_shape=[
            jax.ShapeDtypeStruct((PATCH, 256), jnp.bfloat16),
            jax.ShapeDtypeStruct((256, PATCH), jnp.bfloat16),
            jax.ShapeDtypeStruct((SLOTS, 256), jnp.float32),
            jax.ShapeDtypeStruct((SLOTS, HALF), jnp.float32),
        ],
        in_specs=[pl.BlockSpec(memory_space=pltpu.SMEM)] + [vmem] * 4 + [outside] * 3,
        out_specs=[vmem] * 4,
        scratch_shapes=[
            pltpu.VMEM((2 * PAIRS, 2 * HALF, PAIR * TILE), jnp.bfloat16),
            pltpu.VMEM((2 * PAIRS, CHUNK, PAIR * TILE), jnp.float32),
            pltpu.VMEM((2 * HALF, PAIR * TILE), jnp.float32),
            pltpu.VMEM((2 * PAIRS, PAIR * TILE), jnp.float32),
            pltpu.VMEM((2 * PAIRS, PAIR * TILE), jnp.float32),
            pltpu.VMEM((PATCH, 256), jnp.bfloat16),
            pltpu.VMEM((256, 256), jnp.bfloat16),
            pltpu.VMEM((4, HALF), jnp.int32),
            pltpu.SemaphoreType.DMA((3,)),
        ],
        compiler_params=pltpu.CompilerParams(vmem_limit_bytes=24 * 1024 * 1024),
        name="attention",
    )(spans, queries_t, marks_f, keys_g, values_g, points, w_out, cells)


def pool_kernel(
    scale, sums, counts, cells, att, w_out, w_pool, b_pool, pool_gain, cotangent,
    dmixed_ref, datt_ref, datt_t_ref, delta_ref, gw_pool, gw_out, gb_pool, g_gain,
    back_pack, ahead_pack, from_after, from_before, sems,
):
    me, before, after = neighbours()
    back_pack[:, :256] = sums[HALF : HALF + 8, :]
    back_pack[:, 256:] = counts[HALF : HALF + 8, :]
    ahead_pack[:, :256] = sums[HALF - 8 : HALF, :]
    ahead_pack[:, 256:384] = counts[HALF - 8 : HALF, :]
    ahead_pack[:, 384:] = cotangent[HALF - 8 :, :]
    greet_neighbours(before, after)
    copies = [
        send(back_pack, from_after, sems, 0, before),
        send(ahead_pack, from_before, sems, 1, after),
    ]
    member = membership(cells[...]).astype(jnp.bfloat16)
    early_rows = HALF - 16

    def cells_back(sums, counts, cotangent):
        pooled_mean = (sums / counts).astype(jnp.bfloat16)
        pre_norm = jnp.dot(pooled_mean, w_pool[...], preferred_element_type=jnp.float32) + b_pool[...]
        pooled_normed, pooled_inv = layer_stats(pre_norm)
        slope_grad = cotangent * gelu_slope(pooled_normed * pool_gain[...])
        grad_pre = norm_back(slope_grad * pool_gain[...], pooled_normed, pooled_inv)
        grad_pre_b = grad_pre.astype(jnp.bfloat16)
        share = against_rows(grad_pre_b, w_pool[...]) / counts
        return pooled_mean, pooled_normed, slope_grad, grad_pre, grad_pre_b, share

    early_back = cells_back(
        sums[:early_rows, :], counts[:early_rows, :1], cotangent[:early_rows, :]
    )
    for copy in copies:
        copy.wait()
    row = lax.broadcasted_iota(jnp.int32, (8, 1), 0)
    late, early = from_after[0:1, :], from_before[7:8, :]
    last_sum = sums[HALF - 8 : HALF, :] + jnp.where(row == 7, late[:, :256], 0.0)
    lead_sum = jnp.where(row == 0, sums[HALF : HALF + 8, :] + early[:, :256], 0.0)
    last_count = counts[HALF - 8 : HALF, :] + jnp.where(row == 7, late[:, 256:], 0.0)
    lead_count = jnp.where(row == 0, counts[HALF : HALF + 8, :] + early[:, 256:384], 0.0)
    spare = jnp.zeros((8, 256), jnp.float32)
    middle = slice(early_rows, HALF - 8)
    late_sums = jnp.concatenate([sums[middle, :], last_sum, lead_sum, spare], axis=0)
    late_counts = jnp.concatenate(
        [counts[middle, :], last_count, lead_count, spare[:, :HALF]], axis=0
    )[:, :1]
    lead_cot = jnp.where(row == 0, early[:, 384:], 0.0)
    late_cot = jnp.concatenate(
        [cotangent[early_rows:, :], lead_cot, jnp.zeros((8, 512), jnp.float32)], axis=0
    )
    late_back = cells_back(late_sums, jnp.maximum(late_counts, 1.0), late_cot)
    pooled_mean, pooled_normed, slope_grad, grad_pre, grad_pre_b, share = (
        jnp.concatenate(pair, axis=0) for pair in zip(early_back, late_back)
    )
    share_b = share.astype(jnp.bfloat16)
    rest_b = (share - share_b.astype(jnp.float32)).astype(jnp.bfloat16)
    dmixed_main = inner_rows(member, share_b)
    dmixed_ref[...] = dmixed_main + inner_rows(member, rest_b)
    dmixed_b = dmixed_main.astype(jnp.bfloat16)
    datt = against_rows(dmixed_b, w_out[...]).astype(jnp.bfloat16)
    datt_f = datt.astype(jnp.float32)
    datt_ref[...] = (datt_f * 0.25).astype(jnp.bfloat16)
    product = datt_f * att[...].astype(jnp.float32)
    datt_t = against_rows(w_out[...], dmixed_b).astype(jnp.bfloat16).astype(jnp.float32)
    datt_t_ref[...] = (datt_t * 0.25).astype(jnp.bfloat16)
    slot = lax.broadcasted_iota(jnp.int32, (256, 256), 0)
    channel = lax.broadcasted_iota(jnp.int32, (256, 256), 1)
    spot = slot % HALF - LOG_LANE
    place = (channel // HALF == slot // HALF) & (spot >= 0) & (spot < 24)
    place = (place & (spot % PER_HALF == channel % HALF // HEAD_SIZE)).astype(jnp.float32)
    place = place.astype(jnp.bfloat16)
    first = product.astype(jnp.bfloat16)
    second = product - first.astype(jnp.float32)
    second_b = second.astype(jnp.bfloat16)
    third_b = (second - second_b.astype(jnp.float32)).astype(jnp.bfloat16)
    deltas = against_rows(place, first) + against_rows(place, second_b) + against_rows(place, third_b)
    which = (lax.broadcasted_iota(jnp.int32, (256, 1), 0) % HALF - LOG_LANE) // PER_HALF
    delta_ref[...] = split_three(deltas * -0.25, which).astype(jnp.bfloat16)
    gw_pool[...] = (inner_rows(pooled_mean[:HALF], grad_pre_b[:HALF]) * scale).astype(jnp.bfloat16)
    gw_out[...] = (inner_rows(att[...], dmixed_b) * scale).astype(jnp.bfloat16)
    gb_pool[...] = jnp.sum(grad_pre[:HALF], axis=0, keepdims=True) * scale
    g_gain[...] = jnp.sum(slope_grad[:HALF] * pooled_normed[:HALF], axis=0, keepdims=True) * scale


def pool(scale, *arrays):
    half = jnp.bfloat16
    vmem = pl.BlockSpec(memory_space=pltpu.VMEM)
    return pl.pallas_call(
        functools.partial(pool_kernel, scale),
        out_shape=[
            jax.ShapeDtypeStruct((PATCH, 256), jnp.float32),
            jax.ShapeDtypeStruct((PATCH, 256), half),
            jax.ShapeDtypeStruct((256, PATCH), half),
            jax.ShapeDtypeStruct((256, PATCH), half),
            jax.ShapeDtypeStruct((256, 512), half),
            jax.ShapeDtypeStruct((256, 256), half),
            jax.ShapeDtypeStruct((1, 512), jnp.float32),
            jax.ShapeDtypeStruct((1, 512), jnp.float32),
        ],
        in_specs=[vmem] * 9,
        out_specs=[vmem] * 8,
        scratch_shapes=[
            pltpu.VMEM((8, 384), jnp.float32),
            pltpu.VMEM((8, 896), jnp.float32),
            pltpu.VMEM((8, 384), jnp.float32),
            pltpu.VMEM((8, 896), jnp.float32),
            pltpu.SemaphoreType.DMA((2, 2)),
        ],
        compiler_params=pltpu.CompilerParams(
            collective_id=2, has_side_effects=True, vmem_limit_bytes=32 * 1024 * 1024
        ),
        name="pooling",
    )(*arrays)


def backward_kernel(
    spans, q_ref, qt_ref, logs_ref, do_ref, dot_ref, deltas_ref, kg_ref, vg_ref,
    dq_ref, dk_ref, dv_ref, qt, dt, qn, dn, some, slopes, dqt, dk_sum, dv_sum,
):
    qt[...] = jnp.zeros_like(qt)
    dt[...] = jnp.zeros_like(dt)
    dk_sum[...] = jnp.zeros_like(dk_sum)
    dv_sum[...] = jnp.zeros_like(dv_sum)

    def step(tile, carry):
        backward_step(
            tile, spans, q_ref, qt_ref, logs_ref, do_ref, dot_ref, deltas_ref, kg_ref, vg_ref,
            dq_ref, qt, dt, qn, dn, some, slopes, dqt, dk_sum, dv_sum,
        )
        return carry

    lax.fori_loop(0, TILES, step, 0)
    dk_ref[...] = (dk_sum[:WINDOW] * 4.0).astype(jnp.bfloat16)
    dv_ref[...] = (dv_sum[:WINDOW] * 4.0).astype(jnp.bfloat16)


def backward_step(
    tile, spans, q_ref, qt_ref, logs_ref, do_ref, dot_ref, deltas_ref, kg_ref, vg_ref,
    dq_ref, qt, dt, qn, dn, some, slopes, dqt, dk_sum, dv_sum,
):
    start, count = spans[tile, 0], spans[tile, 1]
    mine = block_of(tile, TILE)
    after = HALF + LOG_LANE
    halves = [slice(half * HALF, (half + 1) * HALF) for half in range(2)]
    for half, turned in enumerate(halves):
        queries, douts = q_ref[mine, turned], do_ref[mine, turned]
        queries_t, douts_t = qt_ref[turned, mine], dot_ref[turned, mine]
        logs, deltas = logs_ref[turned, mine], deltas_ref[turned, mine]
        for h in range(PER_HALF):
            p, place = half * PAIRS + h // PAIR, slice(h % PAIR * TILE, (h % PAIR + 1) * TILE)
            own = slice(h * HEAD_SIZE, (h + 1) * HEAD_SIZE)
            terms = head_mask(h, 0)[after : after + 32]
            qt[p, own, place] = queries_t[own]
            qt[p, HALF:after, place] = logs[:LOG_LANE]
            qt[p, after : after + 32, place] = logs[LOG_LANE : LOG_LANE + 32] * terms
            dt[p, own, place] = douts_t[own]
            dt[p, after : after + 32, place] = deltas[LOG_LANE : LOG_LANE + 32] * terms
            lanes = head_mask(h, 1)[:, :HALF]
            qn[p, place, :] = queries * lanes
            dn[p, place, :] = douts * lanes
    dqt[...] = jnp.zeros_like(dqt)
    width = PAIR * TILE

    def chunk(c, carry):
        rows = pl.ds(pl.multiple_of(start + c * CHUNK, 16), CHUNK)
        keys_t = []
        for half in range(2):
            keys_t.append(kg_ref[half, rows, :HALF].astype(jnp.float32).T.astype(jnp.bfloat16))
            for p in range(half * PAIRS, (half + 1) * PAIRS):
                weights = jnp.exp(
                    jnp.dot(kg_ref[half, rows, :], qt[p], preferred_element_type=jnp.float32)
                )
                dweights = jnp.dot(vg_ref[half, rows, :], dt[p], preferred_element_type=jnp.float32)
                place = slice(p * width, (p + 1) * width)
                some[:, place] = weights.astype(jnp.bfloat16)
                slopes[:, place] = (weights * dweights).astype(jnp.bfloat16)
        depth = PAIRS * width
        for half, lanes in enumerate(halves):
            place, pairs = slice(half * depth, (half + 1) * depth), slice(half * PAIRS, (half + 1) * PAIRS)
            dk_sum[rows, lanes] += jnp.dot(
                slopes[:, place], qn[pairs].reshape(depth, HALF), preferred_element_type=jnp.float32
            )
            dv_sum[rows, lanes] += jnp.dot(
                some[:, place], dn[pairs].reshape(depth, HALF), preferred_element_type=jnp.float32
            )
        size = PAIR * HEAD_SIZE
        for p in range(2 * PAIRS):
            inner = slice(p % PAIRS * size, (p % PAIRS + 1) * size)
            dqt[p * size : (p + 1) * size, :] += jnp.dot(
                keys_t[p // PAIRS][inner],
                slopes[:, p * width : (p + 1) * width],
                preferred_element_type=jnp.float32,
            )
        return carry

    lax.fori_loop(0, count, chunk, 0)
    for half, turned in enumerate(halves):
        parts = []
        for h in range(half * PER_HALF, (half + 1) * PER_HALF):
            place = slice(h % PAIR * TILE, (h % PAIR + 1) * TILE)
            parts.append(dqt[h * HEAD_SIZE : (h + 1) * HEAD_SIZE, place])
        dq_ref[mine, turned] = jnp.concatenate(parts, axis=0).T.astype(jnp.bfloat16)


def attend_back(spans, queries, queries_t, logs, douts, douts_t, deltas, keys_g, values_g):
    vmem = pl.BlockSpec(memory_space=pltpu.VMEM)
    half = jnp.bfloat16
    return pl.pallas_call(
        backward_kernel,
        out_shape=[
            jax.ShapeDtypeStruct((PATCH, 256), half),
            jax.ShapeDtypeStruct((WINDOW, 256), half),
            jax.ShapeDtypeStruct((WINDOW, 256), half),
        ],
        in_specs=[pl.BlockSpec(memory_space=pltpu.SMEM)] + [vmem] * 8,
        out_specs=[vmem] * 3,
        scratch_shapes=[
            pltpu.VMEM((2 * PAIRS, 2 * HALF, PAIR * TILE), half),
            pltpu.VMEM((2 * PAIRS, 2 * HALF, PAIR * TILE), half),
            pltpu.VMEM((2 * PAIRS, PAIR * TILE, HALF), half),
            pltpu.VMEM((2 * PAIRS, PAIR * TILE, HALF), half),
            pltpu.VMEM((CHUNK, 2 * PAIRS * PAIR * TILE), half),
            pltpu.VMEM((CHUNK, 2 * PAIRS * PAIR * TILE), half),
            pltpu.VMEM((2 * HALF, PAIR * TILE), jnp.float32),
            pltpu.VMEM((TALL, 2 * HALF), jnp.float32),
            pltpu.VMEM((TALL, 2 * HALF), jnp.float32),
        ],
        compiler_params=pltpu.CompilerParams(vmem_limit_bytes=24 * 1024 * 1024),
        name="attention_back",
    )(spans, queries, queries_t, logs, douts, douts_t, deltas, keys_g, values_g)


UNIT = 128
EXTRA = 16
CORE_ROWS = 12 * UNIT
X_ROWS = CORE_ROWS // 4
Y_ROWS = X_ROWS // 8


def axes():
    me = lax.axis_index("pts")
    core, z, y, x = me % 2, (me // 2) % 8, (me // 16) % 8, me // 128
    return (
        (core, 2, lambda r: x * 128 + y * 16 + z * 2 + r),
        (x, 4, lambda r: r * 128 + y * 16 + z * 2 + core),
        (y, 8, lambda r: x * 128 + r * 16 + z * 2 + core),
        (z, 8, lambda r: x * 128 + y * 16 + r * 2 + core),
    )


def far_first(size):
    return sorted(range(1, size), key=lambda k: -min(k, size - k))


def swap(axis, source, landing, sems, first):
    rank, size, device = axis
    copies = []
    for k in far_first(size):
        peer = (rank + k) % size
        copies.append(send(source(peer), landing(rank), sems, first + k - 1, device(peer)))
    return copies[::-1]


def wait_all(copies):
    for copy in copies:
        copy.wait()


def slot_sum(ref, start, size):
    total = ref[0, start : start + size, :].astype(jnp.float32)
    for r in range(1, ref.shape[0]):
        total = total + ref[r, start : start + size, :].astype(jnp.float32)
    return total


def finish_kernel(
    scale, hidden, dq, dk, dv, dmixed, points, gain, w_qkv, gw_out, gw_pool, gb_pool, g_gain,
    grad_points, reduced, extras,
    low_k, low_v, high_k, high_v, send_c, recv_c, extra_own, extra_in,
    send_x, recv_x, send_y, recv_y, recv_z, gather_c, sems,
):
    me, before, after = neighbours()
    on_core, on_x, on_y, on_z = axes()
    barrier = pltpu.get_barrier_semaphore()
    greeted = []
    for rank, size, device in (on_z, on_y, on_x, on_core):
        greeted += [device((rank + k) % size) for k in far_first(size)]
    greeted += [before, after]
    for device in greeted:
        pl.semaphore_signal(barrier, inc=1, device_id=(device,), device_id_type=MESH)

    def fill(block, first_unit):
        for column in range(block.shape[1] // UNIT):
            unit = first_unit + 2 * column
            start = unit % 12 * UNIT
            for part in range(2):
                at = start + part * UNIT
                rows = slice(at % X_ROWS, at % X_ROWS + UNIT)
                send_c[unit // 12, at // X_ROWS, rows, :] = block[
                    part * UNIT : (part + 1) * UNIT, column * UNIT : (column + 1) * UNIT
                ]

    fill(gw_out[...], 12)
    fill(gw_pool[...], 16)
    pieces = [gb_pool[:, i * UNIT : (i + 1) * UNIT] for i in range(4)]
    pieces += [g_gain[:, i * UNIT : (i + 1) * UNIT] for i in range(4)]
    pieces += [jnp.zeros((EXTRA - 8, UNIT), jnp.float32)]
    packed = jnp.concatenate(pieces, axis=0).astype(jnp.bfloat16)
    extra_own[...] = packed
    own = slice(PATCH, 2 * PATCH)
    fill((inner_rows(hidden[own, :], dq[...]) * scale).astype(jnp.bfloat16), 0)
    fill((inner_rows(hidden[...], dk[...]) * scale).astype(jnp.bfloat16), 4)
    fill((inner_rows(hidden[...], dv[...]) * scale).astype(jnp.bfloat16), 8)

    pl.semaphore_wait(barrier, len(greeted))
    core, core_device = on_core[0], on_core[2](1 - on_core[0])
    x, x_device = on_x[0], on_x[2]
    steps = (2, 1, 3, 0)
    quarters = [(x + k) % 4 for k in steps]
    extra_copy = send(extra_own, extra_in, sems, 57, core_device)
    core_copies = [
        send(send_c.at[1 - core, q], recv_c.at[q], sems, k, core_device) for k, q in enumerate(quarters)
    ]
    extra_copy.wait()
    extra = (extra_own[...].astype(jnp.float32) + extra_in[...].astype(jnp.float32)).astype(jnp.bfloat16)
    copies = []
    for k, q in enumerate(quarters):
        core_copies[k].wait()
        total = send_c[core, q].astype(jnp.float32) + recv_c[q].astype(jnp.float32)
        if k < 3:
            send_x[q, :X_ROWS, :] = total.astype(jnp.bfloat16)
            send_x[q, X_ROWS:, :] = extra
            copies.append(send(send_x.at[q], recv_x.at[x], sems, 4 + steps[k], x_device(q)))
        else:
            recv_x[x, :X_ROWS, :] = total.astype(jnp.bfloat16)
            recv_x[x, X_ROWS:, :] = extra
    rims = [
        send(dk.at[pl.ds(0, PATCH)], high_k, sems, 60, before),
        send(dv.at[pl.ds(0, PATCH)], high_v, sems, 61, before),
        send(dk.at[pl.ds(2 * PATCH, PATCH)], low_k, sems, 62, after),
        send(dv.at[pl.ds(2 * PATCH, PATCH)], low_v, sems, 63, after),
    ]
    dhidden = against_rows(dq[...], w_qkv[:, :256])
    normed, inv_std = layer_stats(points[...].astype(jnp.float32))
    wait_all(copies)
    extra = slot_sum(recv_x, X_ROWS, EXTRA).astype(jnp.bfloat16)
    for r in range(8):
        send_y[r, :Y_ROWS, :] = slot_sum(recv_x, r * Y_ROWS, Y_ROWS).astype(jnp.bfloat16)
        send_y[r, Y_ROWS:, :] = extra

    copies = swap(on_y, lambda r: send_y.at[r], lambda r: recv_y.at[r], sems, 8)
    recv_y[on_y[0]] = send_y[on_y[0]]
    wait_all(rims)
    for columns, mine, low, high in (
        (slice(256, 512), dk, low_k, high_k), (slice(512, 768), dv, low_v, high_v)
    ):
        total = mine[own, :].astype(jnp.float32) + low[...].astype(jnp.float32)
        total = (total + high[...].astype(jnp.float32)).astype(jnp.bfloat16)
        dhidden = dhidden + against_rows(total, w_qkv[:, columns])
    grad_points[...] = dmixed[...] + norm_back(dhidden * gain[...], normed, inv_std)
    wait_all(copies)
    recv_z[on_z[0]] = slot_sum(recv_y, 0, Y_ROWS + EXTRA).astype(jnp.bfloat16)

    wait_all(swap(on_z, lambda r: recv_z.at[on_z[0]], lambda r: recv_z.at[r], sems, 15))
    total = slot_sum(recv_z, 0, Y_ROWS + EXTRA)
    extras[...] = total[Y_ROWS:]
    y, y_device = on_y[0], on_y[2]
    gather_c[core, x, y] = total[:Y_ROWS].astype(jnp.bfloat16)
    order = (1, 7, 2, 6, 3, 5, 4)

    def pass_on(k):
        piece = gather_c.at[core, x, (y + 8 - k) % 8]
        return {i: send(piece, piece, sems, 28 + 3 * k + i, x_device((x + i) % 4)) for i in (2, 1, 3)}

    mine = gather_c.at[core, x, y]
    y_copies = {k: send(mine, mine, sems, 22 + k - 1, y_device((y + k) % 8)) for k in order[::-1]}
    x_copies = {0: pass_on(0)}
    for k in order:
        y_copies[k].wait()
        x_copies[k] = pass_on(k)
    core_copies = [send(gather_c.at[core, x], gather_c.at[core, x], sems, 53, core_device)]
    for i in (1, 3, 2):
        for k in (0,) + order:
            x_copies[k][i].wait()
        slot = gather_c.at[core, (x + 4 - i) % 4]
        core_copies.append(send(slot, slot, sems, 53 + i, core_device))
    wait_all(core_copies)
    for c in range(2):
        for r in range(4):
            for s in range(8):
                start = c * CORE_ROWS + r * X_ROWS + s * Y_ROWS
                reduced[start : start + Y_ROWS, :] = gather_c[c, r, s]
    weighted = jnp.zeros((256, UNIT), jnp.float32)
    for column in range(6):
        block = reduced[column * 256 : (column + 1) * 256, :].astype(jnp.float32)
        lanes = slice(column * UNIT, (column + 1) * UNIT)
        weighted = weighted + block * w_qkv[:, lanes].astype(jnp.float32)
    summed_gain = jnp.sum(weighted.T, axis=0, keepdims=True) / gain[...]
    for i in range(2):
        extras[8 + i : 9 + i, :] = summed_gain[:, i * UNIT : (i + 1) * UNIT]


def finish(scale, *arrays):
    half = jnp.bfloat16
    vmem = pl.BlockSpec(memory_space=pltpu.VMEM)
    return pl.pallas_call(
        functools.partial(finish_kernel, scale),
        out_shape=[
            jax.ShapeDtypeStruct((PATCH, 256), jnp.float32),
            jax.ShapeDtypeStruct((2 * CORE_ROWS, UNIT), half),
            jax.ShapeDtypeStruct((EXTRA, UNIT), jnp.float32),
        ],
        in_specs=[vmem] * 12,
        out_specs=[vmem] * 3,
        scratch_shapes=[pltpu.VMEM((PATCH, 256), half)] * 4
        + [
            pltpu.VMEM((2, 4, X_ROWS, UNIT), half),
            pltpu.VMEM((4, X_ROWS, UNIT), half),
            pltpu.VMEM((EXTRA, UNIT), half),
            pltpu.VMEM((EXTRA, UNIT), half),
            pltpu.VMEM((4, X_ROWS + EXTRA, UNIT), half),
            pltpu.VMEM((4, X_ROWS + EXTRA, UNIT), half),
            pltpu.VMEM((8, Y_ROWS + EXTRA, UNIT), half),
            pltpu.VMEM((8, Y_ROWS + EXTRA, UNIT), half),
            pltpu.VMEM((8, Y_ROWS + EXTRA, UNIT), half),
            pltpu.VMEM((2, 4, 8, Y_ROWS, UNIT), half),
            pltpu.SemaphoreType.DMA((2, 64)),
        ],
        compiler_params=pltpu.CompilerParams(
            collective_id=3, has_side_effects=True, vmem_limit_bytes=40 * 1024 * 1024
        ),
        name="finish",
    )(*arrays)


def unpack_kernel(reduced, extras, rows_in, gq, go, gn, gp, gb, gg, rows_out, sem):
    copy = pltpu.make_async_copy(rows_in, rows_out, sem)
    copy.start()
    for column in range(12):
        block = reduced[column * 256 : (column + 1) * 256, :].astype(jnp.float32)
        if column < 6:
            gq[:, column * UNIT : (column + 1) * UNIT] = block
        elif column < 8:
            go[:, (column - 6) * UNIT : (column - 5) * UNIT] = block
        else:
            gp[:, (column - 8) * UNIT : (column - 7) * UNIT] = block
    for i in range(2):
        gn[:, i * UNIT : (i + 1) * UNIT] = extras[8 + i : 9 + i, :]
    for i in range(4):
        gb[:, i * UNIT : (i + 1) * UNIT] = extras[i : i + 1, :]
        gg[:, i * UNIT : (i + 1) * UNIT] = extras[4 + i : 5 + i, :]
    copy.wait()


def unpack(reduced, extras, rows):
    vmem = pl.BlockSpec(memory_space=pltpu.VMEM)
    outside = pl.BlockSpec(memory_space=pl.ANY)
    shapes = ((256, 768), (256, 256), (1, 256), (256, 512), (1, 512), (1, 512), (PATCH, 256))
    return pl.pallas_call(
        unpack_kernel,
        out_shape=[jax.ShapeDtypeStruct(shape, jnp.float32) for shape in shapes],
        in_specs=[vmem, vmem, vmem],
        out_specs=[vmem] * 6 + [outside],
        scratch_shapes=[pltpu.SemaphoreType.DMA],
        compiler_params=pltpu.CompilerParams(vmem_limit_bytes=16 * 1024 * 1024),
        name="unpack",
    )(reduced, extras, rows)


def body(
    points, patch_ids, cell_ids, norm_gain, w_qkv, w_out, w_pool, b_pool, pool_gain, cotangent
):
    scale = 1.0 / math.sqrt(points.shape[0] * lax.axis_size("pts"))
    gain = norm_gain[None]
    cells = cell_ids.reshape(4, HALF)
    far = [
        pltpu.with_memory_space_constraint(array, pltpu.HBM)
        for array in (points, patch_ids.reshape(4, HALF), gain, w_qkv, w_out, cells)
    ]
    queries, queries_t, keys_g, values_g, marks_f, hidden, spans = prepare(*far[:4])
    attended, logs, sums, counts = attend(
        spans, queries_t, marks_f, keys_g, values_g, far[0], far[4], far[5]
    )
    dmixed, datt, datt_t, deltas, gw_pool, gw_out, gb_pool, g_gain = pool(
        scale, sums, counts, cells, attended, w_out, w_pool, b_pool[None], pool_gain[None], cotangent
    )
    dq, dk, dv = attend_back(
        spans, queries, queries_t, logs, datt, datt_t, deltas, keys_g, values_g
    )
    grad_points, reduced, extras = finish(
        scale, hidden, dq, dk, dv, dmixed, points, gain, w_qkv, gw_out, gw_pool, gb_pool, g_gain
    )
    gq, go, gn, gp, gb, gg, grad_points = unpack(reduced, extras, grad_points)
    return (grad_points, gq, go, gn[0], gp, gb[0], gg[0])


def solution(mesh):
    in_specs = (P("pts", None), P("pts"), P("pts"), P(), P(), P(), P(), P(), P(), P("pts", None))
    out_specs = (P("pts", None), P(), P(), P(), P(), P(), P())
    return jax.shard_map(body, mesh=mesh, in_specs=in_specs, out_specs=out_specs, check_vma=False)
```

```python
import functools
import math

import jax
import jax.numpy as jnp
from jax import lax
from jax.experimental import pallas as pl
from jax.experimental.pallas import tpu as pltpu
from jax.sharding import PartitionSpec as P

PATCH = 512
MESH = pl.DeviceIdType.MESH


EPS = 1e-05
ROOT_HALF = 0.7071067811865476
ROOT_TWO_PI = 2.5066282746310002


def layer_stats(values):
    centered = values - jnp.mean(values, axis=-1, keepdims=True)
    inv_std = lax.rsqrt(jnp.mean(centered * centered, axis=-1, keepdims=True) + EPS)
    return (centered * inv_std, inv_std)


def norm_back(grad_normed, normed, inv_std):
    first_mean = jnp.mean(grad_normed, axis=-1, keepdims=True)
    second_mean = jnp.mean(grad_normed * normed, axis=-1, keepdims=True)
    return inv_std * (grad_normed - first_mean - normed * second_mean)


def gelu_slope(scaled):
    normal_cdf = 0.5 * (1.0 + lax.erf(scaled * ROOT_HALF))
    return normal_cdf + scaled * jnp.exp(-0.5 * scaled * scaled) / ROOT_TWO_PI


def inner_rows(left, right):
    return lax.dot_general(
        left, right, (((0,), (0,)), ((), ())), preferred_element_type=jnp.float32
    )


def against_rows(left, right):
    return lax.dot_general(
        left, right, (((1,), (1,)), ((), ())), preferred_element_type=jnp.float32
    )


HALF = 128
PER_HALF = 8
HEAD_SIZE = 16
TILE = 128
CHUNK = 528
TALL = 3 * CHUNK
TILES = PATCH // TILE
PAIR = 256 // TILE
WINDOW = 3 * PATCH
FAR = float(2**30)
DIGIT = 32
LOG_LANE = 64


def head_mask(h, axis):
    shape = (1, 2 * HALF) if axis else (2 * HALF, 1)
    place = lax.broadcasted_iota(jnp.int32, shape, axis)
    own = (place >= h * HEAD_SIZE) & (place < (h + 1) * HEAD_SIZE)
    marks = (place >= HALF) & (place < HALF + LOG_LANE)
    terms = (place >= HALF + LOG_LANE) & (place < HALF + LOG_LANE + 24) & (place % PER_HALF == h)
    return (own | marks | terms).astype(jnp.float32).astype(jnp.bfloat16)


def split_three(values, which):
    first = values.astype(jnp.bfloat16).astype(jnp.float32)
    second = (values - first).astype(jnp.bfloat16).astype(jnp.float32)
    third = values - first - second
    return jnp.where(which == 0, first, jnp.where(which == 1, second, third))


def neighbours():
    me = lax.axis_index("pts")
    count = lax.axis_size("pts")
    return me, (me + count - 1) % count, (me + 1) % count


def greet_neighbours(before, after):
    barrier = pltpu.get_barrier_semaphore()
    for device in (before, after):
        pl.semaphore_signal(barrier, inc=1, device_id=(device,), device_id_type=MESH)
    pl.semaphore_wait(barrier, 2)


def send(source, landing, sems, index, device):
    copy = pltpu.make_async_remote_copy(
        src_ref=source,
        dst_ref=landing,
        send_sem=sems.at[0, index],
        recv_sem=sems.at[1, index],
        device_id=(device,),
        device_id_type=MESH,
    )
    copy.start()
    return copy


def digit_columns(marks):
    row = lax.broadcasted_iota(jnp.int32, (HALF, HALF), 0)
    high, low = marks // DIGIT, marks % DIGIT
    hit = ((row < DIGIT) & (row == high)) | ((row >= DIGIT) & (row < LOG_LANE) & (row - DIGIT == low))
    return hit.astype(jnp.float32)


def prepare_kernel(
    points_hbm, ids_hbm, gain_hbm, w_hbm, q_ref, qt_ref, kg_ref, vg_ref, f_ref, hidden_ref, spans_ref,
    points, ids, gain, w_qkv, marks, marks_low, marks_high, rows_low, rows_high, sems, local_sems,
):
    me, before, after = neighbours()
    local = []
    for i, (source, target) in enumerate(
        ((ids_hbm, ids), (points_hbm, points), (w_hbm, w_qkv), (gain_hbm, gain))
    ):
        local.append(pltpu.make_async_copy(source, target, local_sems.at[i]))
        local[-1].start()
    marks[...] = jnp.zeros_like(marks)
    greet_neighbours(before, after)
    local[0].wait()
    marks[:4, :] = ids[...] + 1
    local[1].wait()
    copies = [send(marks, marks_high, sems, 0, before), send(marks, marks_low, sems, 1, after)]
    parts = [pl.ds(i * TILE * 2, TILE * 2) for i in range(2)]
    halo = []
    for i, part in enumerate(parts):
        halo.append(
            (
                send(points.at[part], rows_high.at[part], sems, 2 + 2 * i, before),
                send(points.at[part], rows_low.at[part], sems, 3 + 2 * i, after),
            )
        )
    local[2].wait()
    local[3].wait()

    def project(block, first, columns):
        normed, _ = layer_stats(block.astype(jnp.float32))
        hidden = (normed * gain[...]).astype(jnp.bfloat16)
        hidden_ref[first : first + block.shape[0], :] = hidden
        return jnp.dot(hidden, w_qkv[:, columns], preferred_element_type=jnp.float32)

    def place(first, keys, values):
        for g in range(2):
            lanes = slice(g * HALF, (g + 1) * HALF)
            rows = slice(first, first + keys.shape[0])
            kg_ref[g, rows, :HALF] = keys[:, lanes].astype(jnp.bfloat16)
            vg_ref[g, rows, :HALF] = values[:, lanes].astype(jnp.bfloat16)

    def place_marks(block, first, own):
        lane = lax.broadcasted_iota(jnp.int32, (HALF, HALF), 1)
        row = lax.broadcasted_iota(jnp.int32, (HALF, HALF), 0)
        terms = (lane >= LOG_LANE) & (lane < LOG_LANE + 24)
        for i in range(4):
            rows = slice(first + i * HALF, first + (i + 1) * HALF)
            digits = digit_columns(block[i : i + 1, :])
            both = jnp.where(terms, 1.0, digits.T).astype(jnp.bfloat16)
            for g in range(2):
                kg_ref[g, rows, HALF:] = both
                vg_ref[g, rows, HALF:] = both
            if own:
                away = jnp.where(row < LOG_LANE, (1.0 - digits) * -FAR, 0.0)
                f_ref[:, i * HALF : (i + 1) * HALF] = away.astype(jnp.bfloat16)

    qkv = project(points[...], PATCH, slice(None))
    queries = qkv[:, :256].astype(jnp.bfloat16).astype(jnp.float32) * 0.25
    q_ref[...] = queries.astype(jnp.bfloat16)
    qt_ref[...] = queries.T.astype(jnp.bfloat16)
    place(PATCH, qkv[:, 256:512], qkv[:, 512:])
    own = marks[...]
    place_marks(own, PATCH, True)
    lane = lax.broadcasted_iota(jnp.int32, (TALL - WINDOW, 2 * HALF), 1)
    nowhere = ((lane == HALF) | (lane == HALF + DIGIT)).astype(jnp.float32).astype(jnp.bfloat16)
    for g in range(2):
        kg_ref[g, WINDOW:, :] = nowhere
        vg_ref[g, WINDOW:, :] = nowhere
    for copy in copies:
        copy.wait()
    low = jnp.where(me == 0, 0, marks_low[...])
    high = jnp.where(me == lax.axis_size("pts") - 1, 0, marks_high[...])
    place_marks(low, 0, False)
    place_marks(high, 2 * PATCH, False)
    own_f, low_f, high_f = (block[:4].astype(jnp.float32) for block in (own, low, high))
    for t in range(TILES):
        ours = own_f[t * TILE // HALF : (t + 1) * TILE // HALF]
        first, last = jnp.min(ours), jnp.max(ours)
        lower = jnp.sum((low_f < first).astype(jnp.float32) + (own_f < first).astype(jnp.float32))
        upper = jnp.sum(
            ((high_f > 0) & (high_f <= last)).astype(jnp.float32) + (own_f <= last).astype(jnp.float32)
        )
        lower = lower.astype(jnp.int32) // 16 * 16
        count = (PATCH + upper.astype(jnp.int32) - lower + CHUNK - 1) // CHUNK
        spans_ref[t, 0] = jnp.minimum(lower, TALL - count * CHUNK)
        spans_ref[t, 1] = count
    for part, (high_copy, low_copy) in zip(parts, halo):
        for copy, block, first in ((low_copy, rows_low, 0), (high_copy, rows_high, 2 * PATCH)):
            copy.wait()
            kv = project(block[part, :], first + part.start, slice(256, 768))
            place(first + part.start, kv[:, :256], kv[:, 256:])


def prepare(points, ids, gain, w_qkv):
    half = jnp.bfloat16
    vmem = pl.BlockSpec(memory_space=pltpu.VMEM)
    return pl.pallas_call(
        prepare_kernel,
        out_shape=[
            jax.ShapeDtypeStruct((PATCH, 256), half),
            jax.ShapeDtypeStruct((256, PATCH), half),
            jax.ShapeDtypeStruct((2, TALL, 2 * HALF), half),
            jax.ShapeDtypeStruct((2, TALL, 2 * HALF), half),
            jax.ShapeDtypeStruct((HALF, PATCH), half),
            jax.ShapeDtypeStruct((WINDOW, 256), half),
            jax.ShapeDtypeStruct((TILES, 2), jnp.int32),
        ],
        in_specs=[pl.BlockSpec(memory_space=pltpu.HBM)] * 4,
        out_specs=[vmem] * 6 + [pl.BlockSpec(memory_space=pltpu.SMEM)],
        scratch_shapes=[
            pltpu.VMEM((PATCH, 256), half),
            pltpu.VMEM((4, HALF), jnp.int32),
            pltpu.VMEM((1, 256), jnp.float32),
            pltpu.VMEM((256, 768), half),
            pltpu.VMEM((8, HALF), jnp.int32),
            pltpu.VMEM((8, HALF), jnp.int32),
            pltpu.VMEM((8, HALF), jnp.int32),
            pltpu.VMEM((PATCH, 256), half),
            pltpu.VMEM((PATCH, 256), half),
            pltpu.SemaphoreType.DMA((2, 6)),
            pltpu.SemaphoreType.DMA((4,)),
        ],
        compiler_params=pltpu.CompilerParams(
            collective_id=1, has_side_effects=True, vmem_limit_bytes=32 * 1024 * 1024
        ),
        name="prepare",
    )(points, ids, gain, w_qkv)


SLOTS = 144


def membership(cells):
    local = cells - lax.axis_index("pts") * HALF
    local = jnp.where(local < 0, HALF, local)
    slot = lax.broadcasted_iota(jnp.int32, (SLOTS, HALF), 0)
    parts = [(slot == local[i : i + 1, :]).astype(jnp.float32) for i in range(4)]
    return jnp.concatenate(parts, axis=1)


def tall_max(scores):
    part = CHUNK // 6
    folded = scores[:part]
    for i in range(1, 6):
        folded = jnp.maximum(folded, scores[i * part : (i + 1) * part])
    return jnp.max(folded, axis=0, keepdims=True)


def block_of(index, size):
    return pl.ds(pl.multiple_of(index * size, size), size)


def forward_kernel(
    spans, qt_ref, f_ref, kg_ref, vg_ref, points_hbm, w_out_hbm, cells_hbm,
    att_ref, logs_ref, sums_ref, counts_ref, qt, kept, att_t, top_t, total_t, points, w_out, cells, sems,
):
    late = [
        pltpu.make_async_copy(source, target, sems.at[i])
        for i, (source, target) in enumerate(
            ((points_hbm, points), (w_out_hbm, w_out), (cells_hbm, cells))
        )
    ]
    for copy in late:
        copy.start()
    qt[...] = jnp.zeros_like(qt)

    def step(index, carry):
        forward_step(
            index, spans, qt_ref, f_ref, kg_ref, vg_ref, att_ref, logs_ref,
            qt, kept, att_t, top_t, total_t,
        )
        return carry

    lax.fori_loop(0, TILES, step, 0)
    for copy in late:
        copy.wait()
    mixed = points[...].astype(jnp.float32) + jnp.dot(
        att_ref[...], w_out[...], preferred_element_type=jnp.float32
    )
    member = membership(cells[...])
    sums_ref[...] = jnp.dot(
        member.astype(jnp.bfloat16), mixed.astype(jnp.bfloat16), preferred_element_type=jnp.float32
    )
    counts_ref[...] = jnp.broadcast_to(jnp.sum(member, axis=1, keepdims=True), (SLOTS, HALF))


PAIRS = PER_HALF // PAIR


def forward_step(
    tile, spans, qt_ref, f_ref, kg_ref, vg_ref, att_ref, logs_ref, qt, kept, att_t, top_t, total_t
):
    start, count = spans[tile, 0], spans[tile, 1]
    mine = block_of(tile, TILE)
    marks = f_ref[:LOG_LANE, mine]
    for half in range(2):
        queries_t = qt_ref[half * HALF : (half + 1) * HALF, mine]
        for h in range(PER_HALF):
            p, place = half * PAIRS + h // PAIR, slice(h % PAIR * TILE, (h % PAIR + 1) * TILE)
            own = slice(h * HEAD_SIZE, (h + 1) * HEAD_SIZE)
            qt[p, own, place] = queries_t[own]
            qt[p, HALF : HALF + LOG_LANE, place] = marks
    top_t[...] = jnp.full_like(top_t, -3e38)
    total_t[...] = jnp.zeros_like(total_t)
    att_t[...] = jnp.zeros_like(att_t)

    def chunk(c, carry):
        rows = pl.ds(pl.multiple_of(start + c * CHUNK, 16), CHUNK)
        ones = jnp.ones((16, CHUNK), jnp.bfloat16)
        tops, values_t = [], []
        for half in range(2):
            values_t.append(vg_ref[half, rows, :HALF].astype(jnp.float32).T.astype(jnp.bfloat16))
            for p in range(half * PAIRS, (half + 1) * PAIRS):
                scores = jnp.dot(kg_ref[half, rows, :], qt[p], preferred_element_type=jnp.float32)
                kept[p] = scores
                tops.append(jnp.maximum(top_t[p : p + 1, :], tall_max(scores)))
        for p in range(2 * PAIRS):
            before, top = top_t[p : p + 1, :], tops[p]
            weights = jnp.exp(kept[p] - top).astype(jnp.bfloat16)
            decay = jnp.exp(before - top)
            top_t[p : p + 1, :] = top
            size = PAIR * HEAD_SIZE
            own, inner = slice(p * size, (p + 1) * size), slice(p % PAIRS * size, (p % PAIRS + 1) * size)
            left = jnp.concatenate([values_t[p // PAIRS][inner], ones], axis=0)
            mixed = jnp.dot(left, weights, preferred_element_type=jnp.float32)
            total_t[p : p + 1, :] = total_t[p : p + 1, :] * decay + mixed[size : size + 1]
            att_t[own, :] = att_t[own, :] * decay + mixed[:size]
        return carry

    lax.fori_loop(0, count, chunk, 0)
    logs_p = -(top_t[...] + jnp.log(total_t[...]))
    spare = jnp.zeros((HALF - LOG_LANE - 24, TILE), jnp.float32)
    for half in range(2):
        parts, logs = [], []
        for h in range(half * PER_HALF, (half + 1) * PER_HALF):
            p, columns = h // PAIR, slice(h % PAIR * TILE, (h % PAIR + 1) * TILE)
            piece = att_t[h * HEAD_SIZE : (h + 1) * HEAD_SIZE, columns]
            parts.append(piece / total_t[p : p + 1, columns])
            logs.append(logs_p[p : p + 1, columns])
        lanes = slice(half * HALF, (half + 1) * HALF)
        att_ref[mine, lanes] = jnp.concatenate(parts, axis=0).T.astype(jnp.bfloat16)
        logs = jnp.concatenate(logs, axis=0)
        terms = [split_three(logs, i) for i in range(3)]
        ending = jnp.concatenate(terms + [spare], axis=0).astype(jnp.bfloat16)
        logs_ref[lanes, mine] = jnp.concatenate([marks, ending], axis=0)


def attend(spans, queries_t, marks_f, keys_g, values_g, points, w_out, cells):
    vmem = pl.BlockSpec(memory_space=pltpu.VMEM)
    outside = pl.BlockSpec(memory_space=pltpu.HBM)
    return pl.pallas_call(
        forward_kernel,
        out_shape=[
            jax.ShapeDtypeStruct((PATCH, 256), jnp.bfloat16),
            jax.ShapeDtypeStruct((256, PATCH), jnp.bfloat16),
            jax.ShapeDtypeStruct((SLOTS, 256), jnp.float32),
            jax.ShapeDtypeStruct((SLOTS, HALF), jnp.float32),
        ],
        in_specs=[pl.BlockSpec(memory_space=pltpu.SMEM)] + [vmem] * 4 + [outside] * 3,
        out_specs=[vmem] * 4,
        scratch_shapes=[
            pltpu.VMEM((2 * PAIRS, 2 * HALF, PAIR * TILE), jnp.bfloat16),
            pltpu.VMEM((2 * PAIRS, CHUNK, PAIR * TILE), jnp.float32),
            pltpu.VMEM((2 * HALF, PAIR * TILE), jnp.float32),
            pltpu.VMEM((2 * PAIRS, PAIR * TILE), jnp.float32),
            pltpu.VMEM((2 * PAIRS, PAIR * TILE), jnp.float32),
            pltpu.VMEM((PATCH, 256), jnp.bfloat16),
            pltpu.VMEM((256, 256), jnp.bfloat16),
            pltpu.VMEM((4, HALF), jnp.int32),
            pltpu.SemaphoreType.DMA((3,)),
        ],
        compiler_params=pltpu.CompilerParams(vmem_limit_bytes=24 * 1024 * 1024),
        name="attention",
    )(spans, queries_t, marks_f, keys_g, values_g, points, w_out, cells)


def pool_kernel(
    scale, sums, counts, cells, att, w_out, w_pool, b_pool, pool_gain, cotangent,
    dmixed_ref, datt_ref, datt_t_ref, delta_ref, gw_pool, gw_out, gb_pool, g_gain,
    back_pack, ahead_pack, from_after, from_before, sems,
):
    me, before, after = neighbours()
    back_pack[:, :256] = sums[HALF : HALF + 8, :]
    back_pack[:, 256:] = counts[HALF : HALF + 8, :]
    ahead_pack[:, :256] = sums[HALF - 8 : HALF, :]
    ahead_pack[:, 256:384] = counts[HALF - 8 : HALF, :]
    ahead_pack[:, 384:] = cotangent[HALF - 8 :, :]
    greet_neighbours(before, after)
    copies = [
        send(back_pack, from_after, sems, 0, before),
        send(ahead_pack, from_before, sems, 1, after),
    ]
    member = membership(cells[...]).astype(jnp.bfloat16)
    early_rows = HALF - 16

    def cells_back(sums, counts, cotangent):
        pooled_mean = (sums / counts).astype(jnp.bfloat16)
        pre_norm = jnp.dot(pooled_mean, w_pool[...], preferred_element_type=jnp.float32) + b_pool[...]
        pooled_normed, pooled_inv = layer_stats(pre_norm)
        slope_grad = cotangent * gelu_slope(pooled_normed * pool_gain[...])
        grad_pre = norm_back(slope_grad * pool_gain[...], pooled_normed, pooled_inv)
        grad_pre_b = grad_pre.astype(jnp.bfloat16)
        share = against_rows(grad_pre_b, w_pool[...]) / counts
        return pooled_mean, pooled_normed, slope_grad, grad_pre, grad_pre_b, share

    early_back = cells_back(
        sums[:early_rows, :], counts[:early_rows, :1], cotangent[:early_rows, :]
    )
    for copy in copies:
        copy.wait()
    row = lax.broadcasted_iota(jnp.int32, (8, 1), 0)
    late, early = from_after[0:1, :], from_before[7:8, :]
    last_sum = sums[HALF - 8 : HALF, :] + jnp.where(row == 7, late[:, :256], 0.0)
    lead_sum = jnp.where(row == 0, sums[HALF : HALF + 8, :] + early[:, :256], 0.0)
    last_count = counts[HALF - 8 : HALF, :] + jnp.where(row == 7, late[:, 256:], 0.0)
    lead_count = jnp.where(row == 0, counts[HALF : HALF + 8, :] + early[:, 256:384], 0.0)
    spare = jnp.zeros((8, 256), jnp.float32)
    middle = slice(early_rows, HALF - 8)
    late_sums = jnp.concatenate([sums[middle, :], last_sum, lead_sum, spare], axis=0)
    late_counts = jnp.concatenate(
        [counts[middle, :], last_count, lead_count, spare[:, :HALF]], axis=0
    )[:, :1]
    lead_cot = jnp.where(row == 0, early[:, 384:], 0.0)
    late_cot = jnp.concatenate(
        [cotangent[early_rows:, :], lead_cot, jnp.zeros((8, 512), jnp.float32)], axis=0
    )
    late_back = cells_back(late_sums, jnp.maximum(late_counts, 1.0), late_cot)
    pooled_mean, pooled_normed, slope_grad, grad_pre, grad_pre_b, share = (
        jnp.concatenate(pair, axis=0) for pair in zip(early_back, late_back)
    )
    share_b = share.astype(jnp.bfloat16)
    rest_b = (share - share_b.astype(jnp.float32)).astype(jnp.bfloat16)
    dmixed_main = inner_rows(member, share_b)
    dmixed_ref[...] = dmixed_main + inner_rows(member, rest_b)
    dmixed_b = dmixed_main.astype(jnp.bfloat16)
    datt = against_rows(dmixed_b, w_out[...]).astype(jnp.bfloat16)
    datt_f = datt.astype(jnp.float32)
    datt_ref[...] = (datt_f * 0.25).astype(jnp.bfloat16)
    product = datt_f * att[...].astype(jnp.float32)
    datt_t = against_rows(w_out[...], dmixed_b).astype(jnp.bfloat16).astype(jnp.float32)
    datt_t_ref[...] = (datt_t * 0.25).astype(jnp.bfloat16)
    slot = lax.broadcasted_iota(jnp.int32, (256, 256), 0)
    channel = lax.broadcasted_iota(jnp.int32, (256, 256), 1)
    spot = slot % HALF - LOG_LANE
    place = (channel // HALF == slot // HALF) & (spot >= 0) & (spot < 24)
    place = (place & (spot % PER_HALF == channel % HALF // HEAD_SIZE)).astype(jnp.float32)
    place = place.astype(jnp.bfloat16)
    first = product.astype(jnp.bfloat16)
    second = product - first.astype(jnp.float32)
    second_b = second.astype(jnp.bfloat16)
    third_b = (second - second_b.astype(jnp.float32)).astype(jnp.bfloat16)
    deltas = against_rows(place, first) + against_rows(place, second_b) + against_rows(place, third_b)
    which = (lax.broadcasted_iota(jnp.int32, (256, 1), 0) % HALF - LOG_LANE) // PER_HALF
    delta_ref[...] = split_three(deltas * -0.25, which).astype(jnp.bfloat16)
    gw_pool[...] = (inner_rows(pooled_mean[:HALF], grad_pre_b[:HALF]) * scale).astype(jnp.bfloat16)
    gw_out[...] = (inner_rows(att[...], dmixed_b) * scale).astype(jnp.bfloat16)
    gb_pool[...] = jnp.sum(grad_pre[:HALF], axis=0, keepdims=True) * scale
    g_gain[...] = jnp.sum(slope_grad[:HALF] * pooled_normed[:HALF], axis=0, keepdims=True) * scale


def pool(scale, *arrays):
    half = jnp.bfloat16
    vmem = pl.BlockSpec(memory_space=pltpu.VMEM)
    return pl.pallas_call(
        functools.partial(pool_kernel, scale),
        out_shape=[
            jax.ShapeDtypeStruct((PATCH, 256), jnp.float32),
            jax.ShapeDtypeStruct((PATCH, 256), half),
            jax.ShapeDtypeStruct((256, PATCH), half),
            jax.ShapeDtypeStruct((256, PATCH), half),
            jax.ShapeDtypeStruct((256, 512), half),
            jax.ShapeDtypeStruct((256, 256), half),
            jax.ShapeDtypeStruct((1, 512), jnp.float32),
            jax.ShapeDtypeStruct((1, 512), jnp.float32),
        ],
        in_specs=[vmem] * 9,
        out_specs=[vmem] * 8,
        scratch_shapes=[
            pltpu.VMEM((8, 384), jnp.float32),
            pltpu.VMEM((8, 896), jnp.float32),
            pltpu.VMEM((8, 384), jnp.float32),
            pltpu.VMEM((8, 896), jnp.float32),
            pltpu.SemaphoreType.DMA((2, 2)),
        ],
        compiler_params=pltpu.CompilerParams(
            collective_id=2, has_side_effects=True, vmem_limit_bytes=32 * 1024 * 1024
        ),
        name="pooling",
    )(*arrays)


def backward_kernel(
    spans, q_ref, qt_ref, logs_ref, do_ref, dot_ref, deltas_ref, kg_ref, vg_ref,
    dq_ref, dk_ref, dv_ref, qt, dt, qn, dn, some, slopes, dqt, dk_sum, dv_sum,
):
    qt[...] = jnp.zeros_like(qt)
    dt[...] = jnp.zeros_like(dt)
    dk_sum[...] = jnp.zeros_like(dk_sum)
    dv_sum[...] = jnp.zeros_like(dv_sum)

    def step(tile, carry):
        backward_step(
            tile, spans, q_ref, qt_ref, logs_ref, do_ref, dot_ref, deltas_ref, kg_ref, vg_ref,
            dq_ref, qt, dt, qn, dn, some, slopes, dqt, dk_sum, dv_sum,
        )
        return carry

    lax.fori_loop(0, TILES, step, 0)
    dk_ref[...] = (dk_sum[:WINDOW] * 4.0).astype(jnp.bfloat16)
    dv_ref[...] = (dv_sum[:WINDOW] * 4.0).astype(jnp.bfloat16)


def backward_step(
    tile, spans, q_ref, qt_ref, logs_ref, do_ref, dot_ref, deltas_ref, kg_ref, vg_ref,
    dq_ref, qt, dt, qn, dn, some, slopes, dqt, dk_sum, dv_sum,
):
    start, count = spans[tile, 0], spans[tile, 1]
    mine = block_of(tile, TILE)
    after = HALF + LOG_LANE
    halves = [slice(half * HALF, (half + 1) * HALF) for half in range(2)]
    for half, turned in enumerate(halves):
        queries, douts = q_ref[mine, turned], do_ref[mine, turned]
        queries_t, douts_t = qt_ref[turned, mine], dot_ref[turned, mine]
        logs, deltas = logs_ref[turned, mine], deltas_ref[turned, mine]
        for h in range(PER_HALF):
            p, place = half * PAIRS + h // PAIR, slice(h % PAIR * TILE, (h % PAIR + 1) * TILE)
            own = slice(h * HEAD_SIZE, (h + 1) * HEAD_SIZE)
            terms = head_mask(h, 0)[after : after + 32]
            qt[p, own, place] = queries_t[own]
            qt[p, HALF:after, place] = logs[:LOG_LANE]
            qt[p, after : after + 32, place] = logs[LOG_LANE : LOG_LANE + 32] * terms
            dt[p, own, place] = douts_t[own]
            dt[p, after : after + 32, place] = deltas[LOG_LANE : LOG_LANE + 32] * terms
            lanes = head_mask(h, 1)[:, :HALF]
            qn[p, place, :] = queries * lanes
            dn[p, place, :] = douts * lanes
    dqt[...] = jnp.zeros_like(dqt)
    width = PAIR * TILE

    def chunk(c, carry):
        rows = pl.ds(pl.multiple_of(start + c * CHUNK, 16), CHUNK)
        keys_t = []
        for half in range(2):
            keys_t.append(kg_ref[half, rows, :HALF].astype(jnp.float32).T.astype(jnp.bfloat16))
            for p in range(half * PAIRS, (half + 1) * PAIRS):
                weights = jnp.exp(
                    jnp.dot(kg_ref[half, rows, :], qt[p], preferred_element_type=jnp.float32)
                )
                dweights = jnp.dot(vg_ref[half, rows, :], dt[p], preferred_element_type=jnp.float32)
                place = slice(p * width, (p + 1) * width)
                some[:, place] = weights.astype(jnp.bfloat16)
                slopes[:, place] = (weights * dweights).astype(jnp.bfloat16)
        depth = PAIRS * width
        for half, lanes in enumerate(halves):
            place, pairs = slice(half * depth, (half + 1) * depth), slice(half * PAIRS, (half + 1) * PAIRS)
            dk_sum[rows, lanes] += jnp.dot(
                slopes[:, place], qn[pairs].reshape(depth, HALF), preferred_element_type=jnp.float32
            )
            dv_sum[rows, lanes] += jnp.dot(
                some[:, place], dn[pairs].reshape(depth, HALF), preferred_element_type=jnp.float32
            )
        size = PAIR * HEAD_SIZE
        for p in range(2 * PAIRS):
            inner = slice(p % PAIRS * size, (p % PAIRS + 1) * size)
            dqt[p * size : (p + 1) * size, :] += jnp.dot(
                keys_t[p // PAIRS][inner],
                slopes[:, p * width : (p + 1) * width],
                preferred_element_type=jnp.float32,
            )
        return carry

    lax.fori_loop(0, count, chunk, 0)
    for half, turned in enumerate(halves):
        parts = []
        for h in range(half * PER_HALF, (half + 1) * PER_HALF):
            place = slice(h % PAIR * TILE, (h % PAIR + 1) * TILE)
            parts.append(dqt[h * HEAD_SIZE : (h + 1) * HEAD_SIZE, place])
        dq_ref[mine, turned] = jnp.concatenate(parts, axis=0).T.astype(jnp.bfloat16)


def attend_back(spans, queries, queries_t, logs, douts, douts_t, deltas, keys_g, values_g):
    vmem = pl.BlockSpec(memory_space=pltpu.VMEM)
    half = jnp.bfloat16
    return pl.pallas_call(
        backward_kernel,
        out_shape=[
            jax.ShapeDtypeStruct((PATCH, 256), half),
            jax.ShapeDtypeStruct((WINDOW, 256), half),
            jax.ShapeDtypeStruct((WINDOW, 256), half),
        ],
        in_specs=[pl.BlockSpec(memory_space=pltpu.SMEM)] + [vmem] * 8,
        out_specs=[vmem] * 3,
        scratch_shapes=[
            pltpu.VMEM((2 * PAIRS, 2 * HALF, PAIR * TILE), half),
            pltpu.VMEM((2 * PAIRS, 2 * HALF, PAIR * TILE), half),
            pltpu.VMEM((2 * PAIRS, PAIR * TILE, HALF), half),
            pltpu.VMEM((2 * PAIRS, PAIR * TILE, HALF), half),
            pltpu.VMEM((CHUNK, 2 * PAIRS * PAIR * TILE), half),
            pltpu.VMEM((CHUNK, 2 * PAIRS * PAIR * TILE), half),
            pltpu.VMEM((2 * HALF, PAIR * TILE), jnp.float32),
            pltpu.VMEM((TALL, 2 * HALF), jnp.float32),
            pltpu.VMEM((TALL, 2 * HALF), jnp.float32),
        ],
        compiler_params=pltpu.CompilerParams(vmem_limit_bytes=24 * 1024 * 1024),
        name="attention_back",
    )(spans, queries, queries_t, logs, douts, douts_t, deltas, keys_g, values_g)


UNIT = 128
EXTRA = 16
CORE_ROWS = 12 * UNIT
X_ROWS = CORE_ROWS // 4
Y_ROWS = X_ROWS // 8


def axes():
    me = lax.axis_index("pts")
    core, z, y, x = me % 2, (me // 2) % 8, (me // 16) % 8, me // 128
    return (
        (core, 2, lambda r: x * 128 + y * 16 + z * 2 + r),
        (x, 4, lambda r: r * 128 + y * 16 + z * 2 + core),
        (y, 8, lambda r: x * 128 + r * 16 + z * 2 + core),
        (z, 8, lambda r: x * 128 + y * 16 + r * 2 + core),
    )


def far_first(size):
    return sorted(range(1, size), key=lambda k: -min(k, size - k))


def swap(axis, source, landing, sems, first):
    rank, size, device = axis
    copies = []
    for k in far_first(size):
        peer = (rank + k) % size
        copies.append(send(source(peer), landing(rank), sems, first + k - 1, device(peer)))
    return copies[::-1]


def wait_all(copies):
    for copy in copies:
        copy.wait()


def slot_sum(ref, start, size):
    total = ref[0, start : start + size, :].astype(jnp.float32)
    for r in range(1, ref.shape[0]):
        total = total + ref[r, start : start + size, :].astype(jnp.float32)
    return total


def finish_kernel(
    scale, hidden, dq, dk, dv, dmixed, points, gain, w_qkv, gw_out, gw_pool, gb_pool, g_gain,
    grad_points, reduced, extras,
    low_k, low_v, high_k, high_v, send_c, recv_c, extra_own, extra_in,
    send_x, recv_x, send_y, recv_y, recv_z, gather_c, sems,
):
    me, before, after = neighbours()
    on_core, on_x, on_y, on_z = axes()
    barrier = pltpu.get_barrier_semaphore()
    greeted = []
    for rank, size, device in (on_z, on_y, on_x, on_core):
        greeted += [device((rank + k) % size) for k in far_first(size)]
    greeted += [before, after]
    for device in greeted:
        pl.semaphore_signal(barrier, inc=1, device_id=(device,), device_id_type=MESH)

    def fill(block, first_unit):
        for column in range(block.shape[1] // UNIT):
            unit = first_unit + 2 * column
            start = unit % 12 * UNIT
            for part in range(2):
                at = start + part * UNIT
                rows = slice(at % X_ROWS, at % X_ROWS + UNIT)
                send_c[unit // 12, at // X_ROWS, rows, :] = block[
                    part * UNIT : (part + 1) * UNIT, column * UNIT : (column + 1) * UNIT
                ]

    fill(gw_out[...], 12)
    fill(gw_pool[...], 16)
    pieces = [gb_pool[:, i * UNIT : (i + 1) * UNIT] for i in range(4)]
    pieces += [g_gain[:, i * UNIT : (i + 1) * UNIT] for i in range(4)]
    pieces += [jnp.zeros((EXTRA - 8, UNIT), jnp.float32)]
    packed = jnp.concatenate(pieces, axis=0).astype(jnp.bfloat16)
    extra_own[...] = packed
    own = slice(PATCH, 2 * PATCH)
    fill((inner_rows(hidden[own, :], dq[...]) * scale).astype(jnp.bfloat16), 0)
    fill((inner_rows(hidden[...], dk[...]) * scale).astype(jnp.bfloat16), 4)
    fill((inner_rows(hidden[...], dv[...]) * scale).astype(jnp.bfloat16), 8)

    pl.semaphore_wait(barrier, len(greeted))
    core, core_device = on_core[0], on_core[2](1 - on_core[0])
    x, x_device = on_x[0], on_x[2]
    steps = (2, 1, 3, 0)
    quarters = [(x + k) % 4 for k in steps]
    extra_copy = send(extra_own, extra_in, sems, 57, core_device)
    core_copies = [
        send(send_c.at[1 - core, q], recv_c.at[q], sems, k, core_device) for k, q in enumerate(quarters)
    ]
    extra_copy.wait()
    extra = (extra_own[...].astype(jnp.float32) + extra_in[...].astype(jnp.float32)).astype(jnp.bfloat16)
    copies = []
    for k, q in enumerate(quarters):
        core_copies[k].wait()
        total = send_c[core, q].astype(jnp.float32) + recv_c[q].astype(jnp.float32)
        if k < 3:
            send_x[q, :X_ROWS, :] = total.astype(jnp.bfloat16)
            send_x[q, X_ROWS:, :] = extra
            copies.append(send(send_x.at[q], recv_x.at[x], sems, 4 + steps[k], x_device(q)))
        else:
            recv_x[x, :X_ROWS, :] = total.astype(jnp.bfloat16)
            recv_x[x, X_ROWS:, :] = extra
    rims = [
        send(dk.at[pl.ds(0, PATCH)], high_k, sems, 60, before),
        send(dv.at[pl.ds(0, PATCH)], high_v, sems, 61, before),
        send(dk.at[pl.ds(2 * PATCH, PATCH)], low_k, sems, 62, after),
        send(dv.at[pl.ds(2 * PATCH, PATCH)], low_v, sems, 63, after),
    ]
    dhidden = against_rows(dq[...], w_qkv[:, :256])
    normed, inv_std = layer_stats(points[...].astype(jnp.float32))
    wait_all(copies)
    extra = slot_sum(recv_x, X_ROWS, EXTRA).astype(jnp.bfloat16)
    y, y_device = on_y[0], on_y[2]
    copies = []
    for k in far_first(8) + [0]:
        r = (y + k) % 8
        rows = pl.ds(pl.multiple_of(r * Y_ROWS, Y_ROWS), Y_ROWS)
        piece = recv_x[0, rows, :].astype(jnp.float32)
        for q in range(1, 4):
            piece = piece + recv_x[q, rows, :].astype(jnp.float32)
        target = send_y.at[r] if k else recv_y.at[y]
        target[:Y_ROWS, :] = piece.astype(jnp.bfloat16)
        target[Y_ROWS:, :] = extra
        if k:
            copies.append(send(target, recv_y.at[y], sems, 7 + k, y_device(r)))
    copies = copies[::-1]
    wait_all(rims)
    for columns, mine, low, high in (
        (slice(256, 512), dk, low_k, high_k), (slice(512, 768), dv, low_v, high_v)
    ):
        total = mine[own, :].astype(jnp.float32) + low[...].astype(jnp.float32)
        total = (total + high[...].astype(jnp.float32)).astype(jnp.bfloat16)
        dhidden = dhidden + against_rows(total, w_qkv[:, columns])
    grad_points[...] = dmixed[...] + norm_back(dhidden * gain[...], normed, inv_std)
    wait_all(copies)
    recv_z[on_z[0]] = slot_sum(recv_y, 0, Y_ROWS + EXTRA).astype(jnp.bfloat16)

    wait_all(swap(on_z, lambda r: recv_z.at[on_z[0]], lambda r: recv_z.at[r], sems, 15))
    total = slot_sum(recv_z, 0, Y_ROWS + EXTRA)
    extras[...] = total[Y_ROWS:]
    gather_c[core, x, y] = total[:Y_ROWS].astype(jnp.bfloat16)
    order = (1, 7, 2, 6, 3, 5, 4)

    def pass_on(k):
        piece = gather_c.at[core, x, (y + 8 - k) % 8]
        return {i: send(piece, piece, sems, 28 + 3 * k + i, x_device((x + i) % 4)) for i in (2, 1, 3)}

    mine = gather_c.at[core, x, y]
    y_copies = {k: send(mine, mine, sems, 22 + k - 1, y_device((y + k) % 8)) for k in order[::-1]}
    x_copies = {0: pass_on(0)}
    for k in order:
        y_copies[k].wait()
        x_copies[k] = pass_on(k)
    core_copies = [send(gather_c.at[core, x], gather_c.at[core, x], sems, 53, core_device)]
    for i in (1, 3, 2):
        for k in (0,) + order:
            x_copies[k][i].wait()
        slot = gather_c.at[core, (x + 4 - i) % 4]
        core_copies.append(send(slot, slot, sems, 53 + i, core_device))
    wait_all(core_copies)
    for c in range(2):
        for r in range(4):
            for s in range(8):
                start = c * CORE_ROWS + r * X_ROWS + s * Y_ROWS
                reduced[start : start + Y_ROWS, :] = gather_c[c, r, s]
    weighted = jnp.zeros((256, UNIT), jnp.float32)
    for column in range(6):
        block = reduced[column * 256 : (column + 1) * 256, :].astype(jnp.float32)
        lanes = slice(column * UNIT, (column + 1) * UNIT)
        weighted = weighted + block * w_qkv[:, lanes].astype(jnp.float32)
    summed_gain = jnp.sum(weighted.T, axis=0, keepdims=True) / gain[...]
    for i in range(2):
        extras[8 + i : 9 + i, :] = summed_gain[:, i * UNIT : (i + 1) * UNIT]


def finish(scale, *arrays):
    half = jnp.bfloat16
    vmem = pl.BlockSpec(memory_space=pltpu.VMEM)
    return pl.pallas_call(
        functools.partial(finish_kernel, scale),
        out_shape=[
            jax.ShapeDtypeStruct((PATCH, 256), jnp.float32),
            jax.ShapeDtypeStruct((2 * CORE_ROWS, UNIT), half),
            jax.ShapeDtypeStruct((EXTRA, UNIT), jnp.float32),
        ],
        in_specs=[vmem] * 12,
        out_specs=[vmem] * 3,
        scratch_shapes=[pltpu.VMEM((PATCH, 256), half)] * 4
        + [
            pltpu.VMEM((2, 4, X_ROWS, UNIT), half),
            pltpu.VMEM((4, X_ROWS, UNIT), half),
            pltpu.VMEM((EXTRA, UNIT), half),
            pltpu.VMEM((EXTRA, UNIT), half),
            pltpu.VMEM((4, X_ROWS + EXTRA, UNIT), half),
            pltpu.VMEM((4, X_ROWS + EXTRA, UNIT), half),
            pltpu.VMEM((8, Y_ROWS + EXTRA, UNIT), half),
            pltpu.VMEM((8, Y_ROWS + EXTRA, UNIT), half),
            pltpu.VMEM((8, Y_ROWS + EXTRA, UNIT), half),
            pltpu.VMEM((2, 4, 8, Y_ROWS, UNIT), half),
            pltpu.SemaphoreType.DMA((2, 64)),
        ],
        compiler_params=pltpu.CompilerParams(
            collective_id=3, has_side_effects=True, vmem_limit_bytes=40 * 1024 * 1024
        ),
        name="finish",
    )(*arrays)


def unpack_kernel(reduced, extras, rows_in, gq, go, gn, gp, gb, gg, rows_out, sem):
    copy = pltpu.make_async_copy(rows_in, rows_out, sem)
    copy.start()
    for column in range(12):
        block = reduced[column * 256 : (column + 1) * 256, :].astype(jnp.float32)
        if column < 6:
            gq[:, column * UNIT : (column + 1) * UNIT] = block
        elif column < 8:
            go[:, (column - 6) * UNIT : (column - 5) * UNIT] = block
        else:
            gp[:, (column - 8) * UNIT : (column - 7) * UNIT] = block
    for i in range(2):
        gn[:, i * UNIT : (i + 1) * UNIT] = extras[8 + i : 9 + i, :]
    for i in range(4):
        gb[:, i * UNIT : (i + 1) * UNIT] = extras[i : i + 1, :]
        gg[:, i * UNIT : (i + 1) * UNIT] = extras[4 + i : 5 + i, :]
    copy.wait()


def unpack(reduced, extras, rows):
    vmem = pl.BlockSpec(memory_space=pltpu.VMEM)
    outside = pl.BlockSpec(memory_space=pl.ANY)
    shapes = ((256, 768), (256, 256), (1, 256), (256, 512), (1, 512), (1, 512), (PATCH, 256))
    return pl.pallas_call(
        unpack_kernel,
        out_shape=[jax.ShapeDtypeStruct(shape, jnp.float32) for shape in shapes],
        in_specs=[vmem, vmem, vmem],
        out_specs=[vmem] * 6 + [outside],
        scratch_shapes=[pltpu.SemaphoreType.DMA],
        compiler_params=pltpu.CompilerParams(vmem_limit_bytes=16 * 1024 * 1024),
        name="unpack",
    )(reduced, extras, rows)


def body(
    points, patch_ids, cell_ids, norm_gain, w_qkv, w_out, w_pool, b_pool, pool_gain, cotangent
):
    scale = 1.0 / math.sqrt(points.shape[0] * lax.axis_size("pts"))
    gain = norm_gain[None]
    cells = cell_ids.reshape(4, HALF)
    far = [
        pltpu.with_memory_space_constraint(array, pltpu.HBM)
        for array in (points, patch_ids.reshape(4, HALF), gain, w_qkv, w_out, cells)
    ]
    queries, queries_t, keys_g, values_g, marks_f, hidden, spans = prepare(*far[:4])
    attended, logs, sums, counts = attend(
        spans, queries_t, marks_f, keys_g, values_g, far[0], far[4], far[5]
    )
    dmixed, datt, datt_t, deltas, gw_pool, gw_out, gb_pool, g_gain = pool(
        scale, sums, counts, cells, attended, w_out, w_pool, b_pool[None], pool_gain[None], cotangent
    )
    dq, dk, dv = attend_back(
        spans, queries, queries_t, logs, datt, datt_t, deltas, keys_g, values_g
    )
    grad_points, reduced, extras = finish(
        scale, hidden, dq, dk, dv, dmixed, points, gain, w_qkv, gw_out, gw_pool, gb_pool, g_gain
    )
    gq, go, gn, gp, gb, gg, grad_points = unpack(reduced, extras, grad_points)
    return (grad_points, gq, go, gn[0], gp, gb[0], gg[0])


def solution(mesh):
    in_specs = (P("pts", None), P("pts"), P("pts"), P(), P(), P(), P(), P(), P(), P("pts", None))
    out_specs = (P("pts", None), P(), P(), P(), P(), P(), P())
    return jax.shard_map(body, mesh=mesh, in_specs=in_specs, out_specs=out_specs, check_vma=False)
```
